128 devices in a mesh: seq: 4 (over y), fsdp: 32 (over x, z, core).
Axes of the slice: x: 4, y: 4, z: 4, core: 2. Of those that a mesh axis runs over, the one named last changes fastest.
Arguments:
- tokens: bfloat16 [32, 1024, 768], P('fsdp', 'seq'), may hold values from -6 to 6
- gain_attn: bfloat16 [768], P('fsdp'), may hold values from 0.5 to 1.5
- gain_ffn: bfloat16 [768], P('fsdp'), may hold values from 0.5 to 1.5
- w_query: bfloat16 [768, 768], P('fsdp'), may hold values from -0.21875 to 0.21875
- w_key: bfloat16 [768, 768], P('fsdp'), may hold values from -0.21875 to 0.21875
- w_value: bfloat16 [768, 768], P('fsdp'), may hold values from -0.21875 to 0.21875
- w_out: bfloat16 [768, 768], P('fsdp'), may hold values from -1.75 to 1.75
- router: bfloat16 [768, 64], P('fsdp'), may hold values from -0.109375 to 0.109375
- bias_table: bfloat16 [32, 12], P('fsdp'), may hold values from -4 to 4
- expert_in: bfloat16 [64, 768, 3072], P('fsdp', None, 'seq'), may hold values from -0.21875 to 0.21875
- expert_out: bfloat16 [64, 3072, 768], P('fsdp', 'seq'), may hold values from -0.109375 to 0.109375
- choices: int32 [32, 1024, 2], P('fsdp', 'seq'), may hold values from 0 to 63, all different within a row; in each aligned block of 256 rows (0 to 255, 256 to 511, ..., all dimensions but the last counted through in order) at most 12 rows name the same one
- buckets: int32 [1024], replicated, may hold values from 0 to 31, never falling along the last dimension, each value on 1 to 256 neighbouring positions
- cotangent: bfloat16 [32, 1024, 768], P('fsdp', 'seq'), may hold values from -6 to 6
Outputs:
- layer_out: bfloat16 [32, 1024, 768], P('fsdp', 'seq')
- grad_tokens: float32 [32, 1024, 768], P('fsdp', 'seq')
- grad_gain_attn: float32 [768], P('fsdp')
- grad_gain_ffn: float32 [768], P('fsdp')
- grad_w_query: float32 [768, 768], P('fsdp')
- grad_w_key: float32 [768, 768], P('fsdp')
- grad_w_value: float32 [768, 768], P('fsdp')
- grad_w_out: float32 [768, 768], P('fsdp')
- grad_router: float32 [768, 64], P('fsdp')
- grad_bias_table: float32 [32, 12], P('fsdp')
- grad_expert_in: float32 [64, 768, 3072], P('fsdp', None, 'seq')
- grad_expert_out: float32 [64, 3072, 768], P('fsdp', 'seq')
The draws below stay inside these ranges and needn't reach their ends.
Inputs may be any that keep to these rules, and one draw needn't show every extreme that they name: `choices`: each token names two different experts. In every aligned block of 256 tokens (one sequence's positions on one device) no expert is named more than 12 times, and in some block some expert exactly 12 times. `buckets`: never falling from one distance to the next, starting at 0; every bucket occurs.
All inputs are finite; a program needn't handle non-finite values.
Results may differ from the reference program's by a relative error of at most 0.023.
Values may be sent and summed in bfloat16 or wider, within the bound.
A program may use at most 192 MiB of HBM per device.

```python
import math
from functools import partial
import jax
import jax.numpy as jnp
import numpy as np
from jax import lax

D = 768
H = 12
HD = 64
FF = 3072
NB = 32
LEN = 1024
E = 64
SEQS = 32
LB = 256
CAP = 12
N_SEQ = 4


def level_of(rng, shape, shards, smallest, high):
    gain, own = 1.0, jax.random.fold_in(rng, 6)
    for dim, parts in shards:
        steps = jnp.exp(jax.random.uniform(jax.random.fold_in(own, dim), (parts,), jnp.float32, smallest / len(shards), high / len(shards)))
        gain = gain * jnp.repeat(steps, shape[dim] // parts).reshape([-1 if axis == dim else 1 for axis in range(len(shape))])
    return gain


def length_profile(number_of, total, reach, skew):
    loads = [(1 << 20) // math.isqrt(standing ** skew) + 1 for standing in range(2, number_of + 1)]
    surplus, counts = total - reach - (number_of - 1), [1] * (number_of - 1)
    while surplus > 0:
        movable = [i for i in range(number_of - 1) if counts[i] < reach]
        whole, remaining = sum([loads[i] for i in movable]), surplus
        for i in movable:
            addition = min(reach - counts[i], max(1, remaining * loads[i] // whole), surplus)
            counts[i] = counts[i] + addition
            surplus = surplus - addition
    return np.array([reach] + counts)


def uneven_parts(stream_key, count, total, most, lean):
    if count == 2:
        one = jax.random.randint(stream_key, (), max(1, total - most), min(most, total - 1) + 1)
        return jnp.stack([one, total - one])
    lengths = jnp.asarray(length_profile(count, total, most, lean), jnp.int32)
    couples = (count - 1) // 2
    donor, taker = lengths[1:1 + 2 * couples:2], lengths[2:2 + 2 * couples:2]
    slack = jnp.minimum(donor - 1, most - taker)
    moved = jax.random.randint(jax.random.fold_in(stream_key, 1), (couples,), 0, 1 << 20) % (slack + 1)
    lengths = lengths.at[1:1 + 2 * couples:2].set(donor - moved).at[2:2 + 2 * couples:2].set(taker + moved)
    return lengths[jax.random.permutation(jax.random.fold_in(stream_key, 2), count)]


def assign_block(key, own, number, rows, number_of, top, reach, lean):
    order = jax.random.permutation(key, number_of)
    heavy_load, common = portions_of(number_of, rows * top, reach, lean, True), portions_of(number_of, rows * top, reach, lean, False)
    places = jnp.arange(number_of)

    def named(sizes, offset_by):
        used = int((sizes > 0).sum())
        fixed = max(1, used // 4)
        shifted = fixed + (places - fixed + offset_by * (used - fixed)) % max(1, number_of - fixed)
        return jnp.zeros((number_of,), jnp.int32).at[order[jnp.where(places < fixed, places, shifted)]].set(jnp.asarray(sizes, jnp.int32))

    sizes = jnp.where(number % 4 == 0, named(heavy_load, number // 4), named(common, number - number // 4 - 1))
    mixed = jax.random.permutation(jax.random.fold_in(own, 3), number_of)
    source_of, taker = mixed[0:number_of // 2 * 2:2], mixed[1:number_of // 2 * 2:2]
    margin = jnp.minimum(sizes[source_of] - 1, reach - sizes[taker]) // 2
    margin = jnp.where((source_of == order[0]) | (taker == order[0]) | (sizes[taker] == 0), 0, jnp.maximum(margin, 0))
    shifted = jax.random.randint(jax.random.fold_in(own, 4), (number_of // 2,), 0, 1 << 20) % (margin + 1)
    sizes = sizes.at[source_of].add(-shifted).at[taker].add(shifted)
    members = jnp.searchsorted(jnp.cumsum(sizes), jnp.arange(rows * top), side="right").astype(jnp.int32)
    grid = members.reshape(top, rows).T
    grid = grid[jax.random.permutation(jax.random.fold_in(own, 1), rows)]
    offset_by = jax.random.randint(jax.random.fold_in(own, 2), (rows, 1), 0, top)
    return jnp.take_along_axis(grid, (jnp.arange(top)[None, :] + offset_by) % top, axis=1)


def portions_of(number_of, total, bound, lean, full):
    portions = [(1 << 20) // math.isqrt(standing ** lean) + 1 for standing in range(1, number_of + 1)]
    largest = bound if full else min(bound, max(-(-total // number_of), total * portions[0] // sum(portions)))
    least = 1 if total - largest >= number_of - 1 else 0
    given, surplus = [largest] + [least] * (number_of - 1), total - largest - least * (number_of - 1)
    while surplus > 0:
        candidates = [i for i in range(1, number_of) if given[i] < largest] or [i for i in range(1, number_of) if given[i] < bound]
        mass, remaining = sum([portions[i] for i in candidates]), surplus
        for i in candidates:
            extra = min(bound - given[i], max(1, remaining * portions[i] // mass), surplus)
            given[i] = given[i] + extra
            surplus = surplus - extra
    return np.array(given)


def normal_values(key, dims, width, bound, split=(), held_as=jnp.bfloat16):
    level = level_of(key, dims, split, -0.22, 0.18) if split else 1.0
    values = jax.random.normal(key, dims, jnp.float32) * width * level
    return jnp.minimum(jnp.maximum(values, -bound), bound).astype(held_as)


def setup_inputs(seed: int = 0) -> dict:
    key_of = jax.random.split(jax.random.key(seed), 15)
    tokens = normal_values(key_of[0], (SEQS, LEN, D), 1.0, 6.0, ((0, 32), (1, 4)))
    gain_attn = jnp.clip(1.0 + 0.1 * jax.random.normal(key_of[1], (D,), jnp.float32), 0.5, 1.5).astype(jnp.bfloat16)
    gain_ffn = jnp.clip(1.0 + 0.1 * jax.random.normal(key_of[2], (D,), jnp.float32), 0.5, 1.5).astype(jnp.bfloat16)
    w_query = normal_values(key_of[3], (D, D), D ** -0.5, 0.21875, ((0, 32),))
    w_key = normal_values(key_of[4], (D, D), D ** -0.5, 0.21875, ((0, 32),))
    w_value = normal_values(key_of[5], (D, D), D ** -0.5, 0.21875, ((0, 32),))
    w_out = normal_values(key_of[6], (D, D), (D // 64) ** -0.5, 1.75, ((0, 32),))
    router = normal_values(key_of[7], (D, E), (4 * D) ** -0.5, 0.109375, ((0, 32),))
    bias_table = normal_values(key_of[8], (NB, H), 1.0, 4.0, ((0, 32),))
    expert_in = normal_values(key_of[9], (E, D, FF), D ** -0.5, 0.21875, ((0, 32), (2, 4)))
    expert_out = normal_values(key_of[10], (E, FF, D), FF ** -0.5, 0.109375, ((0, 32), (1, 4)))
    choices_keys = jax.random.split(jax.random.fold_in(key_of[11], 1), SEQS * LEN // LB)
    choices_turns = jax.random.permutation(jax.random.fold_in(key_of[11], 3), SEQS * LEN // LB)
    choices = jax.vmap(lambda own, number: assign_block(jax.random.fold_in(key_of[11], 2), own, number, LB, E, 2, CAP, 2))(choices_keys, choices_turns).reshape((SEQS, LEN, 2))
    buckets = jnp.searchsorted(jnp.cumsum(uneven_parts(key_of[12], NB, LEN, LEN // 4, 2)), jnp.arange(LEN), side="right").astype(jnp.int32)
    cotangent = normal_values(key_of[13], (SEQS, LEN, D), 1.0, 6.0, ((0, 32), (1, 4)))
    return dict(tokens=tokens, gain_attn=gain_attn, gain_ffn=gain_ffn, w_query=w_query, w_key=w_key, w_value=w_value, w_out=w_out, router=router, bias_table=bias_table, expert_in=expert_in, expert_out=expert_out, choices=choices, buckets=buckets, cotangent=cotangent)


@jax.custom_vjp
def low(v):
    return lax.optimization_barrier(v.astype(jnp.bfloat16)).astype(jnp.float32)

@jax.custom_vjp
def low_back(v):
    return v

def low_keep(v):
    return (low(v), None)

def low_pass(kept, grad):
    return (grad,)

def back_keep(v):
    return (v, None)

def back_low(kept, grad):
    return (low(grad),)
low.defvjp(low_keep, low_pass)
low_back.defvjp(back_keep, back_low)
epsilon = 1e-06
highest = lax.Precision.HIGHEST

def rms_norm(values, gain_vector):
    factor = lax.rsqrt(lax.optimization_barrier(jnp.mean(values * values, axis=-1, keepdims=True)) + epsilon)
    return values * factor * gain_vector

def slot_numbers(choices):
    blocks = choices.reshape(SEQS * N_SEQ, LB * 2)
    expert_ids = jnp.arange(E, dtype=jnp.int32)
    one_hot = (blocks[:, :, None] == expert_ids[None, None, :]).astype(jnp.int32)
    earlier = jnp.cumsum(one_hot, axis=1) - one_hot
    return lax.optimization_barrier(jnp.sum(earlier * one_hot, axis=2)).reshape(SEQS * LEN, 2)

def attend(inputs, bias_rows):
    query_rows, key_rows, value_rows = inputs
    query_heads = query_rows.reshape(LEN, H, HD)
    key_heads = key_rows.reshape(LEN, H, HD)
    value_heads = value_rows.reshape(LEN, H, HD)
    raw_scores = low_back(jnp.einsum('qhd,khd->hqk', query_heads, key_heads, precision=highest))
    position = jnp.arange(LEN, dtype=jnp.int32)
    distance = position[:, None] - position[None, :]
    near_bias = jnp.take(bias_rows, jnp.maximum(distance, 0), axis=1)
    scores = jnp.where(distance[None] >= 0, raw_scores * HD ** (-0.5) + near_bias, -1e+30)
    row_max = lax.optimization_barrier(jnp.max(scores, axis=-1, keepdims=True))
    exp_scores = jnp.exp(scores - row_max)
    attn_probs = exp_scores / lax.optimization_barrier(jnp.sum(exp_scores, axis=-1, keepdims=True))
    mixed = jnp.einsum('hqk,khd->qhd', low(attn_probs), value_heads, precision=highest)
    return mixed.reshape(LEN, D)

def expert_apply(inputs):
    slot_rows, first_weight, second_weight = inputs
    hidden = low(jax.nn.gelu(low_back(jnp.dot(slot_rows, first_weight, precision=highest))))
    return low_back(jnp.dot(hidden, second_weight, precision=highest))

def forward(tokens, gain_attn, gain_ffn, w_query, w_key, w_value, w_out, router, bias_table, expert_in, expert_out, chosen_ids, buckets, places, slot_owner):
    row_values = tokens.reshape(SEQS * LEN, D)
    normed = low(rms_norm(row_values, gain_attn))
    query_all = low(low_back(jnp.dot(normed, w_query, precision=highest))).reshape(SEQS, LEN, D)
    key_all = low(low_back(jnp.dot(normed, w_key, precision=highest))).reshape(SEQS, LEN, D)
    value_all = low(low_back(jnp.dot(normed, w_value, precision=highest))).reshape(SEQS, LEN, D)
    bias_rows = jnp.take(bias_table, buckets, axis=0).T
    attended = lax.map(jax.checkpoint(partial(attend, bias_rows=bias_rows)), (query_all, key_all, value_all))
    mixed = low(low_back(attended.reshape(SEQS * LEN, D)))
    inner = row_values + low_back(jnp.dot(mixed, w_out, precision=highest))
    normed_ffn = low(rms_norm(inner, gain_ffn))
    logits = low_back(jnp.dot(normed_ffn, router, precision=highest))
    gate_weights = jax.nn.softmax(jnp.take_along_axis(logits, chosen_ids, axis=1), axis=1)
    source = normed_ffn[jnp.maximum(slot_owner - 1, 0) // 2]
    slot_rows = jnp.where(slot_owner[:, None] > 0, source, 0.0).reshape(E, SEQS * N_SEQ * CAP, D)
    results = lax.map(jax.checkpoint(expert_apply), (slot_rows, expert_in, expert_out))
    results = results.reshape(E * SEQS * N_SEQ * CAP, D)
    back_rows = results[places]
    summed_out = inner + lax.optimization_barrier(jnp.sum(gate_weights[:, :, None] * back_rows, axis=1))
    return summed_out.reshape(SEQS, LEN, D)

def reference(tokens, gain_attn, gain_ffn, w_query, w_key, w_value, w_out, router, bias_table, expert_in, expert_out, choices, buckets, cotangent):
    chosen_ids = choices.reshape(SEQS * LEN, 2)
    slot_index = slot_numbers(choices)
    block_ids = (jnp.arange(SEQS * LEN, dtype=jnp.int32) // LB)[:, None]
    places = chosen_ids * (SEQS * N_SEQ * CAP) + block_ids * CAP + slot_index
    slot_owner = jnp.zeros((E * SEQS * N_SEQ * CAP,), jnp.int32).at[places.reshape(-1)].set(jnp.arange(SEQS * LEN * 2, dtype=jnp.int32) + 1)
    floats = [argument.astype(jnp.float32) for argument in (tokens, gain_attn, gain_ffn, w_query, w_key, w_value, w_out, router, bias_table, expert_in, expert_out)]

    def whole_layer(tokens_f, gain_one, gain_two, query_w, key_w, value_w, out_w, router_w, table_w, first_w, second_w):
        return forward(tokens_f, gain_one, gain_two, query_w, key_w, value_w, out_w, router_w, table_w, first_w, second_w, chosen_ids, buckets, places, slot_owner)
    layer_out, pull_back = jax.vjp(whole_layer, *floats)
    gradients = pull_back(cotangent.astype(jnp.float32))
    return (layer_out.astype(jnp.bfloat16), gradients[0], gradients[1], gradients[2], gradients[3], gradients[4], gradients[5], gradients[6], gradients[7], gradients[8], gradients[9], gradients[10])
```

```python
from functools import partial

import jax
import jax.numpy as jnp
from jax import lax
from jax.experimental import pallas as pl
from jax.experimental.pallas import tpu as pltpu
from jax.sharding import PartitionSpec as P

D = 768
H = 12
HD = 64
NS = 4
NF = 32
HL = H // NS
HW = HL * HD
LB = 256
LEN = 1024
E = 64
CAP = 12
ROWS = 2 * CAP
MSG = D + 128
PACK = 1536
NB = 32
SPAN = 2 * LB

epsilon = 1e-06
highest = lax.Precision.HIGHEST
MESH = pl.DeviceIdType.MESH
F32 = jnp.float32
BF16 = jnp.bfloat16
MIB = 1024 * 1024


def any_spec():
    return pl.BlockSpec(memory_space=pl.ANY)


def vmem_spec():
    return pl.BlockSpec(memory_space=pltpu.VMEM)


def dot(a, b, dims=((1,), (0,))):
    return lax.dot_general(a, b, (dims, ((), ())), preferred_element_type=F32)


def params(collective_id=None, vmem=48):
    if collective_id is None:
        return pltpu.CompilerParams(vmem_limit_bytes=vmem * MIB)
    return pltpu.CompilerParams(
        collective_id=collective_id, has_side_effects=True, vmem_limit_bytes=vmem * MIB
    )


def place_of():
    return lax.axis_index("seq"), lax.axis_index("fsdp")


def greet_seq(s):
    barrier = pltpu.get_barrier_semaphore()
    for k in range(1, NS):
        pl.semaphore_signal(
            barrier, inc=1, device_id={"seq": lax.rem(s + k, NS)}, device_id_type=MESH
        )
    return NS - 1


def greet_fsdp(f):
    barrier = pltpu.get_barrier_semaphore()

    def one(k, carried):
        pl.semaphore_signal(
            barrier, inc=1, device_id={"fsdp": lax.rem(f + k, NF)}, device_id_type=MESH
        )
        return carried

    lax.fori_loop(1, NF, one, 0)
    return NF - 1


def arrive(count):
    pl.semaphore_wait(pltpu.get_barrier_semaphore(), count)


def send_seq(s, source, target, send, recv):
    for k in range(1, NS):
        peer = lax.rem(s + k, NS)
        pltpu.make_async_remote_copy(
            src_ref=source(peer),
            dst_ref=target,
            send_sem=send,
            recv_sem=recv,
            device_id={"seq": peer},
            device_id_type=MESH,
        ).start()


def send_fsdp(f, source, target, send, recv):
    def one(k, carried):
        peer = lax.rem(f + k, NF)
        pltpu.make_async_remote_copy(
            src_ref=source(peer),
            dst_ref=target,
            send_sem=send,
            recv_sem=recv,
            device_id={"fsdp": peer},
            device_id_type=MESH,
        ).start()
        return carried

    lax.fori_loop(1, NF, one, 0)


def await_bytes(ref, sem):
    pltpu.make_async_copy(ref, ref, sem).wait()


def ring_gather(s, out, own, sems, send, recv, half):
    right, left = lax.rem(s + 1, NS), lax.rem(s + NS - 1, NS)

    def copy(block, rows, to, n):
        ref = out.at[block] if rows is None else out.at[block, rows]
        source = own if own is not None and rows is None else ref
        return pltpu.make_async_remote_copy(
            src_ref=source,
            dst_ref=ref,
            send_sem=send.at[sems + n],
            recv_sem=recv.at[sems + n],
            device_id={"seq": to},
            device_id_type=MESH,
        )

    first, second = pl.ds(0, half), pl.ds(half, half)
    far = lax.rem(s + 2, NS)
    begin = [copy(s, None, right, 0), copy(s, None, left, 1)]
    relay = [copy(left, first, right, 2), copy(right, second, left, 3)]
    come = [copy(left, None, right, 0), copy(right, None, left, 1)]
    last = [copy(far, first, right, 2), copy(far, second, left, 3)]
    return begin, relay, come, last


def start_kernel(w_ref, x_ref, dy_ref, wg, xg, dyg, send, recv, local):
    s, f = place_of()
    pair, core = f // 2, lax.rem(f, 2)
    count = greet_fsdp(f) + greet_seq(s)
    arrive(count)
    x_begin, x_relay, x_come, x_last = ring_gather(s, xg, x_ref, 0, send, recv, LB // 2)
    y_begin, y_relay, y_come, y_last = ring_gather(s, dyg, None, 4, send, recv, NF // 2)
    for copy in x_begin:
        copy.start()
    own_x = pltpu.make_async_copy(x_ref, xg.at[s], local.at[0])
    own_w = pltpu.make_async_copy(w_ref, wg.at[pair, core], local.at[1])
    own_dy = pltpu.make_async_copy(dy_ref.at[f], dyg.at[s, f], local.at[2])
    own_x.start()
    own_w.start()
    own_dy.start()

    def one(k, carried):
        peer = lax.rem(pair + k, NF // 2)
        pltpu.make_async_remote_copy(
            src_ref=w_ref,
            dst_ref=wg.at[pair, core],
            send_sem=send.at[8],
            recv_sem=recv.at[8],
            device_id={"fsdp": 2 * peer + core},
            device_id_type=MESH,
        ).start()
        return carried

    lax.fori_loop(1, NF // 2, one, 0)
    send_fsdp(f, lambda peer: dy_ref.at[peer], dyg.at[s, f], send.at[9], recv.at[9])
    own_x.wait()
    own_w.wait()
    own_dy.wait()
    for n in range(2):
        x_come[n].wait_recv()
        x_relay[n].start()
    others = wg.at[pl.ds(0, NF // 2 - 1), core]
    await_bytes(others, recv.at[8])
    swap = pltpu.make_async_remote_copy(
        src_ref=wg.at[:, core],
        dst_ref=wg.at[:, core],
        send_sem=send.at[10],
        recv_sem=recv.at[10],
        device_id={"fsdp": 2 * pair + 1 - core},
        device_id_type=MESH,
    )
    swap.start()
    await_bytes(dyg.at[s, pl.ds(0, NF - 1)], recv.at[9])
    for copy in y_begin:
        copy.start()
    for n in range(2):
        y_come[n].wait_recv()
        y_relay[n].start()
    for n in range(2):
        x_last[n].wait_recv()
        y_last[n].wait_recv()
    swap.wait_recv()
    for copy in x_begin + x_relay + y_begin + y_relay + [swap]:
        copy.wait_send()
    await_bytes(others, send.at[8])
    await_bytes(dyg.at[s, pl.ds(0, NF - 1)], send.at[9])


def start_exchange(packed, tokens, dy_rows):
    return pl.pallas_call(
        start_kernel,
        out_shape=(
            jax.ShapeDtypeStruct((NF // 2, 2) + packed.shape, packed.dtype),
            jax.ShapeDtypeStruct((NS,) + tokens.shape, tokens.dtype),
            jax.ShapeDtypeStruct((NS,) + dy_rows.shape, dy_rows.dtype),
        ),
        in_specs=[any_spec()] * 3,
        out_specs=(any_spec(), any_spec(), any_spec()),
        scratch_shapes=[
            pltpu.SemaphoreType.DMA((11,)),
            pltpu.SemaphoreType.DMA((11,)),
            pltpu.SemaphoreType.DMA((3,)),
        ],
        compiler_params=params(0),
        name="start_exchange",
    )(packed, tokens, dy_rows)


def seq_kernel(x_ref, out, send, recv, local):
    s, f = place_of()
    arrive(greet_seq(s))
    send_seq(s, lambda peer: x_ref.at[peer], out.at[s], send, recv)
    own = pltpu.make_async_copy(x_ref.at[s], out.at[s], local)
    own.start()
    own.wait()
    await_bytes(out.at[pl.ds(0, NS - 1)], send)
    await_bytes(out.at[pl.ds(0, NS - 1)], recv)


def seq_exchange(x, collective_id, name):
    return pl.pallas_call(
        seq_kernel,
        out_shape=jax.ShapeDtypeStruct(x.shape, x.dtype),
        in_specs=[any_spec()],
        out_specs=any_spec(),
        scratch_shapes=[pltpu.SemaphoreType.DMA] * 3,
        compiler_params=params(collective_id),
        name=name,
    )(x)


def seq_gather_kernel(x_ref, out, send, recv, local):
    s, f = place_of()
    arrive(greet_seq(s))
    send_seq(s, lambda peer: x_ref, out.at[s], send, recv)
    own = pltpu.make_async_copy(x_ref, out.at[s], local)
    own.start()
    own.wait()
    await_bytes(out.at[pl.ds(0, NS - 1)], send)
    await_bytes(out.at[pl.ds(0, NS - 1)], recv)


def seq_gather(x, collective_id, name):
    return pl.pallas_call(
        seq_gather_kernel,
        out_shape=jax.ShapeDtypeStruct((NS,) + x.shape, x.dtype),
        in_specs=[any_spec()],
        out_specs=any_spec(),
        scratch_shapes=[pltpu.SemaphoreType.DMA] * 3,
        compiler_params=params(collective_id),
        name=name,
    )(x)


def last_kernel(w_ref, x_ref, wg, xg, mine, theirs, send, recv, local):
    s, f = place_of()
    pair, core = f // 2, lax.rem(f, 2)
    arrive(greet_fsdp(f) + greet_seq(s))
    swap = pltpu.make_async_remote_copy(
        src_ref=w_ref.at[:, 1 - core],
        dst_ref=theirs,
        send_sem=send.at[0],
        recv_sem=recv.at[0],
        device_id={"fsdp": 2 * pair + 1 - core},
        device_id_type=MESH,
    )
    swap.start()
    own_w = pltpu.make_async_copy(w_ref.at[:, core], mine, local.at[0])
    own_w.start()
    send_seq(s, lambda peer: x_ref.at[peer], xg.at[s], send.at[1], recv.at[1])
    own_x = pltpu.make_async_copy(x_ref.at[s], xg.at[s], local.at[1])
    own_x.start()
    own_w.wait()
    swap.wait_recv()

    def add(i, carried):
        mine[i] = (mine[i].astype(F32) + theirs[i].astype(F32)).astype(BF16)
        return carried

    lax.fori_loop(0, NF // 2, add, 0)

    def one(k, carried):
        peer = lax.rem(pair + k, NF // 2)
        pltpu.make_async_remote_copy(
            src_ref=mine.at[peer],
            dst_ref=wg.at[pair],
            send_sem=send.at[2],
            recv_sem=recv.at[2],
            device_id={"fsdp": 2 * peer + core},
            device_id_type=MESH,
        ).start()
        return carried

    lax.fori_loop(1, NF // 2, one, 0)
    keep = pltpu.make_async_copy(mine.at[pair], wg.at[pair], local.at[2])
    keep.start()
    keep.wait()
    own_x.wait()
    swap.wait_send()
    others = wg.at[pl.ds(0, NF // 2 - 1)]
    await_bytes(xg.at[pl.ds(0, NS - 1)], send.at[1])
    await_bytes(others, send.at[2])
    await_bytes(xg.at[pl.ds(0, NS - 1)], recv.at[1])
    await_bytes(others, recv.at[2])


def last_exchange(w, x, collective_id):
    half = (w.shape[0],) + w.shape[2:]
    return pl.pallas_call(
        last_kernel,
        out_shape=(
            jax.ShapeDtypeStruct(half, w.dtype),
            jax.ShapeDtypeStruct(x.shape, x.dtype),
        ),
        in_specs=[any_spec()] * 2,
        out_specs=(any_spec(), any_spec()),
        scratch_shapes=[
            pltpu.VMEM(half, BF16),
            pltpu.VMEM(half, BF16),
            pltpu.SemaphoreType.DMA((3,)),
            pltpu.SemaphoreType.DMA((3,)),
            pltpu.SemaphoreType.DMA((3,)),
        ],
        compiler_params=params(collective_id, 16),
        name="last_exchange",
    )(w, x)


def bias_tiles(base_ref, tiles, head):
    for d in range(NS):
        wide = jnp.broadcast_to(base_ref[head, d : d + 1, :], (LB, SPAN))
        tiles[d] = pltpu.roll(wide, 0, 1, stride=1, stride_axis=0)[:, :LB]


def score_tiles(query, key_ref, tiles, cols, block):
    parts = []
    for kb in range(block + 1):
        keys = key_ref[kb * LB : (kb + 1) * LB, cols]
        parts.append(dot(query, keys, ((1,), (1,))) * (HD**-0.5) + tiles[block - kb])
    return parts


def forward_kernel(q_ref, k_ref, v_ref, base_ref, o_ref, lse_ref, tiles):
    for head in range(HL):
        cols = slice(head * HD, (head + 1) * HD)
        bias_tiles(base_ref, tiles, head)
        for block in range(NS):
            rows = slice(block * LB, (block + 1) * LB)
            parts = score_tiles(q_ref[rows, cols], k_ref, tiles, cols, block)
            top = parts[0].max(axis=1, keepdims=True)
            for part in parts[1:]:
                top = jnp.maximum(top, part.max(axis=1, keepdims=True))
            parts = [jnp.exp(part - top) for part in parts]
            total = parts[0].sum(axis=1, keepdims=True)
            for part in parts[1:]:
                total = total + part.sum(axis=1, keepdims=True)
            inverse = 1.0 / total
            mixed = None
            for kb, part in enumerate(parts):
                term = dot((part * inverse).astype(BF16), v_ref[kb * LB : (kb + 1) * LB, cols])
                mixed = term if mixed is None else mixed + term
            o_ref[rows, cols] = mixed.astype(BF16)
            lse_ref[head, rows, :] = top + jnp.log(total)


def attend_forward(q, k, v, base):
    return pl.pallas_call(
        forward_kernel,
        out_shape=(
            jax.ShapeDtypeStruct((LEN, HW), BF16),
            jax.ShapeDtypeStruct((HL, LEN, 1), F32),
        ),
        in_specs=[vmem_spec()] * 4,
        out_specs=(vmem_spec(), vmem_spec()),
        scratch_shapes=[pltpu.VMEM((NS, LB, LB), F32)],
        compiler_params=params(),
        name="attend_forward",
    )(q, k, v, base)


def flip_rows(values):
    down = lax.broadcasted_iota(jnp.int32, (LB, LB), 0)
    across = lax.broadcasted_iota(jnp.int32, (LB, LB), 1)
    swap = (down + across == LB - 1).astype(BF16)
    high = values.astype(BF16)
    low = (values - high.astype(F32)).astype(BF16)
    return dot(swap, high) + dot(swap, low)


def backward_kernel(
    q_ref, k_ref, v_ref, do_ref, lse_ref, base_ref, g_ref, diag_ref, tiles, folds, dk, dv
):
    scale = HD**-0.5
    for head in range(HL):
        cols = slice(head * HD, (head + 1) * HD)
        bias_tiles(base_ref, tiles, head)
        for block in range(NS):
            rows = slice(block * LB, (block + 1) * LB)
            query, grad = q_ref[rows, cols], do_ref[rows, cols]
            lse = lse_ref[head, rows, :]
            parts = score_tiles(query, k_ref, tiles, cols, block)
            probs = [jnp.exp(part - lse) for part in parts]
            grads = [
                dot(grad, v_ref[kb * LB : (kb + 1) * LB, cols], ((1,), (1,)))
                for kb in range(block + 1)
            ]
            delta = None
            for prob, part in zip(probs, grads):
                term = (prob * part).sum(axis=1, keepdims=True)
                delta = term if delta is None else delta + term
            grad_query = None
            for kb in range(block + 1):
                keys = slice(kb * LB, (kb + 1) * LB)
                d = block - kb
                ds = probs[kb] * (grads[kb] - delta)
                if kb == 0:
                    folds[d] = ds
                else:
                    folds[d] += ds
                raw = (ds * scale).astype(BF16)
                term = dot(raw, k_ref[keys, cols])
                grad_query = term if grad_query is None else grad_query + term
                to_key = dot(raw, query, ((0,), (0,)))
                to_value = dot(probs[kb].astype(BF16), grad, ((0,), (0,)))
                if d == 0:
                    dk[keys, :] = to_key
                    dv[keys, :] = to_value
                else:
                    dk[keys, :] += to_key
                    dv[keys, :] += to_value
            g_ref[rows, cols] = grad_query.astype(BF16)
        g_ref[:, HW + head * HD : HW + (head + 1) * HD] = dk[...].astype(BF16)
        g_ref[:, 2 * HW + head * HD : 2 * HW + (head + 1) * HD] = dv[...].astype(BF16)
        for d in range(NS):
            wide = jnp.concatenate(
                [flip_rows(folds[d]), jnp.zeros((LB, SPAN - LB), F32)], axis=1
            )
            turned = pltpu.roll(wide, LB + 1, 1, stride=1, stride_axis=0)
            diag_ref[head, d : d + 1, :] = turned.sum(axis=0, keepdims=True)


def attend_backward(q, k, v, do, lse, base):
    return pl.pallas_call(
        backward_kernel,
        out_shape=(
            jax.ShapeDtypeStruct((LEN, 3 * HW), BF16),
            jax.ShapeDtypeStruct((HL, NS, SPAN), F32),
        ),
        in_specs=[vmem_spec()] * 6,
        out_specs=(vmem_spec(), vmem_spec()),
        scratch_shapes=[
            pltpu.VMEM((NS, LB, LB), F32),
            pltpu.VMEM((NS, LB, LB), F32),
            pltpu.VMEM((LEN, HD), F32),
            pltpu.VMEM((LEN, HD), F32),
        ],
        compiler_params=params(),
        name="attend_backward",
    )(q, k, v, do, lse, base)


def split_rows(rows):
    width = rows.shape[-1]
    half = NF // 2
    mixed = rows[:, 16:24]
    left, right = mixed[:half], mixed[half:]
    low = lax.broadcasted_iota(jnp.int32, left.shape, 1) < 4
    one = jnp.where(low, left, pltpu.roll(right, 4, 1)).reshape(half * 8, width)
    two = jnp.where(low, pltpu.roll(left, 4, 1), right).reshape(half * 8, width)
    return (
        jnp.concatenate([rows[:, 0:8].reshape(NF * 8, width), one], axis=0),
        jnp.concatenate([rows[:, 8:16].reshape(NF * 8, width), two], axis=0),
    )


def join_rows(first, second):
    width = first.shape[-1]
    half = NF // 2
    one = first[NF * 8 :].reshape(half, 8, width)
    two = second[NF * 8 :].reshape(half, 8, width)
    low = lax.broadcasted_iota(jnp.int32, one.shape, 1) < 4
    left = jnp.where(low, one, pltpu.roll(two, 4, 1))
    right = jnp.where(low, pltpu.roll(one, 4, 1), two)
    return jnp.concatenate(
        [
            first[: NF * 8].reshape(NF, 8, width),
            second[: NF * 8].reshape(NF, 8, width),
            jnp.concatenate([left, right], axis=0),
        ],
        axis=1,
    )


def expert_rows(x, dy, ids, own, router, w_in, w_out):
    logits = dot(x, router)
    lane = lax.broadcasted_iota(jnp.int32, logits.shape, 1)
    one = jnp.sum(jnp.where(lane == own, logits, 0.0), axis=1, keepdims=True)
    two = jnp.sum(jnp.where(lane == ids, logits, 0.0), axis=1, keepdims=True)
    top = jnp.maximum(one, two)
    one, two = jnp.exp(one - top), jnp.exp(two - top)
    gate = one / (one + two)
    grad = (dy * gate).astype(BF16)
    u = dot(x, w_in)
    square = u * u
    tanh = jnp.tanh(u * (0.7978845608028654 + (0.7978845608028654 * 0.044715) * square))
    half = 0.5 * (1.0 + tanh)
    hid = (u * half).astype(BF16)
    slope = half + (0.5 * u) * (1.0 - tanh * tanh) * (
        0.7978845608028654 + (3.0 * 0.7978845608028654 * 0.044715) * square
    )
    y = dot(hid, w_out)
    du = (dot(grad, w_out, ((1,), (1,))) * slope).astype(BF16)
    dx = dot(du, w_in, ((1,), (1,)))
    return y, dx, hid, grad, du


def expert_kernel(
    x_ref, dy_ref, router_ref, wi_ref, wo_ref, y_out, dx_out, gi_ref, go_ref,
    x, dy, part, near, summed, kept, send, recv, local,
):
    s, f = place_of()
    right, left = lax.rem(s + 1, NS), lax.rem(s + NS - 1, NS)
    far = lax.rem(s + 2, NS)
    half = NF // 2
    first, second = pl.ds(0, half), pl.ds(half, half)
    arrive(greet_fsdp(f) + greet_seq(s))

    def hop(source, target, to, n):
        return pltpu.make_async_remote_copy(
            src_ref=source,
            dst_ref=target,
            send_sem=send.at[n],
            recv_sem=recv.at[n],
            device_id={"seq": to},
            device_id_type=MESH,
        )

    send_fsdp(f, lambda peer: x_ref.at[peer], x.at[s, f], send.at[4], recv.at[4])
    own_x = pltpu.make_async_copy(x_ref.at[f], x.at[s, f], local.at[0])
    own_x.start()
    gi_ref[...] = jnp.zeros_like(gi_ref)
    go_ref[...] = jnp.zeros_like(go_ref)
    begin, relay, come, last = ring_gather(s, x, None, 0, send, recv, half)
    early, onward, late = [], [], []
    for a in range(2):
        early.append(
            [
                hop(part.at[a, right, second], near.at[a, 0, second], right, 5 + 2 * a),
                hop(part.at[a, left, first], near.at[a, 1, first], left, 6 + 2 * a),
            ]
        )
        onward.append(
            [
                hop(part.at[a, far, first], summed.at[a, 0], right, 9 + 2 * a),
                hop(part.at[a, far, second], summed.at[a, 1], left, 10 + 2 * a),
            ]
        )
        late.append(
            [
                hop(part.at[a, right, first], near.at[a, 0, first], right, 13 + 2 * a),
                hop(part.at[a, left, second], near.at[a, 1, second], left, 14 + 2 * a),
            ]
        )
    own_x.wait()
    await_bytes(x.at[s, pl.ds(0, NF - 1)], recv.at[4])
    for copy in begin:
        copy.start()

    def step(k, carried):
        chunk = lax.rem(s + jnp.where(k == 1, 3, jnp.where(k == 0, 0, k - 1)), NS)
        load = pltpu.make_async_copy(dy_ref.at[chunk], dy, local.at[1])
        load.start()

        @pl.when(k == 1)
        def _():
            for n in range(2):
                come[n].wait_recv()
                relay[n].start()

        @pl.when(k == 3)
        def _():
            for n in range(2):
                last[n].wait_recv()

        load.wait()
        xs = split_rows(x[chunk].astype(F32))
        dys = split_rows(dy[...].astype(F32))
        ys, dxs = [], []
        for j in range(2):
            rows = xs[j].astype(BF16)
            ids = dys[j][:, D:].astype(jnp.int32)
            y, dx, hid, grad, du = expert_rows(
                rows, dys[j][:, :D], ids, 2 * f + j, router_ref[...], wi_ref[j], wo_ref[j]
            )
            ys.append(y)
            dxs.append(dx)
            for n, value in enumerate((rows, hid, grad, du)):
                kept[n, j] = value
        part[0, chunk] = join_rows(*ys).astype(BF16)
        part[1, chunk] = join_rows(*dxs).astype(BF16)

        @pl.when(k == 1)
        def _():
            for a in range(2):
                early[a][1].start()

        @pl.when(k == 2)
        def _():
            for a in range(2):
                early[a][0].start()

        @pl.when(k == 3)
        def _():
            for a in range(2):
                for n in range(2):
                    onward[a][n].start()

        for j in range(2):
            go_ref[j] += dot(kept[1, j], kept[2, j], ((0,), (0,)))
            gi_ref[j] += dot(kept[0, j], kept[3, j], ((0,), (0,)))
        return carried

    lax.fori_loop(0, NS, step, 0)

    def add(a, block, offset, other):
        def one(i, carried):
            total = part[a, block, offset + i].astype(F32) + other(i)
            part[a, block, offset + i] = total.astype(BF16)
            return carried

        return one

    for a in range(2):
        for n, block, offset in ((0, right, 0), (1, left, half)):
            onward[a][n].wait_recv()
            lax.fori_loop(
                0, half, add(a, block, offset, lambda i: summed[a, n, i].astype(F32)), 0
            )
            late[a][n].start()
    outs = (y_out, dx_out)
    keeps = []
    for a in range(2):
        for n in range(2):
            early[a][n].wait_recv()
            late[a][n].wait_recv()
        lax.fori_loop(
            0,
            NF,
            add(a, s, 0, lambda i: near[a, 0, i].astype(F32) + near[a, 1, i].astype(F32)),
            0,
        )
        send_fsdp(
            f, lambda peer: part.at[a, s, peer], outs[a].at[f], send.at[17 + a], recv.at[17 + a]
        )
        keep = pltpu.make_async_copy(part.at[a, s, f], outs[a].at[f], local.at[2 + a])
        keep.start()
        keeps.append(keep)
    for a in range(2):
        keeps[a].wait()
        others = outs[a].at[pl.ds(0, NF - 1)]
        await_bytes(others, recv.at[17 + a])
        await_bytes(others, send.at[17 + a])
        for copy in early[a] + onward[a] + late[a]:
            copy.wait_send()
    for copy in begin + relay:
        copy.wait_send()
    await_bytes(x.at[s, pl.ds(0, NF - 1)], send.at[4])


def run_experts(x, dy, router, w_in, w_out, collective_id):
    rows = (NF, ROWS, D)
    return pl.pallas_call(
        expert_kernel,
        out_shape=(
            jax.ShapeDtypeStruct(rows, BF16),
            jax.ShapeDtypeStruct(rows, BF16),
            jax.ShapeDtypeStruct((2, D, D), F32),
            jax.ShapeDtypeStruct((2, D, D), F32),
        ),
        in_specs=[any_spec(), any_spec(), vmem_spec(), vmem_spec(), vmem_spec()],
        out_specs=(any_spec(), any_spec(), vmem_spec(), vmem_spec()),
        scratch_shapes=[
            pltpu.VMEM((NS,) + rows, BF16),
            pltpu.VMEM((NF, ROWS, MSG), BF16),
            pltpu.VMEM((2, NS) + rows, BF16),
            pltpu.VMEM((2, 2) + rows, BF16),
            pltpu.VMEM((2, 2, NF // 2, ROWS, D), BF16),
            pltpu.VMEM((4, 2, NF * CAP, D), BF16),
            pltpu.SemaphoreType.DMA((19,)),
            pltpu.SemaphoreType.DMA((19,)),
            pltpu.SemaphoreType.DMA((4,)),
        ],
        compiler_params=params(collective_id, 63),
        name="run_experts",
    )(x, dy, router, w_in, w_out)


def distance_base(values, near, far):
    long = jnp.concatenate(
        [jnp.full((LB,), near, values.dtype), values, jnp.full((1,), far, values.dtype)]
    )
    rows = []
    for d in range(NS):
        rows.append(long[d * LB + 1 : d * LB + LB + 1][::-1])
        rows.append(long[LB + d * LB + 1 : LB + d * LB + LB + 1][::-1])
    return jnp.concatenate(rows)


def norm_factor(values):
    return lax.rsqrt(jnp.mean(values * values, axis=-1, keepdims=True) + epsilon)


def shards(
    tokens,
    gain_attn,
    gain_ffn,
    w_query,
    w_key,
    w_value,
    w_out,
    router,
    bias_table,
    expert_in,
    expert_out,
    choices,
    buckets,
    cotangent,
):
    s = lax.axis_index("seq")
    share = D // NF
    own_tokens = tokens.reshape(LB, D)

    def own_heads(w):
        return lax.dynamic_slice_in_dim(w, s * HW, HW, 1)

    misc = jnp.concatenate(
        [
            gain_attn[:, None],
            gain_ffn[:, None],
            jnp.pad(bias_table, ((0, share - 1), (0, 0))),
            jnp.zeros((share, 128 - 2 - H), BF16),
        ],
        axis=1,
    )
    packed = jnp.concatenate(
        [w_out, own_heads(w_query), own_heads(w_key), own_heads(w_value), router, misc], axis=1
    )

    picks = choices.reshape(LB, 2)
    flat = picks.reshape(2 * LB)
    hot = flat[:, None] == jnp.arange(E, dtype=jnp.int32)[None, :]
    order = jnp.arange(2 * LB, dtype=jnp.int32)
    before = (order[:, None] > order[None, :]).astype(BF16)
    counts = dot(before, hot.astype(BF16))
    rank = jnp.sum(jnp.where(hot, counts, 0.0), axis=1).astype(jnp.int32)
    odd = flat % 2
    row = jnp.where(rank < 8, 8 * odd + rank, 16 + 4 * odd + rank - 8)
    places = ((flat // 2) * ROWS + row).reshape(LB, 2)
    slot_ids = jnp.arange(NF * ROWS, dtype=jnp.int32)
    held = [slot_ids[:, None] == places[None, :, c] for c in range(2)]
    held_hot = [h.astype(BF16) for h in held]
    both_hot = (held[0] | held[1]).astype(BF16)
    dy_bf = cotangent.reshape(LB, D)
    others = dot(held_hot[0], jnp.broadcast_to(picks[:, 1:2], (LB, 128)).astype(BF16)) + dot(
        held_hot[1], jnp.broadcast_to(picks[:, 0:1], (LB, 128)).astype(BF16)
    )
    dy_rows = jnp.concatenate([dot(both_hot, dy_bf).astype(BF16), others.astype(BF16)], axis=1)

    gathered, all_tokens, dy_slots = start_exchange(
        packed, own_tokens, dy_rows.reshape(NF, ROWS, MSG)
    )

    full = gathered.reshape(D, PACK)
    full_out = full[:, :D]
    full_qkv = full[:, D : D + 3 * HW]
    full_router = full[:, D + 3 * HW : D + 3 * HW + E]
    gain_one = full[:, PACK - 128].astype(F32)
    gain_two = full[:, PACK - 127].astype(F32)
    table = gathered[:, :, 0, PACK - 126 : PACK - 126 + H].reshape(NB, H).astype(F32)
    router_pad = jnp.pad(full_router, ((0, 0), (0, 128 - E)))

    x_all = all_tokens.reshape(LEN, D).astype(F32)
    r1 = norm_factor(x_all)
    xn1 = (x_all * r1 * gain_one).astype(BF16)
    qkv = dot(xn1, full_qkv).astype(BF16)
    q, k, v = qkv[:, :HW], qkv[:, HW : 2 * HW], qkv[:, 2 * HW :]

    slots = distance_base(buckets, -1, -1)
    slot_hot = (slots[:, None] == jnp.arange(NB, dtype=jnp.int32)[None, :]).astype(F32)
    own_table = lax.dynamic_slice_in_dim(table, s * HL, HL, 1)
    base = jnp.einsum("ln,nh->hl", slot_hot, own_table, precision=highest)
    base = jnp.where(slots[None, :] < 0, -1e30, base).reshape(HL, NS, SPAN)

    mixed_heads, lse = attend_forward(q, k, v, base)
    mixed = seq_exchange(mixed_heads.reshape(NS, LB, HW), 2, "exchange_mixed")
    mixed = jnp.concatenate([mixed[i] for i in range(NS)], axis=1)

    x = own_tokens.astype(F32)
    x1 = x + dot(mixed, full_out)
    r2 = norm_factor(x1)
    xn2 = (x1 * r2 * gain_two).astype(BF16)
    x_rows = dot(both_hot, xn2).astype(BF16)
    y_back, dx_back, grad_in, grad_out = run_experts(
        x_rows.reshape(NF, ROWS, D), dy_slots, router_pad, expert_in, expert_out, 4
    )
    y_back = y_back.reshape(NF * ROWS, D)
    dx_back = dx_back.reshape(NF * ROWS, D)

    logits = dot(xn2, full_router)
    pick_hot = picks[:, :, None] == jnp.arange(E, dtype=jnp.int32)[None, None, :]
    chosen = jnp.sum(jnp.where(pick_hot, logits[:, None, :], 0.0), axis=2)
    gates = jax.nn.softmax(chosen, axis=1)
    dy = dy_bf.astype(F32)

    def back(hot_rows, rows):
        return dot(hot_rows, rows, ((0,), (0,)))

    y_each = [back(held_hot[c], y_back) for c in range(2)]
    x2 = x1 + gates[:, 0:1] * y_each[0] + gates[:, 1:2] * y_each[1]
    layer_out = x2.astype(BF16).reshape(1, LB, D)
    dgate = jnp.stack([jnp.sum(dy * y, axis=1) for y in y_each], axis=1)
    dpick = gates * (dgate - jnp.sum(gates * dgate, axis=1, keepdims=True))
    dlogits = jnp.sum(jnp.where(pick_hot, dpick[:, :, None], 0.0), axis=1).astype(BF16)
    grad_router = dot(xn2, dlogits, ((0,), (0,)))
    dxn2 = back(both_hot, dx_back) + dot(dlogits, full_router, ((1,), (1,)))
    grad_gain_two = jnp.sum(dxn2 * x1 * r2, axis=0)
    scaled = dxn2 * gain_two
    dx1 = dy + r2 * scaled - x1 * (r2 * r2 * r2) * jnp.mean(scaled * x1, axis=1, keepdims=True)
    dat = dx1.astype(BF16)
    grad_w_out = dot(mixed, dat, ((0,), (0,)))
    do = dot(dat, full_out, ((1,), (1,))).astype(BF16)
    do = jnp.stack([do[:, i * HW : (i + 1) * HW] for i in range(NS)], axis=0)
    do = seq_exchange(do, 5, "exchange_grad").reshape(LEN, HW)

    dqkv, diag = attend_backward(q, k, v, do, lse, base)
    grad_table = jnp.einsum("ln,hl->nh", slot_hot, diag.reshape(HL, NS * SPAN), precision=highest)
    part = dot(dqkv, full_qkv, ((1,), (1,)))
    grad_qkv = dot(xn1, dqkv, ((0,), (0,)))
    grad_gain_one = jnp.sum(part * x_all * r1, axis=0)

    grad_misc = jnp.concatenate(
        [
            grad_gain_one.reshape(NF, share, 1),
            grad_gain_two.reshape(NF, share, 1),
            jnp.pad(grad_table[:, None, :], ((0, 0), (0, share - 1), (0, 0))),
            jnp.zeros((NF, share, 128 - 2 - HL), F32),
        ],
        axis=2,
    )
    grad_pack = jnp.concatenate(
        [
            grad_w_out.reshape(NF, share, D),
            grad_qkv.reshape(NF, share, 3 * HW),
            grad_router.reshape(NF, share, E),
            grad_misc,
        ],
        axis=2,
    ).astype(BF16)
    pack_back, part_back = last_exchange(
        grad_pack.reshape(NF // 2, 2, share, PACK), part.astype(BF16).reshape(NS, LB, D), 6
    )
    own_pack = jnp.sum(pack_back.astype(F32), axis=0)
    all_pack = seq_gather(own_pack, 7, "gather_shares")
    summed = jnp.sum(all_pack, axis=0)
    own_qkv = all_pack[:, :, D : D + 3 * HW]

    def whole(i):
        return jnp.concatenate([own_qkv[n, :, i * HW : (i + 1) * HW] for n in range(NS)], axis=1)

    grad_bias = jnp.concatenate(
        [all_pack[n, 0:1, PACK - 126 : PACK - 126 + HL] for n in range(NS)], axis=1
    )
    dxn1 = jnp.sum(part_back.astype(F32), axis=0)
    scaled = dxn1 * gain_one
    own_r1 = norm_factor(x)
    grad_x = (
        dx1
        + own_r1 * scaled
        - x * (own_r1 * own_r1 * own_r1) * jnp.mean(scaled * x, axis=1, keepdims=True)
    )
    return (
        layer_out,
        grad_x.reshape(1, LB, D),
        summed[:, PACK - 128],
        summed[:, PACK - 127],
        whole(0),
        whole(1),
        whole(2),
        summed[:, :D],
        summed[:, D + 3 * HW : D + 3 * HW + E],
        grad_bias,
        grad_in,
        grad_out,
    )


def solution(mesh):
    placed = (
        P("fsdp", "seq", None),
        P("fsdp"),
        P("fsdp"),
        P("fsdp", None),
        P("fsdp", None),
        P("fsdp", None),
        P("fsdp", None),
        P("fsdp", None),
        P("fsdp", None),
        P("fsdp", None, "seq"),
        P("fsdp", "seq", None),
        P("fsdp", "seq", None),
        P(),
        P("fsdp", "seq", None),
    )
    return jax.shard_map(
        shards,
        mesh=mesh,
        in_specs=placed,
        out_specs=(
            P("fsdp", "seq", None),
            P("fsdp", "seq", None),
            P("fsdp"),
            P("fsdp"),
            P("fsdp", None),
            P("fsdp", None),
            P("fsdp", None),
            P("fsdp", None),
            P("fsdp", None),
            P("fsdp", None),
            P("fsdp", None, "seq"),
            P("fsdp", "seq", None),
        ),
        check_vma=False,
    )
```

```python
from functools import partial

import jax
import jax.numpy as jnp
from jax import lax
from jax.experimental import pallas as pl
from jax.experimental.pallas import tpu as pltpu
from jax.sharding import PartitionSpec as P

D = 768
H = 12
HD = 64
NS = 4
NF = 32
HL = H // NS
HW = HL * HD
LB = 256
LEN = 1024
E = 64
CAP = 12
ROWS = 2 * CAP
MSG = D + 128
PACK = 1536
NB = 32
SPAN = 2 * LB

epsilon = 1e-06
highest = lax.Precision.HIGHEST
MESH = pl.DeviceIdType.MESH
F32 = jnp.float32
BF16 = jnp.bfloat16
MIB = 1024 * 1024


def any_spec():
    return pl.BlockSpec(memory_space=pl.ANY)


def vmem_spec():
    return pl.BlockSpec(memory_space=pltpu.VMEM)


def dot(a, b, dims=((1,), (0,))):
    return lax.dot_general(a, b, (dims, ((), ())), preferred_element_type=F32)


def params(collective_id=None, vmem=48):
    if collective_id is None:
        return pltpu.CompilerParams(vmem_limit_bytes=vmem * MIB)
    return pltpu.CompilerParams(
        collective_id=collective_id, has_side_effects=True, vmem_limit_bytes=vmem * MIB
    )


def place_of():
    return lax.axis_index("seq"), lax.axis_index("fsdp")


def greet_seq(s):
    barrier = pltpu.get_barrier_semaphore()
    for k in range(1, NS):
        pl.semaphore_signal(
            barrier, inc=1, device_id={"seq": lax.rem(s + k, NS)}, device_id_type=MESH
        )
    return NS - 1


def greet_fsdp(f):
    barrier = pltpu.get_barrier_semaphore()

    def one(k, carried):
        pl.semaphore_signal(
            barrier, inc=1, device_id={"fsdp": lax.rem(f + k, NF)}, device_id_type=MESH
        )
        return carried

    lax.fori_loop(1, NF, one, 0)
    return NF - 1


def arrive(count):
    pl.semaphore_wait(pltpu.get_barrier_semaphore(), count)


def send_seq(s, source, target, send, recv):
    for k in range(1, NS):
        peer = lax.rem(s + k, NS)
        pltpu.make_async_remote_copy(
            src_ref=source(peer),
            dst_ref=target,
            send_sem=send,
            recv_sem=recv,
            device_id={"seq": peer},
            device_id_type=MESH,
        ).start()


def send_fsdp(f, source, target, send, recv):
    def one(k, carried):
        peer = lax.rem(f + k, NF)
        pltpu.make_async_remote_copy(
            src_ref=source(peer),
            dst_ref=target,
            send_sem=send,
            recv_sem=recv,
            device_id={"fsdp": peer},
            device_id_type=MESH,
        ).start()
        return carried

    lax.fori_loop(1, NF, one, 0)


def await_bytes(ref, sem):
    pltpu.make_async_copy(ref, ref, sem).wait()


def hop(source, target, to, send, recv, n):
    return pltpu.make_async_remote_copy(
        src_ref=source,
        dst_ref=target,
        send_sem=send.at[n],
        recv_sem=recv.at[n],
        device_id={"seq": to},
        device_id_type=MESH,
    )


def around(s):
    return lax.rem(s + 1, NS), lax.rem(s + NS - 1, NS), lax.rem(s + 2, NS)


def start_kernel(w_ref, x_ref, dy_ref, wg, xg, dy_own, dy_near, send, recv, local):
    s, f = place_of()
    right, left, far = around(s)
    pair, core = f // 2, lax.rem(f, 2)
    arrive(greet_fsdp(f) + greet_seq(s))
    first, second = pl.ds(0, LB // 2), pl.ds(LB // 2, LB // 2)
    x_begin = [hop(x_ref, xg.at[s], to, send, recv, n) for n, to in enumerate((right, left))]
    x_relay = [
        hop(xg.at[left, first], xg.at[left, first], right, send, recv, 2),
        hop(xg.at[right, second], xg.at[right, second], left, send, recv, 3),
    ]
    half = dy_own.at[pl.ds(0, NF // 2)]
    y_begin = [
        hop(half, dy_near.at[n], to, send, recv, 4 + n) for n, to in enumerate((right, left))
    ]
    for copy in x_begin:
        copy.start()
    own_x = pltpu.make_async_copy(x_ref, xg.at[s], local.at[0])
    own_w = pltpu.make_async_copy(w_ref, wg.at[pair, core], local.at[1])
    own_dy = pltpu.make_async_copy(dy_ref.at[f], dy_own.at[f], local.at[2])
    own_dy.start()
    own_x.start()
    own_w.start()
    send_fsdp(f, lambda peer: dy_ref.at[peer], dy_own.at[f], send.at[7], recv.at[7])

    def one(k, carried):
        peer = lax.rem(pair + k, NF // 2)
        pltpu.make_async_remote_copy(
            src_ref=w_ref,
            dst_ref=wg.at[pair, core],
            send_sem=send.at[6],
            recv_sem=recv.at[6],
            device_id={"fsdp": 2 * peer + core},
            device_id_type=MESH,
        ).start()
        return carried

    lax.fori_loop(1, NF // 2, one, 0)
    for n in range(2):
        x_begin[n].wait_recv()
        x_relay[n].start()
    own_dy.wait()
    others_dy = dy_own.at[pl.ds(0, NF - 1)]
    await_bytes(others_dy, recv.at[7])
    for copy in y_begin:
        copy.start()
    own_x.wait()
    own_w.wait()
    others = wg.at[pl.ds(0, NF // 2 - 1), core]
    await_bytes(others, recv.at[6])
    swap = pltpu.make_async_remote_copy(
        src_ref=wg.at[:, core],
        dst_ref=wg.at[:, core],
        send_sem=send.at[8],
        recv_sem=recv.at[8],
        device_id={"fsdp": 2 * pair + 1 - core},
        device_id_type=MESH,
    )
    swap.start()
    for copy in x_relay + [swap] + y_begin:
        copy.wait_recv()
    for copy in x_begin + x_relay + y_begin + [swap]:
        copy.wait_send()
    await_bytes(others, send.at[6])
    await_bytes(others_dy, send.at[7])


def start_exchange(packed, tokens, dy_rows):
    return pl.pallas_call(
        start_kernel,
        out_shape=(
            jax.ShapeDtypeStruct((NF // 2, 2) + packed.shape, packed.dtype),
            jax.ShapeDtypeStruct((NS,) + tokens.shape, tokens.dtype),
            jax.ShapeDtypeStruct(dy_rows.shape, dy_rows.dtype),
            jax.ShapeDtypeStruct((2, NF // 2) + dy_rows.shape[1:], dy_rows.dtype),
        ),
        in_specs=[any_spec()] * 3,
        out_specs=(any_spec(),) * 4,
        scratch_shapes=[
            pltpu.SemaphoreType.DMA((9,)),
            pltpu.SemaphoreType.DMA((9,)),
            pltpu.SemaphoreType.DMA((3,)),
        ],
        compiler_params=params(0),
        name="start_exchange",
    )(packed, tokens, dy_rows)


def sum_pairs(f, w_ref, wg, mine, theirs, send, recv, local, first):
    pair, core = f // 2, lax.rem(f, 2)
    swap = pltpu.make_async_remote_copy(
        src_ref=w_ref.at[:, 1 - core],
        dst_ref=theirs,
        send_sem=send.at[first],
        recv_sem=recv.at[first],
        device_id={"fsdp": 2 * pair + 1 - core},
        device_id_type=MESH,
    )
    own = pltpu.make_async_copy(w_ref.at[:, core], mine, local.at[first])
    keep = pltpu.make_async_copy(mine.at[pair], wg.at[pair], local.at[first + 1])
    others = wg.at[pl.ds(0, NF // 2 - 1)]

    def begin():
        swap.start()
        own.start()

    def middle():
        own.wait()
        swap.wait_recv()

        def add(i, carried):
            mine[i] = (mine[i].astype(F32) + theirs[i].astype(F32)).astype(BF16)
            return carried

        lax.fori_loop(0, NF // 2, add, 0)

        def one(k, carried):
            peer = lax.rem(pair + k, NF // 2)
            pltpu.make_async_remote_copy(
                src_ref=mine.at[peer],
                dst_ref=wg.at[pair],
                send_sem=send.at[first + 1],
                recv_sem=recv.at[first + 1],
                device_id={"fsdp": 2 * peer + core},
                device_id_type=MESH,
            ).start()
            return carried

        lax.fori_loop(1, NF // 2, one, 0)
        keep.start()

    def finish():
        keep.wait()
        await_bytes(others, recv.at[first + 1])

    def end():
        swap.wait_send()
        await_bytes(others, send.at[first + 1])

    return begin, middle, finish, end


def last_kernel(
    b_ref, x_ref, a_ref, all_a, all_b, xg, mine, theirs, got, sum_a, sum_b, summed, work,
    send, recv, local,
):
    s, f = place_of()
    right, left, far = around(s)
    half = LB // 2
    first, second = pl.ds(0, half), pl.ds(half, half)
    arrive(greet_fsdp(f) + greet_seq(s))
    begin, middle, finish, end = sum_pairs(f, b_ref, got, mine, theirs, send, recv, local, 0)
    onward = [
        hop(x_ref.at[far, first], summed.at[0], right, send, recv, 2),
        hop(x_ref.at[far, second], summed.at[1], left, send, recv, 3),
    ]
    early = [
        hop(x_ref.at[right, second], xg.at[0, second], right, send, recv, 4),
        hop(x_ref.at[left, first], xg.at[1, first], left, send, recv, 5),
    ]
    late = [
        hop(work.at[0], xg.at[0, first], right, send, recv, 6),
        hop(work.at[1], xg.at[1, second], left, send, recv, 7),
    ]
    for copy in onward:
        copy.start()
    begin()
    for copy in early:
        copy.start()
    own_x = pltpu.make_async_copy(x_ref.at[s], xg.at[2], local.at[2])
    own_x.start()
    middle()
    for n, block, rows in ((0, right, first), (1, left, second)):
        onward[n].wait_recv()
        work[n] = (x_ref[block, rows].astype(F32) + summed[n].astype(F32)).astype(BF16)
        late[n].start()

    def total(blocks):
        value = blocks[0].astype(F32)
        for i in range(1, NF // 2):
            value = value + blocks[i].astype(F32)
        return value

    sum_a[...] = total(a_ref)
    send_seq(s, lambda peer: sum_a, all_a.at[s], send.at[8], recv.at[8])
    own_a = pltpu.make_async_copy(sum_a, all_a.at[s], local.at[3])
    own_a.start()
    finish()
    sum_b[...] = total(got)
    send_seq(s, lambda peer: sum_b, all_b.at[s], send.at[9], recv.at[9])
    own_b = pltpu.make_async_copy(sum_b, all_b.at[s], local.at[4])
    own_b.start()
    own_x.wait()
    own_a.wait()
    own_b.wait()
    for n, out in ((8, all_a), (9, all_b)):
        others = out.at[pl.ds(0, NS - 1)]
        await_bytes(others, recv.at[n])
        await_bytes(others, send.at[n])
    for copy in early + late:
        copy.wait_recv()
    for copy in onward + early + late:
        copy.wait_send()
    end()


def last_exchange(b, x, a, collective_id):
    half = (b.shape[0],) + b.shape[2:]
    return pl.pallas_call(
        last_kernel,
        out_shape=(
            jax.ShapeDtypeStruct((NS,) + a.shape[1:], F32),
            jax.ShapeDtypeStruct((NS,) + b.shape[2:], F32),
            jax.ShapeDtypeStruct((3,) + x.shape[1:], x.dtype),
        ),
        in_specs=[any_spec(), vmem_spec(), vmem_spec()],
        out_specs=(any_spec(), any_spec(), any_spec()),
        scratch_shapes=[
            pltpu.VMEM(half, BF16),
            pltpu.VMEM(half, BF16),
            pltpu.VMEM(half, BF16),
            pltpu.VMEM(a.shape[1:], F32),
            pltpu.VMEM(b.shape[2:], F32),
            pltpu.VMEM((2, LB // 2, D), BF16),
            pltpu.VMEM((2, LB // 2, D), BF16),
            pltpu.SemaphoreType.DMA((10,)),
            pltpu.SemaphoreType.DMA((10,)),
            pltpu.SemaphoreType.DMA((5,)),
        ],
        compiler_params=params(collective_id, 24),
        name="last_exchange",
    )(b, x, a)


def bias_tiles(base_ref, tiles, head):
    for d in range(NS):
        wide = jnp.broadcast_to(base_ref[head, d : d + 1, :], (LB, SPAN))
        tiles[d] = pltpu.roll(wide, 0, 1, stride=1, stride_axis=0)[:, :LB]


def score_tiles(query, key_ref, tiles, cols, block):
    parts = []
    for kb in range(block + 1):
        keys = key_ref[kb * LB : (kb + 1) * LB, cols]
        parts.append(dot(query, keys, ((1,), (1,))) * (HD**-0.5) + tiles[block - kb])
    return parts


def forward_kernel(
    q_ref, k_ref, v_ref, base_ref, dy_ref, mixed, lse_ref, dy_near, o, tiles, send, recv, local
):
    s, f = place_of()
    right, left, _ = around(s)
    arrive(greet_seq(s))
    half = dy_ref.at[pl.ds(NF // 2, NF // 2)]
    beside = [hop(half, dy_near.at[n], to, send, recv, n) for n, to in enumerate((right, left))]
    for copy in beside:
        copy.start()
    for head in range(HL):
        bias_tiles(base_ref, tiles.at[head], head)
    for block in range(NS):
        rows = slice(block * LB, (block + 1) * LB)
        for head in range(HL):
            cols = slice(head * HD, (head + 1) * HD)
            parts = score_tiles(q_ref[rows, cols], k_ref, tiles.at[head], cols, block)
            top = parts[0].max(axis=1, keepdims=True)
            for part in parts[1:]:
                top = jnp.maximum(top, part.max(axis=1, keepdims=True))
            parts = [jnp.exp(part - top) for part in parts]
            total = parts[0].sum(axis=1, keepdims=True)
            for part in parts[1:]:
                total = total + part.sum(axis=1, keepdims=True)
            inverse = 1.0 / total
            value = None
            for kb, part in enumerate(parts):
                term = dot((part * inverse).astype(BF16), v_ref[kb * LB : (kb + 1) * LB, cols])
                value = term if value is None else value + term
            o[block, :, cols] = value.astype(BF16)
            lse_ref[head, rows, :] = top + jnp.log(total)

        @pl.when(s != block)
        def _():
            pltpu.make_async_remote_copy(
                src_ref=o.at[block],
                dst_ref=mixed.at[s],
                send_sem=send.at[2],
                recv_sem=recv.at[2],
                device_id={"seq": block},
                device_id_type=MESH,
            ).start()

    own = pltpu.make_async_copy(o.at[s], mixed.at[s], local)
    own.start()
    own.wait()
    others = mixed.at[pl.ds(0, NS - 1)]
    await_bytes(others, recv.at[2])
    await_bytes(others, send.at[2])
    for copy in beside:
        copy.wait_recv()
        copy.wait_send()


def attend_forward(q, k, v, base, dy_own, collective_id):
    return pl.pallas_call(
        forward_kernel,
        out_shape=(
            jax.ShapeDtypeStruct((NS, LB, HW), BF16),
            jax.ShapeDtypeStruct((HL, LEN, 1), F32),
            jax.ShapeDtypeStruct((2, NF // 2) + dy_own.shape[1:], BF16),
        ),
        in_specs=[vmem_spec()] * 4 + [any_spec()],
        out_specs=(any_spec(), vmem_spec(), any_spec()),
        scratch_shapes=[
            pltpu.VMEM((NS, LB, HW), BF16),
            pltpu.VMEM((HL, NS, LB, LB), F32),
            pltpu.SemaphoreType.DMA((3,)),
            pltpu.SemaphoreType.DMA((3,)),
            pltpu.SemaphoreType.DMA,
        ],
        compiler_params=params(collective_id),
        name="attend_forward",
    )(q, k, v, base, dy_own)


def flip_rows(values):
    down = lax.broadcasted_iota(jnp.int32, (LB, LB), 0)
    across = lax.broadcasted_iota(jnp.int32, (LB, LB), 1)
    swap = (down + across == LB - 1).astype(BF16)
    high = values.astype(BF16)
    low = (values - high.astype(F32)).astype(BF16)
    return dot(swap, high) + dot(swap, low)


def backward_kernel(
    q_ref, k_ref, v_ref, do_ref, lse_ref, base_ref, pack_ref, g_ref, diag_ref, sums,
    do, tiles, folds, dk, dv, mine, theirs, send, recv, local,
):
    s, f = place_of()
    arrive(greet_fsdp(f) + greet_seq(s))
    begin, middle, finish, end = sum_pairs(
        f, pack_ref, sums, mine, theirs, send, recv, local, 0
    )
    send_seq(s, lambda peer: do_ref.at[peer], do.at[s], send.at[2], recv.at[2])
    own = pltpu.make_async_copy(do_ref.at[s], do.at[s], local.at[2])
    own.start()
    begin()
    own.wait()
    others = do.at[pl.ds(0, NS - 1)]
    await_bytes(others, recv.at[2])
    scale = HD**-0.5
    for head in range(HL):
        cols = slice(head * HD, (head + 1) * HD)
        bias_tiles(base_ref, tiles, head)
        for block in range(NS):
            rows = slice(block * LB, (block + 1) * LB)
            query, grad = q_ref[rows, cols], do[block, :, cols]
            lse = lse_ref[head, rows, :]
            parts = score_tiles(query, k_ref, tiles, cols, block)
            probs = [jnp.exp(part - lse) for part in parts]
            grads = [
                dot(grad, v_ref[kb * LB : (kb + 1) * LB, cols], ((1,), (1,)))
                for kb in range(block + 1)
            ]
            delta = None
            for prob, part in zip(probs, grads):
                term = (prob * part).sum(axis=1, keepdims=True)
                delta = term if delta is None else delta + term
            grad_query = None
            for kb in range(block + 1):
                keys = slice(kb * LB, (kb + 1) * LB)
                d = block - kb
                ds = probs[kb] * (grads[kb] - delta)
                if kb == 0:
                    folds[d] = ds
                else:
                    folds[d] += ds
                raw = (ds * scale).astype(BF16)
                term = dot(raw, k_ref[keys, cols])
                grad_query = term if grad_query is None else grad_query + term
                to_key = dot(raw, query, ((0,), (0,)))
                to_value = dot(probs[kb].astype(BF16), grad, ((0,), (0,)))
                if d == 0:
                    dk[keys, :] = to_key
                    dv[keys, :] = to_value
                else:
                    dk[keys, :] += to_key
                    dv[keys, :] += to_value
            g_ref[rows, cols] = grad_query.astype(BF16)
        g_ref[:, HW + head * HD : HW + (head + 1) * HD] = dk[...].astype(BF16)
        g_ref[:, 2 * HW + head * HD : 2 * HW + (head + 1) * HD] = dv[...].astype(BF16)
        for d in range(NS):
            wide = jnp.concatenate(
                [flip_rows(folds[d]), jnp.zeros((LB, SPAN - LB), F32)], axis=1
            )
            turned = pltpu.roll(wide, LB + 1, 1, stride=1, stride_axis=0)
            diag_ref[head, d : d + 1, :] = turned.sum(axis=0, keepdims=True)
        if head == 0:
            middle()
    await_bytes(others, send.at[2])
    finish()
    end()


def attend_backward(q, k, v, do, lse, base, pack, collective_id):
    half = (pack.shape[0],) + pack.shape[2:]
    return pl.pallas_call(
        backward_kernel,
        out_shape=(
            jax.ShapeDtypeStruct((LEN, 3 * HW), BF16),
            jax.ShapeDtypeStruct((HL, NS, SPAN), F32),
            jax.ShapeDtypeStruct(half, BF16),
        ),
        in_specs=[vmem_spec()] * 3 + [any_spec()] + [vmem_spec()] * 2 + [any_spec()],
        out_specs=(vmem_spec(), vmem_spec(), any_spec()),
        scratch_shapes=[
            pltpu.VMEM((NS, LB, HW), BF16),
            pltpu.VMEM((NS, LB, LB), F32),
            pltpu.VMEM((NS, LB, LB), F32),
            pltpu.VMEM((LEN, HD), F32),
            pltpu.VMEM((LEN, HD), F32),
            pltpu.VMEM(half, BF16),
            pltpu.VMEM(half, BF16),
            pltpu.SemaphoreType.DMA((3,)),
            pltpu.SemaphoreType.DMA((3,)),
            pltpu.SemaphoreType.DMA((3,)),
        ],
        compiler_params=params(collective_id),
        name="attend_backward",
    )(q, k, v, do, lse, base, pack)


def split_rows(rows):
    width = rows.shape[-1]
    half = NF // 2
    mixed = rows[:, 16:24]
    left, right = mixed[:half], mixed[half:]
    low = lax.broadcasted_iota(jnp.int32, left.shape, 1) < 4
    one = jnp.where(low, left, pltpu.roll(right, 4, 1)).reshape(half * 8, width)
    two = jnp.where(low, pltpu.roll(left, 4, 1), right).reshape(half * 8, width)
    return (
        jnp.concatenate([rows[:, 0:8].reshape(NF * 8, width), one], axis=0),
        jnp.concatenate([rows[:, 8:16].reshape(NF * 8, width), two], axis=0),
    )


def join_rows(first, second):
    width = first.shape[-1]
    half = NF // 2
    one = first[NF * 8 :].reshape(half, 8, width)
    two = second[NF * 8 :].reshape(half, 8, width)
    low = lax.broadcasted_iota(jnp.int32, one.shape, 1) < 4
    left = jnp.where(low, one, pltpu.roll(two, 4, 1))
    right = jnp.where(low, pltpu.roll(one, 4, 1), two)
    return jnp.concatenate(
        [
            first[: NF * 8].reshape(NF, 8, width),
            second[: NF * 8].reshape(NF, 8, width),
            jnp.concatenate([left, right], axis=0),
        ],
        axis=1,
    )


def expert_rows(x, dy, ids, own, router, w_in, w_out):
    logits = dot(x, router)
    lane = lax.broadcasted_iota(jnp.int32, logits.shape, 1)
    one = jnp.sum(jnp.where(lane == own, logits, 0.0), axis=1, keepdims=True)
    two = jnp.sum(jnp.where(lane == ids, logits, 0.0), axis=1, keepdims=True)
    top = jnp.maximum(one, two)
    one, two = jnp.exp(one - top), jnp.exp(two - top)
    gate = one / (one + two)
    grad = (dy * gate).astype(BF16)
    u = dot(x, w_in)
    square = u * u
    tanh = jnp.tanh(u * (0.7978845608028654 + (0.7978845608028654 * 0.044715) * square))
    half = 0.5 * (1.0 + tanh)
    hid = (u * half).astype(BF16)
    slope = half + (0.5 * u) * (1.0 - tanh * tanh) * (
        0.7978845608028654 + (3.0 * 0.7978845608028654 * 0.044715) * square
    )
    y = dot(hid, w_out)
    du = (dot(grad, w_out, ((1,), (1,))) * slope).astype(BF16)
    dx = dot(du, w_in, ((1,), (1,)))
    return y, dx, hid, grad, du


def expert_kernel(
    x_ref, dy_own, near_a, near_b, router_ref, wi_ref, wo_ref,
    y_out, dx_out, gi_ref, go_ref, dy_far,
    x, dy, part, near, summed, kept, send, recv, local,
):
    s, f = place_of()
    right, left, far = around(s)
    half = NF // 2
    first, second = pl.ds(0, half), pl.ds(half, half)
    columns = [pl.ds(0, D // 2), pl.ds(D // 2, D // 2)]
    arrive(greet_fsdp(f) + greet_seq(s))

    def step_to(source, target, to, n):
        return hop(source, target, to, send, recv, n)

    for c in range(2):
        send_fsdp(
            f,
            lambda peer: x_ref.at[peer, :, columns[c]],
            x.at[s, f, :, columns[c]],
            send.at[c],
            recv.at[c],
        )
    dy_relay = [
        step_to(near_a.at[0], dy_far.at[first], right, 2),
        step_to(near_b.at[1], dy_far.at[second], left, 3),
    ]
    for copy in dy_relay:
        copy.start()
    own_x = pltpu.make_async_copy(x_ref.at[f], x.at[s, f], local.at[0])
    own_x.start()
    gi_ref[...] = jnp.zeros_like(gi_ref)
    go_ref[...] = jnp.zeros_like(go_ref)
    begin, early, onward, late = [], [], [], []
    for c in range(2):
        block = x.at[s, :, :, columns[c]]
        begin.append([step_to(block, block, to, 4 + 2 * c + n) for n, to in enumerate((right, left))])
    relay = [
        step_to(x.at[left, first], x.at[left, first], right, 8),
        step_to(x.at[right, second], x.at[right, second], left, 9),
    ]
    for a in range(2):
        early.append(
            [
                step_to(part.at[a, right, second], near.at[a, 0, second], right, 10 + 2 * a),
                step_to(part.at[a, left, first], near.at[a, 1, first], left, 11 + 2 * a),
            ]
        )
        onward.append(
            [
                step_to(part.at[a, far, first], summed.at[a, 0], right, 14 + 2 * a),
                step_to(part.at[a, far, second], summed.at[a, 1], left, 15 + 2 * a),
            ]
        )
        late.append(
            [
                [
                    step_to(
                        part.at[a, right, first, :, columns[c]],
                        near.at[a, 0, first, :, columns[c]],
                        right,
                        18 + 4 * a + 2 * c,
                    ),
                    step_to(
                        part.at[a, left, second, :, columns[c]],
                        near.at[a, 1, second, :, columns[c]],
                        left,
                        19 + 4 * a + 2 * c,
                    ),
                ]
                for c in range(2)
            ]
        )
    own_x.wait()
    others_x = [x.at[s, pl.ds(0, NF - 1), :, columns[c]] for c in range(2)]
    for c in range(2):
        await_bytes(others_x[c], recv.at[c])
        for copy in begin[c]:
            copy.start()

    def step(k, carried):
        chunk = lax.rem(s + jnp.where(k == 1, 3, jnp.where(k == 0, 0, k - 1)), NS)

        @pl.when(k == 3)
        def _():
            for copy in dy_relay + relay:
                copy.wait_recv()

        for n, (low, high) in enumerate(
            (
                (dy_own.at[first], dy_own.at[second]),
                (near_a.at[0], near_b.at[0]),
                (near_a.at[1], near_b.at[1]),
                (dy_far.at[first], dy_far.at[second]),
            )
        ):

            @pl.when(k == n)
            def _():
                loads = [
                    pltpu.make_async_copy(low, dy.at[first], local.at[1]),
                    pltpu.make_async_copy(high, dy.at[second], local.at[2]),
                ]
                for load in loads:
                    load.start()
                for load in loads:
                    load.wait()

        @pl.when(k == 1)
        def _():
            for n in range(2):
                for c in range(2):
                    begin[c][n].wait_recv()
                relay[n].start()

        xs = split_rows(x[chunk].astype(F32))
        dys = split_rows(dy[...].astype(F32))
        ys, dxs = [], []
        for j in range(2):
            rows = xs[j].astype(BF16)
            ids = dys[j][:, D:].astype(jnp.int32)
            y, dx, hid, grad, du = expert_rows(
                rows, dys[j][:, :D], ids, 2 * f + j, router_ref[...], wi_ref[j], wo_ref[j]
            )
            ys.append(y)
            dxs.append(dx)
            for n, value in enumerate((rows, hid, grad, du)):
                kept[n, j] = value
        part[0, chunk] = join_rows(*ys).astype(BF16)
        part[1, chunk] = join_rows(*dxs).astype(BF16)

        @pl.when(k == 1)
        def _():
            for a in range(2):
                early[a][1].start()

        @pl.when(k == 2)
        def _():
            early[0][0].start()

        @pl.when(k == 3)
        def _():
            for a in range(2):
                for n in range(2):
                    onward[a][n].start()

        for j in range(2):
            go_ref[j] += dot(kept[1, j], kept[2, j], ((0,), (0,)))
            gi_ref[j] += dot(kept[0, j], kept[3, j], ((0,), (0,)))
        return carried

    lax.fori_loop(0, NS, step, 0)

    def add(a, block, offset, cols, other):
        def one(i, carried):
            total = part[a, block, offset + i, :, cols].astype(F32) + other(i)
            part[a, block, offset + i, :, cols] = total.astype(BF16)
            return carried

        return one

    for a in range(2):
        for n in range(2):
            onward[a][n].wait_recv()
        for c in range(2):
            for n, block, offset in ((0, right, 0), (1, left, half)):
                lax.fori_loop(
                    0,
                    half,
                    add(
                        a,
                        block,
                        offset,
                        columns[c],
                        lambda i: summed[a, n, i, :, columns[c]].astype(F32),
                    ),
                    0,
                )
                late[a][c][n].start()
        if a == 0:
            early[1][0].start()
    outs = (y_out, dx_out)
    pieces = []
    for a in range(2):
        for n in range(2):
            early[a][n].wait_recv()
        for c in range(2):
            cols = columns[c]
            for n in range(2):
                late[a][c][n].wait_recv()
            lax.fori_loop(
                0,
                NF,
                add(
                    a,
                    s,
                    0,
                    cols,
                    lambda i: near[a, 0, i, :, cols].astype(F32)
                    + near[a, 1, i, :, cols].astype(F32),
                ),
                0,
            )
            p = 2 * a + c
            send_fsdp(
                f,
                lambda peer: part.at[a, s, peer, :, cols],
                outs[a].at[f, :, cols],
                send.at[26 + p],
                recv.at[26 + p],
            )
            keep = pltpu.make_async_copy(
                part.at[a, s, f, :, cols], outs[a].at[f, :, cols], local.at[3 + p]
            )
            keep.start()
            pieces.append((keep, outs[a].at[pl.ds(0, NF - 1), :, cols], 26 + p))
    for keep, others, n in pieces:
        keep.wait()
        await_bytes(others, recv.at[n])
        await_bytes(others, send.at[n])
    for a in range(2):
        for copy in early[a] + onward[a] + late[a][0] + late[a][1]:
            copy.wait_send()
    for copy in begin[0] + begin[1] + relay + dy_relay:
        copy.wait_send()
    for c in range(2):
        await_bytes(others_x[c], send.at[c])


def run_experts(x, dy, near_a, near_b, router, w_in, w_out, collective_id):
    rows = (NF, ROWS, D)
    return pl.pallas_call(
        expert_kernel,
        out_shape=(
            jax.ShapeDtypeStruct(rows, BF16),
            jax.ShapeDtypeStruct(rows, BF16),
            jax.ShapeDtypeStruct((2, D, D), F32),
            jax.ShapeDtypeStruct((2, D, D), F32),
            jax.ShapeDtypeStruct((NF, ROWS, MSG), BF16),
        ),
        in_specs=[any_spec()] * 4 + [vmem_spec()] * 3,
        out_specs=(any_spec(), any_spec(), vmem_spec(), vmem_spec(), any_spec()),
        scratch_shapes=[
            pltpu.VMEM((NS,) + rows, BF16),
            pltpu.VMEM((NF, ROWS, MSG), BF16),
            pltpu.VMEM((2, NS) + rows, BF16),
            pltpu.VMEM((2, 2) + rows, BF16),
            pltpu.VMEM((2, 2, NF // 2, ROWS, D), BF16),
            pltpu.VMEM((4, 2, NF * CAP, D), BF16),
            pltpu.SemaphoreType.DMA((30,)),
            pltpu.SemaphoreType.DMA((30,)),
            pltpu.SemaphoreType.DMA((7,)),
        ],
        compiler_params=params(collective_id, 63),
        name="run_experts",
    )(x, dy, near_a, near_b, router, w_in, w_out)


def row_factor(values):
    return lax.rsqrt(jnp.mean(values * values, axis=1, keepdims=True) + epsilon)


def token_kernel(
    y_ref, dx_ref, hot_ref, x1_ref, xn2_ref, dy_ref, picks_ref, gain_ref, router_ref, w_ref,
    mixed_ref, out_ref, dx1_ref, do_ref, pack_ref,
):
    xn2, x1, router = xn2_ref[...], x1_ref[...], router_ref[...]
    dy = dy_ref[...].astype(F32)
    logits = dot(xn2, router)
    lane = lax.broadcasted_iota(jnp.int32, logits.shape, 1)
    named = [lane == picks_ref[:, c : c + 1] for c in range(2)]
    chosen = [jnp.sum(jnp.where(n, logits, 0.0), axis=1, keepdims=True) for n in named]
    top = jnp.maximum(chosen[0], chosen[1])
    chosen = [jnp.exp(value - top) for value in chosen]
    both = chosen[0] + chosen[1]
    gates = [value / both for value in chosen]
    ys = [dot(hot_ref[c], y_ref[...], ((0,), (0,))) for c in range(2)]
    out_ref[...] = (x1 + (gates[0] * ys[0] + gates[1] * ys[1])).astype(BF16)
    dgates = [jnp.sum(dy * y, axis=1, keepdims=True) for y in ys]
    mean = gates[0] * dgates[0] + gates[1] * dgates[1]
    dpicks = [gates[c] * (dgates[c] - mean) for c in range(2)]
    dlogits = sum(jnp.where(named[c], dpicks[c], 0.0) for c in range(2)).astype(BF16)
    dxn2 = dot(hot_ref[0] + hot_ref[1], dx_ref[...], ((0,), (0,)))
    dxn2 = dxn2 + dot(dlogits, router, ((1,), (1,)))
    r2 = row_factor(x1)
    terms = (dxn2 * x1 * r2).astype(BF16)
    grad_gain = dot(terms, jnp.ones((LB, 128), BF16), ((0,), (0,)))
    grad_router = dot(xn2, dlogits, ((0,), (0,)))
    lane = lax.broadcasted_iota(jnp.int32, grad_gain.shape, 1)
    pack_ref[:, D:] = jnp.where(lane == E, grad_gain, grad_router).astype(BF16)
    scaled = dxn2 * gain_ref[...]
    mean = jnp.mean(scaled * x1, axis=1, keepdims=True)
    dx1 = dy + r2 * scaled - x1 * (r2 * r2 * r2) * mean
    dx1_ref[...] = dx1
    dat = dx1.astype(BF16)
    for i in range(NS):
        rows = slice(i * HW, (i + 1) * HW)
        do_ref[i] = dot(dat, w_ref[rows, :], ((1,), (1,))).astype(BF16)
        pack_ref[rows, :D] = dot(mixed_ref[i], dat, ((0,), (0,))).astype(BF16)


def token_side(y, dx, hot, x1, xn2, dy, picks, gain, router, w_out, mixed):
    return pl.pallas_call(
        token_kernel,
        out_shape=(
            jax.ShapeDtypeStruct((LB, D), BF16),
            jax.ShapeDtypeStruct((LB, D), F32),
            jax.ShapeDtypeStruct((NS, LB, HW), BF16),
            jax.ShapeDtypeStruct((D, D + 128), BF16),
        ),
        in_specs=[vmem_spec()] * 11,
        out_specs=(vmem_spec(),) * 4,
        compiler_params=params(),
        name="token_side",
    )(y, dx, hot, x1, xn2, dy, picks, gain, router, w_out, mixed)


def project_kernel(
    g_ref, x_ref, gain_ref, w_ref, slots_ref, diag_ref, gi_ref, go_ref,
    part_ref, pack_ref, gi_out, go_out, weight, held, local,
):
    loads = [
        pltpu.make_async_copy(gi_ref, held.at[0], local.at[0]),
        pltpu.make_async_copy(go_ref, held.at[1], local.at[1]),
    ]
    stores = [
        pltpu.make_async_copy(held.at[0], gi_out, local.at[2]),
        pltpu.make_async_copy(held.at[1], go_out, local.at[3]),
    ]
    for copy in loads:
        copy.start()
    weight[...] = jnp.zeros_like(weight)
    misc = jnp.zeros((D, 64), F32)
    for block in range(NS):
        rows = slice(block * LB, (block + 1) * LB)
        x = x_ref[rows, :].astype(F32)
        r1 = row_factor(x)
        xn1 = (x * r1 * gain_ref[...]).astype(BF16)
        g = g_ref[rows, :]
        weight[...] += dot(xn1, g, ((0,), (0,)))
        part = dot(g, w_ref[...], ((1,), (1,)))
        part_ref[block] = part.astype(BF16)
        terms = (part * x * r1).astype(BF16)
        misc = misc + dot(terms, jnp.ones((LB, 64), BF16), ((0,), (0,)))
        if block < 2:
            loads[block].wait()
            stores[block].start()
    lane = lax.broadcasted_iota(jnp.int32, misc.shape, 1)
    row = lax.broadcasted_iota(jnp.int32, (NB, NS * SPAN), 0)
    hot = (slots_ref[...] == row).astype(BF16)
    diag = jnp.concatenate(
        [jnp.zeros((8, NS * SPAN), F32), diag_ref[...], jnp.zeros((56 - HL, NS * SPAN), F32)],
        axis=0,
    )
    high = diag.astype(BF16)
    low = (diag - high.astype(F32)).astype(BF16)
    table = dot(hot, high, ((1,), (1,))) + dot(hot, low, ((1,), (1,)))
    table = jnp.broadcast_to(table[:, None, :], (NB, D // NF, 64)).reshape(D, 64)
    misc = jnp.where(lane == 0, misc, table)
    pack_ref[:, : 3 * HW] = weight[...].astype(BF16)
    pack_ref[:, 3 * HW :] = misc.astype(BF16)
    for copy in stores:
        copy.wait()


def project_back(g, x, gain, w, slots, diag, gi, go):
    return pl.pallas_call(
        project_kernel,
        out_shape=(
            jax.ShapeDtypeStruct((NS, LB, D), BF16),
            jax.ShapeDtypeStruct((D, 3 * HW + 64), BF16),
            jax.ShapeDtypeStruct(gi.shape, F32),
            jax.ShapeDtypeStruct(go.shape, F32),
        ),
        in_specs=[vmem_spec()] * 6 + [any_spec()] * 2,
        out_specs=(vmem_spec(), vmem_spec(), any_spec(), any_spec()),
        scratch_shapes=[
            pltpu.VMEM((D, 3 * HW), F32),
            pltpu.VMEM((2,) + gi.shape, F32),
            pltpu.SemaphoreType.DMA((4,)),
        ],
        compiler_params=params(),
        name="project_back",
    )(g, x, gain, w, slots, diag, gi, go)


def finish_kernel(
    a_ref, b_ref, part_ref, x_ref, dx1_ref, gain_ref,
    gx_ref, g1_ref, g2_ref, wq_ref, wk_ref, wv_ref, wo_ref, router_ref, table_ref,
):
    total = a_ref[0] + a_ref[1] + a_ref[2] + a_ref[3]
    wo_ref[...] = total[:, :D]
    router_ref[...] = total[:, D : D + E]
    g2_ref[...] = total[:, D + E : D + E + 1]
    misc = [b_ref[n, :, 3 * HW :] for n in range(NS)]
    g1_ref[...] = (misc[0] + misc[1] + misc[2] + misc[3])[:, 0:1]
    table_ref[...] = jnp.concatenate([m[0:1, 8 : 8 + HL] for m in misc], axis=1)
    for i, out in enumerate((wq_ref, wk_ref, wv_ref)):
        out[...] = jnp.concatenate(
            [b_ref[n, :, i * HW : (i + 1) * HW] for n in range(NS)], axis=1
        )
    x = x_ref[...].astype(F32)
    r1 = row_factor(x)
    dxn1 = part_ref[0].astype(F32) + part_ref[1].astype(F32) + part_ref[2].astype(F32)
    scaled = dxn1 * gain_ref[...]
    mean = jnp.mean(scaled * x, axis=1, keepdims=True)
    gx_ref[...] = dx1_ref[...] + r1 * scaled - x * (r1 * r1 * r1) * mean


def finish(a, b, part, x, dx1, gain):
    share = D // NF
    return pl.pallas_call(
        finish_kernel,
        out_shape=(
            jax.ShapeDtypeStruct((LB, D), F32),
            jax.ShapeDtypeStruct((share, 1), F32),
            jax.ShapeDtypeStruct((share, 1), F32),
            jax.ShapeDtypeStruct((share, D), F32),
            jax.ShapeDtypeStruct((share, D), F32),
            jax.ShapeDtypeStruct((share, D), F32),
            jax.ShapeDtypeStruct((share, D), F32),
            jax.ShapeDtypeStruct((share, E), F32),
            jax.ShapeDtypeStruct((1, H), F32),
        ),
        in_specs=[vmem_spec()] * 6,
        out_specs=(vmem_spec(),) * 9,
        compiler_params=params(),
        name="finish",
    )(a, b, part, x, dx1, gain)


def distance_base(values, near, far):
    long = jnp.concatenate(
        [jnp.full((LB,), near, values.dtype), values, jnp.full((1,), far, values.dtype)]
    )
    rows = []
    for d in range(NS):
        rows.append(long[d * LB + 1 : d * LB + LB + 1][::-1])
        rows.append(long[LB + d * LB + 1 : LB + d * LB + LB + 1][::-1])
    return jnp.concatenate(rows)


def norm_factor(values):
    return lax.rsqrt(jnp.mean(values * values, axis=-1, keepdims=True) + epsilon)


def shards(
    tokens,
    gain_attn,
    gain_ffn,
    w_query,
    w_key,
    w_value,
    w_out,
    router,
    bias_table,
    expert_in,
    expert_out,
    choices,
    buckets,
    cotangent,
):
    s = lax.axis_index("seq")
    share = D // NF
    own_tokens = tokens.reshape(LB, D)

    def own_heads(w):
        return lax.dynamic_slice_in_dim(w, s * HW, HW, 1)

    misc = jnp.concatenate(
        [
            gain_attn[:, None],
            gain_ffn[:, None],
            jnp.pad(bias_table, ((0, share - 1), (0, 0))),
            jnp.zeros((share, 128 - 2 - H), BF16),
        ],
        axis=1,
    )
    packed = jnp.concatenate(
        [w_out, own_heads(w_query), own_heads(w_key), own_heads(w_value), router, misc], axis=1
    )

    picks = choices.reshape(LB, 2)
    flat = picks.reshape(2 * LB)
    hot = flat[:, None] == jnp.arange(E, dtype=jnp.int32)[None, :]
    order = jnp.arange(2 * LB, dtype=jnp.int32)
    before = (order[:, None] > order[None, :]).astype(BF16)
    counts = dot(before, hot.astype(BF16))
    rank = jnp.sum(jnp.where(hot, counts, 0.0), axis=1).astype(jnp.int32)
    odd = flat % 2
    row = jnp.where(rank < 8, 8 * odd + rank, 16 + 4 * odd + rank - 8)
    places = ((flat // 2) * ROWS + row).reshape(LB, 2)
    slot_ids = jnp.arange(NF * ROWS, dtype=jnp.int32)
    held = [slot_ids[:, None] == places[None, :, c] for c in range(2)]
    held_hot = [h.astype(BF16) for h in held]
    both_hot = (held[0] | held[1]).astype(BF16)
    dy_bf = cotangent.reshape(LB, D)
    others = dot(held_hot[0], jnp.broadcast_to(picks[:, 1:2], (LB, 128)).astype(BF16)) + dot(
        held_hot[1], jnp.broadcast_to(picks[:, 0:1], (LB, 128)).astype(BF16)
    )
    dy_rows = jnp.concatenate([dot(both_hot, dy_bf).astype(BF16), others.astype(BF16)], axis=1)

    gathered, all_tokens, dy_own, near_a = start_exchange(
        packed, own_tokens, dy_rows.reshape(NF, ROWS, MSG)
    )

    full = gathered.reshape(D, PACK)
    full_out = full[:, :D]
    full_qkv = full[:, D : D + 3 * HW]
    full_router = full[:, D + 3 * HW : D + 3 * HW + E]
    gain_one = full[:, PACK - 128].astype(F32)
    gain_two = full[:, PACK - 127].astype(F32)
    table = gathered[:, :, 0, PACK - 126 : PACK - 126 + H].reshape(NB, H).astype(F32)
    router_pad = jnp.pad(full_router, ((0, 0), (0, 128 - E)))

    x_all = all_tokens.reshape(LEN, D).astype(F32)
    r1 = norm_factor(x_all)
    xn1 = (x_all * r1 * gain_one).astype(BF16)
    qkv = dot(xn1, full_qkv).astype(BF16)
    q, k, v = qkv[:, :HW], qkv[:, HW : 2 * HW], qkv[:, 2 * HW :]

    slots = distance_base(buckets, -1, -1)
    slot_hot = (slots[:, None] == jnp.arange(NB, dtype=jnp.int32)[None, :]).astype(F32)
    own_table = lax.dynamic_slice_in_dim(table, s * HL, HL, 1)
    base = jnp.einsum("ln,nh->hl", slot_hot, own_table, precision=highest)
    base = jnp.where(slots[None, :] < 0, -1e30, base).reshape(HL, NS, SPAN)

    mixed, lse, near_b = attend_forward(q, k, v, base, dy_own, 1)

    x = own_tokens.astype(F32)
    x1 = x + sum(dot(mixed[i], full_out[i * HW : (i + 1) * HW]) for i in range(NS))
    xn2 = (x1 * norm_factor(x1) * gain_two).astype(BF16)
    x_rows = dot(both_hot, xn2).astype(BF16)
    y_back, dx_back, grad_in, grad_out, _ = run_experts(
        x_rows.reshape(NF, ROWS, D), dy_own, near_a, near_b, router_pad, expert_in, expert_out, 2
    )
    layer_out, dx1, do, pack_a = token_side(
        y_back.reshape(NF * ROWS, D),
        dx_back.reshape(NF * ROWS, D),
        jnp.stack(held_hot),
        x1,
        xn2,
        dy_bf,
        picks,
        gain_two.reshape(1, D),
        router_pad,
        full_out,
        mixed,
    )
    dqkv, diag, shares_a = attend_backward(
        q, k, v, do, lse, base, pack_a.reshape(NF // 2, 2, share, D + 128), 3
    )
    part, pack_b, grad_in, grad_out = project_back(
        dqkv,
        all_tokens.reshape(LEN, D),
        gain_one.reshape(1, D),
        full_qkv,
        slots.reshape(1, NS * SPAN),
        diag.reshape(HL, NS * SPAN),
        grad_in,
        grad_out,
    )
    all_a, all_b, part_back = last_exchange(
        pack_b.reshape(NF // 2, 2, share, 3 * HW + 64), part, shares_a, 4
    )
    grad_x, grad_one, grad_two, grad_q, grad_k, grad_v, grad_o, grad_router, grad_table = finish(
        all_a, all_b, part_back, own_tokens, dx1, gain_one.reshape(1, D)
    )
    return (
        layer_out.reshape(1, LB, D),
        grad_x.reshape(1, LB, D),
        grad_one.reshape(share),
        grad_two.reshape(share),
        grad_q,
        grad_k,
        grad_v,
        grad_o,
        grad_router,
        grad_table,
        grad_in,
        grad_out,
    )


def solution(mesh):
    placed = (
        P("fsdp", "seq", None),
        P("fsdp"),
        P("fsdp"),
        P("fsdp", None),
        P("fsdp", None),
        P("fsdp", None),
        P("fsdp", None),
        P("fsdp", None),
        P("fsdp", None),
        P("fsdp", None, "seq"),
        P("fsdp", "seq", None),
        P("fsdp", "seq", None),
        P(),
        P("fsdp", "seq", None),
    )
    return jax.shard_map(
        shards,
        mesh=mesh,
        in_specs=placed,
        out_specs=(
            P("fsdp", "seq", None),
            P("fsdp", "seq", None),
            P("fsdp"),
            P("fsdp"),
            P("fsdp", None),
            P("fsdp", None),
            P("fsdp", None),
            P("fsdp", None),
            P("fsdp", None),
            P("fsdp", None),
            P("fsdp", None, "seq"),
            P("fsdp", "seq", None),
        ),
        check_vma=False,
    )
```

```python
from functools import partial

import jax
import jax.numpy as jnp
from jax import lax
from jax.experimental import pallas as pl
from jax.experimental.pallas import tpu as pltpu
from jax.sharding import PartitionSpec as P

D = 768
H = 12
HD = 64
NS = 4
NF = 32
HL = H // NS
HW = HL * HD
LB = 256
LEN = 1024
E = 64
CAP = 12
ROWS = 2 * CAP
MSG = D + 128
PACK = 1536
NB = 32
MISC = PACK - 128
SPAN = 2 * LB

epsilon = 1e-06
MESH = pl.DeviceIdType.MESH
F32 = jnp.float32
BF16 = jnp.bfloat16
MIB = 1024 * 1024


def any_spec():
    return pl.BlockSpec(memory_space=pl.ANY)


def hbm_spec():
    return pl.BlockSpec(memory_space=pltpu.HBM)


def vmem_spec():
    return pl.BlockSpec(memory_space=pltpu.VMEM)


def dot(a, b, dims=((1,), (0,))):
    return lax.dot_general(a, b, (dims, ((), ())), preferred_element_type=F32)


def row_factor(values):
    return lax.rsqrt(jnp.mean(values * values, axis=1, keepdims=True) + epsilon)


def params(collective_id=None, vmem=63):
    if collective_id is None:
        return pltpu.CompilerParams(vmem_limit_bytes=vmem * MIB)
    return pltpu.CompilerParams(
        collective_id=collective_id, has_side_effects=True, vmem_limit_bytes=vmem * MIB
    )


def place_of():
    return lax.axis_index("seq"), lax.axis_index("fsdp")


def greet_seq(s):
    barrier = pltpu.get_barrier_semaphore()
    for k in range(1, NS):
        pl.semaphore_signal(
            barrier, inc=1, device_id={"seq": lax.rem(s + k, NS)}, device_id_type=MESH
        )
    return NS - 1


def greet_fsdp(f):
    barrier = pltpu.get_barrier_semaphore()

    def one(k, carried):
        pl.semaphore_signal(
            barrier, inc=1, device_id={"fsdp": lax.rem(f + k, NF)}, device_id_type=MESH
        )
        return carried

    lax.fori_loop(1, NF, one, 0)
    return NF - 1


def arrive(count):
    pl.semaphore_wait(pltpu.get_barrier_semaphore(), count)


def send_seq(s, source, target, send, recv):
    for k in range(1, NS):
        peer = lax.rem(s + k, NS)
        pltpu.make_async_remote_copy(
            src_ref=source(peer),
            dst_ref=target,
            send_sem=send,
            recv_sem=recv,
            device_id={"seq": peer},
            device_id_type=MESH,
        ).start()


def send_fsdp(f, source, target, send, recv):
    def one(k, carried):
        peer = lax.rem(f + k, NF)
        pltpu.make_async_remote_copy(
            src_ref=source(peer),
            dst_ref=target,
            send_sem=send,
            recv_sem=recv,
            device_id={"fsdp": peer},
            device_id_type=MESH,
        ).start()
        return carried

    lax.fori_loop(1, NF, one, 0)


def await_bytes(ref, sem):
    pltpu.make_async_copy(ref, ref, sem).wait()


def hop(source, target, to, send, recv, n):
    return pltpu.make_async_remote_copy(
        src_ref=source,
        dst_ref=target,
        send_sem=send.at[n],
        recv_sem=recv.at[n],
        device_id={"seq": to},
        device_id_type=MESH,
    )


def around(s):
    return lax.rem(s + 1, NS), lax.rem(s + NS - 1, NS), lax.rem(s + 2, NS)


def slot_hots(picks):
    lane = lax.broadcasted_iota(jnp.int32, (LB, E), 1)
    named = [picks[:, c : c + 1] == lane for c in range(2)]
    down = lax.broadcasted_iota(jnp.int32, (LB, LB), 0)
    across = lax.broadcasted_iota(jnp.int32, (LB, LB), 1)
    counts = dot((across < down).astype(BF16), (named[0] | named[1]).astype(BF16))
    slots = lax.broadcasted_iota(jnp.int32, (LB, NF * ROWS), 1)
    hots = []
    for c in range(2):
        rank = jnp.sum(jnp.where(named[c], counts, 0.0), axis=1, keepdims=True).astype(jnp.int32)
        pick = picks[:, c : c + 1]
        odd = pick & 1
        row = jnp.where(rank < 8, 8 * odd + rank, 8 + 4 * odd + rank)
        hots.append((slots == (pick >> 1) * ROWS + row).astype(BF16))
    return hots


def start_kernel(
    wo_ref, wq_ref, wk_ref, wv_ref, router_ref, misc_ref, x_ref, picks_ref, dy_in,
    wg_out, xg, dy_own, dy_near, hots_out, packed, wg, dy_rows, hots, send, recv, local,
):
    s, f = place_of()
    right, left, far = around(s)
    pair, core = f // 2, lax.rem(f, 2)
    packed[:, :D] = wo_ref[...]
    for i in range(NS):

        @pl.when(s == i)
        def _():
            for n, w in enumerate((wq_ref, wk_ref, wv_ref)):
                at = D + n * HW
                packed[:, at : at + HW] = w[:, i * HW : (i + 1) * HW]

    packed[:, D + 3 * HW : MISC] = jnp.zeros((D // NF, MISC - D - 3 * HW), BF16)
    packed[:, MISC : MISC + E] = router_ref[...]
    packed[:, MISC + E :] = misc_ref[...]
    count = greet_fsdp(f) + greet_seq(s)
    picks = picks_ref[...]
    one_hot, two_hot = slot_hots(picks)
    hots[0] = one_hot
    hots[1] = two_hot
    dy = dot(one_hot + two_hot, dy_in[...], ((0,), (0,)))
    dy_rows[:, :, :D] = dy.reshape(NF, ROWS, D).astype(BF16)
    named = [jnp.broadcast_to(picks[:, c : c + 1].astype(F32), (LB, 128)) for c in range(2)]
    others = dot(one_hot, named[1].astype(BF16), ((0,), (0,)))
    others = others + dot(two_hot, named[0].astype(BF16), ((0,), (0,)))
    dy_rows[:, :, D:] = others.reshape(NF, ROWS, 128).astype(BF16)
    arrive(count)
    first, second = pl.ds(0, LB // 2), pl.ds(LB // 2, LB // 2)
    x_begin = [hop(x_ref, xg.at[s], to, send, recv, n) for n, to in enumerate((right, left))]
    x_relay = [
        hop(xg.at[left, first], xg.at[left, first], right, send, recv, 2),
        hop(xg.at[right, second], xg.at[right, second], left, send, recv, 3),
    ]
    half = dy_own.at[pl.ds(0, NF // 2)]
    y_begin = [
        hop(half, dy_near.at[n], to, send, recv, 4 + n) for n, to in enumerate((right, left))
    ]
    for copy in x_begin:
        copy.start()
    send_fsdp(f, lambda peer: dy_rows.at[peer], dy_own.at[f], send.at[7], recv.at[7])

    def one(k, carried):
        peer = lax.rem(pair + k, NF // 2)
        pltpu.make_async_remote_copy(
            src_ref=packed,
            dst_ref=wg.at[pair, core],
            send_sem=send.at[6],
            recv_sem=recv.at[6],
            device_id={"fsdp": 2 * peer + core},
            device_id_type=MESH,
        ).start()
        return carried

    lax.fori_loop(1, NF // 2, one, 0)
    own_x = pltpu.make_async_copy(x_ref, xg.at[s], local.at[0])
    own_w = pltpu.make_async_copy(packed, wg.at[pair, core], local.at[1])
    own_x.start()
    own_w.start()
    own_dy = pltpu.make_async_copy(dy_rows.at[f], dy_own.at[f], local.at[2])
    own_dy.start()
    keep = pltpu.make_async_copy(hots, hots_out, local.at[3])
    keep.start()
    for n in range(2):
        x_begin[n].wait_recv()
        x_relay[n].start()
    own_w.wait()
    others_w = wg.at[pl.ds(0, NF // 2 - 1), core]
    swap = pltpu.make_async_remote_copy(
        src_ref=wg.at[:, core],
        dst_ref=wg.at[:, core],
        send_sem=send.at[8],
        recv_sem=recv.at[8],
        device_id={"fsdp": 2 * pair + 1 - core},
        device_id_type=MESH,
    )
    own_dy.wait()
    others_dy = dy_own.at[pl.ds(0, NF - 1)]
    await_bytes(others_dy, recv.at[7])
    for copy in y_begin:
        copy.start()
    await_bytes(others_w, recv.at[6])
    swap.start()
    swap.wait_recv()
    store = pltpu.make_async_copy(wg, wg_out, local.at[4])
    store.start()
    own_x.wait()
    keep.wait()
    store.wait()
    for copy in x_relay + y_begin:
        copy.wait_recv()
    for copy in x_begin + x_relay + y_begin + [swap]:
        copy.wait_send()
    await_bytes(others_w, send.at[6])
    await_bytes(others_dy, send.at[7])


def start_exchange(w_out, w_query, w_key, w_value, router, misc, tokens, picks, dy):
    share = D // NF
    rows = (NF, ROWS, MSG)
    return pl.pallas_call(
        start_kernel,
        out_shape=(
            jax.ShapeDtypeStruct((NF // 2, 2, share, PACK), BF16),
            jax.ShapeDtypeStruct((NS, LB, D), BF16),
            jax.ShapeDtypeStruct(rows, BF16),
            jax.ShapeDtypeStruct((2, NF // 2, ROWS, MSG), BF16),
            jax.ShapeDtypeStruct((2, LB, NF * ROWS), BF16),
        ),
        in_specs=[vmem_spec()] * 9,
        out_specs=(hbm_spec(),) * 5,
        scratch_shapes=[
            pltpu.VMEM((share, PACK), BF16),
            pltpu.VMEM((NF // 2, 2, share, PACK), BF16),
            pltpu.VMEM(rows, BF16),
            pltpu.VMEM((2, LB, NF * ROWS), BF16),
            pltpu.SemaphoreType.DMA((9,)),
            pltpu.SemaphoreType.DMA((9,)),
            pltpu.SemaphoreType.DMA((5,)),
        ],
        compiler_params=params(0),
        name="start_exchange",
    )(w_out, w_query, w_key, w_value, router, misc, tokens, picks, dy)


def sum_pairs(f, w_ref, wg, mine, theirs, send, recv, local, first):
    pair, core = f // 2, lax.rem(f, 2)
    swap = pltpu.make_async_remote_copy(
        src_ref=w_ref.at[:, 1 - core],
        dst_ref=theirs,
        send_sem=send.at[first],
        recv_sem=recv.at[first],
        device_id={"fsdp": 2 * pair + 1 - core},
        device_id_type=MESH,
    )
    own = pltpu.make_async_copy(w_ref.at[:, core], mine, local.at[first])
    keep = pltpu.make_async_copy(mine.at[pair], wg.at[pair], local.at[first + 1])
    others = wg.at[pl.ds(0, NF // 2 - 1)]

    def begin():
        swap.start()
        own.start()

    def middle():
        own.wait()
        swap.wait_recv()

        def add(i, carried):
            mine[i] = (mine[i].astype(F32) + theirs[i].astype(F32)).astype(BF16)
            return carried

        lax.fori_loop(0, NF // 2, add, 0)

        def one(k, carried):
            peer = lax.rem(pair + k, NF // 2)
            pltpu.make_async_remote_copy(
                src_ref=mine.at[peer],
                dst_ref=wg.at[pair],
                send_sem=send.at[first + 1],
                recv_sem=recv.at[first + 1],
                device_id={"fsdp": 2 * peer + core},
                device_id_type=MESH,
            ).start()
            return carried

        lax.fori_loop(1, NF // 2, one, 0)
        keep.start()

    def finish():
        keep.wait()
        await_bytes(others, recv.at[first + 1])

    def end():
        swap.wait_send()
        await_bytes(others, send.at[first + 1])

    return begin, middle, finish, end


def last_kernel(
    b_ref, x_ref, a_ref, all_a, all_b, xg, mine, theirs, got, sum_a, sum_b, summed, work,
    send, recv, local,
):
    s, f = place_of()
    right, left, far = around(s)
    half = LB // 2
    first, second = pl.ds(0, half), pl.ds(half, half)
    arrive(greet_fsdp(f) + greet_seq(s))
    begin, middle, finish, end = sum_pairs(f, b_ref, got, mine, theirs, send, recv, local, 0)
    onward = [
        hop(x_ref.at[far, first], summed.at[0], right, send, recv, 2),
        hop(x_ref.at[far, second], summed.at[1], left, send, recv, 3),
    ]
    early = [
        hop(x_ref.at[right, second], xg.at[0, second], right, send, recv, 4),
        hop(x_ref.at[left, first], xg.at[1, first], left, send, recv, 5),
    ]
    late = [
        hop(work.at[0], xg.at[0, first], right, send, recv, 6),
        hop(work.at[1], xg.at[1, second], left, send, recv, 7),
    ]
    for copy in onward:
        copy.start()
    begin()
    for copy in early:
        copy.start()
    own_x = pltpu.make_async_copy(x_ref.at[s], xg.at[2], local.at[2])
    own_x.start()
    middle()
    for n, block, rows in ((0, right, first), (1, left, second)):
        onward[n].wait_recv()
        work[n] = (x_ref[block, rows].astype(F32) + summed[n].astype(F32)).astype(BF16)
        late[n].start()

    def total(blocks):
        value = blocks[0].astype(F32)
        for i in range(1, NF // 2):
            value = value + blocks[i].astype(F32)
        return value

    sum_a[...] = total(a_ref)
    send_seq(s, lambda peer: sum_a, all_a.at[s], send.at[8], recv.at[8])
    own_a = pltpu.make_async_copy(sum_a, all_a.at[s], local.at[3])
    own_a.start()
    finish()
    sum_b[...] = total(got)
    send_seq(s, lambda peer: sum_b, all_b.at[s], send.at[9], recv.at[9])
    own_b = pltpu.make_async_copy(sum_b, all_b.at[s], local.at[4])
    own_b.start()
    own_x.wait()
    own_a.wait()
    own_b.wait()
    for n, out in ((8, all_a), (9, all_b)):
        others = out.at[pl.ds(0, NS - 1)]
        await_bytes(others, recv.at[n])
        await_bytes(others, send.at[n])
    for copy in early + late:
        copy.wait_recv()
    for copy in onward + early + late:
        copy.wait_send()
    end()


def last_exchange(b, x, a, collective_id):
    half = (b.shape[0],) + b.shape[2:]
    return pl.pallas_call(
        last_kernel,
        out_shape=(
            jax.ShapeDtypeStruct((NS,) + a.shape[1:], F32),
            jax.ShapeDtypeStruct((NS,) + b.shape[2:], F32),
            jax.ShapeDtypeStruct((3,) + x.shape[1:], x.dtype),
        ),
        in_specs=[vmem_spec()] * 3,
        out_specs=(any_spec(), any_spec(), any_spec()),
        scratch_shapes=[
            pltpu.VMEM(half, BF16),
            pltpu.VMEM(half, BF16),
            pltpu.VMEM(half, BF16),
            pltpu.VMEM(a.shape[1:], F32),
            pltpu.VMEM(b.shape[2:], F32),
            pltpu.VMEM((2, LB // 2, D), BF16),
            pltpu.VMEM((2, LB // 2, D), BF16),
            pltpu.SemaphoreType.DMA((10,)),
            pltpu.SemaphoreType.DMA((10,)),
            pltpu.SemaphoreType.DMA((5,)),
        ],
        compiler_params=params(collective_id),
        name="last_exchange",
    )(b, x, a)


def bias_tiles(base_ref, tiles, head):
    for d in range(NS):
        wide = jnp.broadcast_to(base_ref[head, d : d + 1, :], (LB, SPAN))
        tiles[d] = pltpu.roll(wide, 0, 1, stride=1, stride_axis=0)[:, :LB]


def score_tiles(qkv_ref, tiles, head, block):
    rows, cols = slice(block * LB, (block + 1) * LB), head * HD
    query = qkv_ref[rows, cols : cols + HD]
    parts = []
    for kb in range(block + 1):
        keys = qkv_ref[kb * LB : (kb + 1) * LB, HW + cols : HW + cols + HD]
        parts.append(dot(query, keys, ((1,), (1,))) * (HD**-0.5) + tiles[block - kb])
    return parts


def front_kernel(
    full_in, all_in, x_in, slots_in, hots_in, dy_ref,
    qkv_out, base_out, lse_out, mixed_out, x1_out, xn2_out, rows_out, gains_out, dy_near,
    full_ref, all_ref, x_ref, slots_ref, hots_ref,
    qkv_ref, base_ref, lse_ref, mixed, x1_ref, xn2_ref, rows_ref, gains_ref,
    o, tiles, send, recv, local, stage,
):
    s, f = place_of()
    right, left, _ = around(s)
    loads = [
        pltpu.make_async_copy(source, target, stage.at[n])
        for n, (source, target) in enumerate(
            (
                (full_in, full_ref),
                (slots_in, slots_ref),
                (all_in, all_ref),
                (x_in, x_ref),
                (hots_in, hots_ref),
            )
        )
    ]
    stores = [
        pltpu.make_async_copy(source, target, stage.at[5 + n])
        for n, (source, target) in enumerate(
            (
                (gains_ref, gains_out),
                (base_ref, base_out),
                (qkv_ref, qkv_out),
                (lse_ref, lse_out),
                (mixed, mixed_out),
                (x1_ref, x1_out),
                (xn2_ref, xn2_out),
                (rows_ref, rows_out),
            )
        )
    ]
    for load in loads:
        load.start()
    arrive(greet_seq(s))
    half = dy_ref.at[pl.ds(NF // 2, NF // 2)]
    beside = [hop(half, dy_near.at[n], to, send, recv, n) for n, to in enumerate((right, left))]
    for copy in beside:
        copy.start()
    for load in loads[:2]:
        load.wait()
    misc = full_ref[:, MISC:].astype(F32)
    turned = jnp.transpose(misc)
    gains_ref[...] = turned[E : E + 8]
    stores[0].start()
    gain_one, gain_two = turned[E : E + 1], turned[E + 1 : E + 2]
    table = misc.reshape(NB, D // NF, 128)[:, 0, :].astype(BF16)
    slots = slots_ref[...]
    hot = (slots == lax.broadcasted_iota(jnp.int32, (NB, NS * SPAN), 0)).astype(BF16)
    base = dot(table, hot, ((0,), (0,)))[E : E + 8]
    base = jnp.where(slots < 0, -1e30, base)
    for head in range(HL):
        for d in range(NS):
            line = base[2 + head : 3 + head, d * SPAN : (d + 1) * SPAN]
            base_ref[head, d : d + 1, :] = line
        bias_tiles(base_ref, tiles.at[head], head)
    stores[1].start()
    loads[2].wait()
    for block in range(NS):
        x = all_ref[block].astype(F32)
        xn1 = (x * row_factor(x) * gain_one).astype(BF16)
        rows = slice(block * LB, (block + 1) * LB)
        qkv_ref[rows, :] = dot(xn1, full_ref[:, D : D + 3 * HW]).astype(BF16)
    stores[2].start()
    for block in range(NS):
        rows = slice(block * LB, (block + 1) * LB)
        for head in range(HL):
            cols = slice(head * HD, (head + 1) * HD)
            parts = score_tiles(qkv_ref, tiles.at[head], head, block)
            top = parts[0].max(axis=1, keepdims=True)
            for part in parts[1:]:
                top = jnp.maximum(top, part.max(axis=1, keepdims=True))
            parts = [jnp.exp(part - top) for part in parts]
            total = parts[0].sum(axis=1, keepdims=True)
            for part in parts[1:]:
                total = total + part.sum(axis=1, keepdims=True)
            inverse = 1.0 / total
            value = None
            for kb, part in enumerate(parts):
                keys = slice(kb * LB, (kb + 1) * LB)
                values = qkv_ref[keys, 2 * HW + head * HD : 2 * HW + (head + 1) * HD]
                term = dot((part * inverse).astype(BF16), values)
                value = term if value is None else value + term
            o[block, :, cols] = value.astype(BF16)
            lse_ref[rows, head : head + 1] = top + jnp.log(total)

        @pl.when(s != block)
        def _():
            pltpu.make_async_remote_copy(
                src_ref=o.at[block],
                dst_ref=mixed.at[s],
                send_sem=send.at[2],
                recv_sem=recv.at[2],
                device_id={"seq": block},
                device_id_type=MESH,
            ).start()

    own = pltpu.make_async_copy(o.at[s], mixed.at[s], local)
    own.start()
    stores[3].start()
    for load in loads[3:]:
        load.wait()
    own.wait()
    others = mixed.at[pl.ds(0, NS - 1)]
    await_bytes(others, recv.at[2])
    stores[4].start()
    x1 = x_ref[...].astype(F32)
    for i in range(NS):
        x1 = x1 + dot(mixed[i], full_ref[i * HW : (i + 1) * HW, :D])
    x1_ref[...] = x1
    stores[5].start()
    xn2 = (x1 * row_factor(x1) * gain_two).astype(BF16)
    xn2_ref[...] = xn2
    stores[6].start()
    rows = dot(hots_ref[0] + hots_ref[1], xn2, ((0,), (0,)))
    rows_ref[...] = rows.reshape(NF, ROWS, D).astype(BF16)
    stores[7].start()
    await_bytes(others, send.at[2])
    for copy in beside:
        copy.wait_recv()
        copy.wait_send()
    for store in stores:
        store.wait()


def front(full, all_tokens, tokens, slots, hots, dy_own, collective_id):
    inputs = (full, all_tokens, tokens, slots, hots)
    made = [
        ((LEN, 3 * HW), BF16),
        ((HL, NS, SPAN), F32),
        ((LEN, 128), F32),
        ((NS, LB, HW), BF16),
        ((LB, D), F32),
        ((LB, D), BF16),
        ((NF, ROWS, D), BF16),
        ((8, D), F32),
    ]
    return pl.pallas_call(
        front_kernel,
        out_shape=tuple(jax.ShapeDtypeStruct(*m) for m in made)
        + (jax.ShapeDtypeStruct((2, NF // 2) + dy_own.shape[1:], BF16),),
        in_specs=[hbm_spec()] * 6,
        out_specs=(hbm_spec(),) * 9,
        scratch_shapes=[pltpu.VMEM(i.shape, i.dtype) for i in inputs]
        + [pltpu.VMEM(*m) for m in made]
        + [
            pltpu.VMEM((NS, LB, HW), BF16),
            pltpu.VMEM((HL, NS, LB, LB), F32),
            pltpu.SemaphoreType.DMA((3,)),
            pltpu.SemaphoreType.DMA((3,)),
            pltpu.SemaphoreType.DMA,
            pltpu.SemaphoreType.DMA((13,)),
        ],
        compiler_params=params(collective_id),
        name="front",
    )(full, all_tokens, tokens, slots, hots, dy_own)


def flip_rows(values):
    down = lax.broadcasted_iota(jnp.int32, (LB, LB), 0)
    across = lax.broadcasted_iota(jnp.int32, (LB, LB), 1)
    swap = (down + across == LB - 1).astype(BF16)
    high = values.astype(BF16)
    low = (values - high.astype(F32)).astype(BF16)
    return dot(swap, high) + dot(swap, low)


def backward_kernel(
    qkv_ref, do_ref, lse_ref, base_ref, pack_ref, g_ref, diag_ref, sums,
    do, tiles, folds, dk, dv, mine, theirs, send, recv, local,
):
    s, f = place_of()
    arrive(greet_fsdp(f) + greet_seq(s))
    begin, middle, finish, end = sum_pairs(
        f, pack_ref, sums, mine, theirs, send, recv, local, 0
    )
    send_seq(s, lambda peer: do_ref.at[peer], do.at[s], send.at[2], recv.at[2])
    own = pltpu.make_async_copy(do_ref.at[s], do.at[s], local.at[2])
    own.start()
    begin()
    middle()
    own.wait()
    others = do.at[pl.ds(0, NS - 1)]
    await_bytes(others, recv.at[2])
    scale = HD**-0.5
    for head in range(HL):
        cols = slice(head * HD, (head + 1) * HD)
        values = slice(2 * HW + head * HD, 2 * HW + (head + 1) * HD)
        bias_tiles(base_ref, tiles, head)
        for block in range(NS):
            rows = slice(block * LB, (block + 1) * LB)
            query, grad = qkv_ref[rows, cols], do[block, :, cols]
            lse = lse_ref[rows, head : head + 1]
            parts = score_tiles(qkv_ref, tiles, head, block)
            probs = [jnp.exp(part - lse) for part in parts]
            grads = [
                dot(grad, qkv_ref[kb * LB : (kb + 1) * LB, values], ((1,), (1,)))
                for kb in range(block + 1)
            ]
            delta = None
            for prob, part in zip(probs, grads):
                term = (prob * part).sum(axis=1, keepdims=True)
                delta = term if delta is None else delta + term
            grad_query = None
            for kb in range(block + 1):
                keys = slice(kb * LB, (kb + 1) * LB)
                d = block - kb
                ds = probs[kb] * (grads[kb] - delta)
                if kb == 0:
                    folds[d] = ds
                else:
                    folds[d] += ds
                raw = (ds * scale).astype(BF16)
                term = dot(raw, qkv_ref[keys, HW + head * HD : HW + (head + 1) * HD])
                grad_query = term if grad_query is None else grad_query + term
                to_key = dot(raw, query, ((0,), (0,)))
                to_value = dot(probs[kb].astype(BF16), grad, ((0,), (0,)))
                if d == 0:
                    dk[keys, :] = to_key
                    dv[keys, :] = to_value
                else:
                    dk[keys, :] += to_key
                    dv[keys, :] += to_value
            g_ref[rows, cols] = grad_query.astype(BF16)
        g_ref[:, HW + head * HD : HW + (head + 1) * HD] = dk[...].astype(BF16)
        g_ref[:, 2 * HW + head * HD : 2 * HW + (head + 1) * HD] = dv[...].astype(BF16)
        for d in range(NS):
            wide = jnp.concatenate(
                [flip_rows(folds[d]), jnp.zeros((LB, SPAN - LB), F32)], axis=1
            )
            turned = pltpu.roll(wide, LB + 1, 1, stride=1, stride_axis=0)
            diag_ref[head, d : d + 1, :] = turned.sum(axis=0, keepdims=True)
    await_bytes(others, send.at[2])
    finish()
    end()


def attend_backward(qkv, do, lse, base, pack, collective_id):
    half = (pack.shape[0],) + pack.shape[2:]
    return pl.pallas_call(
        backward_kernel,
        out_shape=(
            jax.ShapeDtypeStruct((LEN, 3 * HW), BF16),
            jax.ShapeDtypeStruct((HL, NS, SPAN), F32),
            jax.ShapeDtypeStruct(half, BF16),
        ),
        in_specs=[vmem_spec()] * 5,
        out_specs=(vmem_spec(), vmem_spec(), any_spec()),
        scratch_shapes=[
            pltpu.VMEM((NS, LB, HW), BF16),
            pltpu.VMEM((NS, LB, LB), F32),
            pltpu.VMEM((NS, LB, LB), F32),
            pltpu.VMEM((LEN, HD), F32),
            pltpu.VMEM((LEN, HD), F32),
            pltpu.VMEM(half, BF16),
            pltpu.VMEM(half, BF16),
            pltpu.SemaphoreType.DMA((3,)),
            pltpu.SemaphoreType.DMA((3,)),
            pltpu.SemaphoreType.DMA((3,)),
        ],
        compiler_params=params(collective_id),
        name="attend_backward",
    )(qkv, do, lse, base, pack)


def split_rows(rows):
    width = rows.shape[-1]
    half = NF // 2
    mixed = rows[:, 16:24]
    left, right = mixed[:half], mixed[half:]
    low = lax.broadcasted_iota(jnp.int32, left.shape, 1) < 4
    one = jnp.where(low, left, pltpu.roll(right, 4, 1)).reshape(half * 8, width)
    two = jnp.where(low, pltpu.roll(left, 4, 1), right).reshape(half * 8, width)
    return (
        jnp.concatenate([rows[:, 0:8].reshape(NF * 8, width), one], axis=0),
        jnp.concatenate([rows[:, 8:16].reshape(NF * 8, width), two], axis=0),
    )


def join_rows(first, second):
    width = first.shape[-1]
    half = NF // 2
    one = first[NF * 8 :].reshape(half, 8, width)
    two = second[NF * 8 :].reshape(half, 8, width)
    low = lax.broadcasted_iota(jnp.int32, one.shape, 1) < 4
    left = jnp.where(low, one, pltpu.roll(two, 4, 1))
    right = jnp.where(low, pltpu.roll(one, 4, 1), two)
    return jnp.concatenate(
        [
            first[: NF * 8].reshape(NF, 8, width),
            second[: NF * 8].reshape(NF, 8, width),
            jnp.concatenate([left, right], axis=0),
        ],
        axis=1,
    )


def expert_rows(x, dy, ids, own, router, w_in, w_out):
    logits = dot(x, router)
    lane = lax.broadcasted_iota(jnp.int32, logits.shape, 1)
    one = jnp.sum(jnp.where(lane == own, logits, 0.0), axis=1, keepdims=True)
    two = jnp.sum(jnp.where(lane == ids, logits, 0.0), axis=1, keepdims=True)
    top = jnp.maximum(one, two)
    one, two = jnp.exp(one - top), jnp.exp(two - top)
    gate = one / (one + two)
    grad = (dy * gate).astype(BF16)
    u = dot(x, w_in)
    square = u * u
    tanh = jnp.tanh(u * (0.7978845608028654 + (0.7978845608028654 * 0.044715) * square))
    half = 0.5 * (1.0 + tanh)
    hid = (u * half).astype(BF16)
    slope = half + (0.5 * u) * (1.0 - tanh * tanh) * (
        0.7978845608028654 + (3.0 * 0.7978845608028654 * 0.044715) * square
    )
    y = dot(hid, w_out)
    du = (dot(grad, w_out, ((1,), (1,))) * slope).astype(BF16)
    dx = dot(du, w_in, ((1,), (1,)))
    return y, dx, hid, grad, du


def expert_kernel(
    x_ref, dy_own, near_a, near_b, full_ref, wi_in, wo_in,
    y_out, dx_out, gi_out, go_out, dy_far,
    router_ref, wi_ref, wo_ref, gi_ref, go_ref,
    x, dy, part, near, summed, kept, send, recv, local,
):
    s, f = place_of()
    right, left, far = around(s)
    half = NF // 2
    first, second = pl.ds(0, half), pl.ds(half, half)
    columns = [pl.ds(0, D // 2), pl.ds(D // 2, D // 2)]
    loads = [
        pltpu.make_async_copy(source, target, local.at[7 + n])
        for n, (source, target) in enumerate(
            ((wi_in, wi_ref), (wo_in, wo_ref), (full_ref.at[:, pl.ds(MISC, 128)], router_ref))
        )
    ]
    stores = [
        pltpu.make_async_copy(gi_ref, gi_out, local.at[10]),
        pltpu.make_async_copy(go_ref, go_out, local.at[11]),
    ]
    for load in loads:
        load.start()
    arrive(greet_fsdp(f) + greet_seq(s))

    def step_to(source, target, to, n):
        return hop(source, target, to, send, recv, n)

    for c in range(2):
        send_fsdp(
            f,
            lambda peer: x_ref.at[peer, :, columns[c]],
            x.at[s, f, :, columns[c]],
            send.at[c],
            recv.at[c],
        )
    dy_relay = [
        step_to(near_a.at[0], dy_far.at[first], right, 2),
        step_to(near_b.at[1], dy_far.at[second], left, 3),
    ]
    for copy in dy_relay:
        copy.start()
    own_x = pltpu.make_async_copy(x_ref.at[f], x.at[s, f], local.at[0])
    own_x.start()
    gi_ref[...] = jnp.zeros_like(gi_ref)
    go_ref[...] = jnp.zeros_like(go_ref)
    begin, early, onward, late = [], [], [], []
    for c in range(2):
        block = x.at[s, :, :, columns[c]]
        begin.append([step_to(block, block, to, 4 + 2 * c + n) for n, to in enumerate((right, left))])
    relay = [
        step_to(x.at[left, first], x.at[left, first], right, 8),
        step_to(x.at[right, second], x.at[right, second], left, 9),
    ]
    for a in range(2):
        early.append(
            [
                step_to(part.at[a, right, second], near.at[a, 0, second], right, 10 + 2 * a),
                step_to(part.at[a, left, first], near.at[a, 1, first], left, 11 + 2 * a),
            ]
        )
        onward.append(
            [
                step_to(part.at[a, far, first], summed.at[a, 0], right, 14 + 2 * a),
                step_to(part.at[a, far, second], summed.at[a, 1], left, 15 + 2 * a),
            ]
        )
        late.append(
            [
                [
                    step_to(
                        part.at[a, right, first, :, columns[c]],
                        near.at[a, 0, first, :, columns[c]],
                        right,
                        18 + 4 * a + 2 * c,
                    ),
                    step_to(
                        part.at[a, left, second, :, columns[c]],
                        near.at[a, 1, second, :, columns[c]],
                        left,
                        19 + 4 * a + 2 * c,
                    ),
                ]
                for c in range(2)
            ]
        )
    for load in loads:
        load.wait()
    own_x.wait()
    others_x = [x.at[s, pl.ds(0, NF - 1), :, columns[c]] for c in range(2)]
    for c in range(2):
        await_bytes(others_x[c], recv.at[c])
        for copy in begin[c]:
            copy.start()

    def step(k, carried):
        chunk = lax.rem(s + jnp.where(k == 1, 3, jnp.where(k == 0, 0, k - 1)), NS)

        @pl.when(k == 3)
        def _():
            for copy in dy_relay + relay:
                copy.wait_recv()

        for n, (low, high) in enumerate(
            (
                (dy_own.at[first], dy_own.at[second]),
                (near_a.at[0], near_b.at[0]),
                (near_a.at[1], near_b.at[1]),
                (dy_far.at[first], dy_far.at[second]),
            )
        ):

            @pl.when(k == n)
            def _():
                loads = [
                    pltpu.make_async_copy(low, dy.at[first], local.at[1]),
                    pltpu.make_async_copy(high, dy.at[second], local.at[2]),
                ]
                for load in loads:
                    load.start()
                for load in loads:
                    load.wait()

        @pl.when(k == 1)
        def _():
            for n in range(2):
                for c in range(2):
                    begin[c][n].wait_recv()
                relay[n].start()

        xs = split_rows(x[chunk].astype(F32))
        dys = split_rows(dy[...].astype(F32))
        ys, dxs = [], []
        for j in range(2):
            rows = xs[j].astype(BF16)
            ids = dys[j][:, D:].astype(jnp.int32)
            y, dx, hid, grad, du = expert_rows(
                rows, dys[j][:, :D], ids, 2 * f + j, router_ref[...], wi_ref[j], wo_ref[j]
            )
            ys.append(y)
            dxs.append(dx)
            slot = jnp.where(k == 0, 0, k - 1)
            for n, value in enumerate((rows, hid, grad, du)):
                kept[slot, n, j] = value
        part[0, chunk] = join_rows(*ys).astype(BF16)
        part[1, chunk] = join_rows(*dxs).astype(BF16)

        @pl.when(k == 1)
        def _():
            for a in range(2):
                early[a][1].start()

        @pl.when(k == 2)
        def _():
            early[0][0].start()

        @pl.when(k == 3)
        def _():
            for a in range(2):
                for n in range(2):
                    onward[a][n].start()

        @pl.when(k == 0)
        def _():
            weights(0, 0)

        return carried

    def weights(slot, carried):
        for j in range(2):
            go_ref[j] += dot(kept[slot, 1, j], kept[slot, 2, j], ((0,), (0,)))
            gi_ref[j] += dot(kept[slot, 0, j], kept[slot, 3, j], ((0,), (0,)))
        return carried

    lax.fori_loop(0, NS, step, 0)
    lax.fori_loop(0, NS - 1, weights, 0)
    for store in stores:
        store.start()

    def add(a, block, offset, cols, other):
        def one(i, carried):
            rows = pl.ds(offset + 8 * i, 8)
            total = part[a, block, rows, :, cols].astype(F32) + other(pl.ds(8 * i, 8))
            part[a, block, rows, :, cols] = total.astype(BF16)
            return carried

        return one

    for a in range(2):
        for n in range(2):
            onward[a][n].wait_recv()
        for c in range(2):
            for n, block, offset in ((0, right, 0), (1, left, half)):
                lax.fori_loop(
                    0,
                    half // 8,
                    add(
                        a,
                        block,
                        offset,
                        columns[c],
                        lambda i: summed[a, n, i, :, columns[c]].astype(F32),
                    ),
                    0,
                )
                late[a][c][n].start()
        if a == 0:
            early[1][0].start()
    outs = (y_out, dx_out)
    pieces = []
    for a in range(2):
        for n in range(2):
            early[a][n].wait_recv()
        for c in range(2):
            cols = columns[c]
            for n in range(2):
                late[a][c][n].wait_recv()
            lax.fori_loop(
                0,
                NF // 8,
                add(
                    a,
                    s,
                    0,
                    cols,
                    lambda i: near[a, 0, i, :, cols].astype(F32)
                    + near[a, 1, i, :, cols].astype(F32),
                ),
                0,
            )
            p = 2 * a + c
            send_fsdp(
                f,
                lambda peer: part.at[a, s, peer, :, cols],
                outs[a].at[f, :, cols],
                send.at[26 + p],
                recv.at[26 + p],
            )
            keep = pltpu.make_async_copy(
                part.at[a, s, f, :, cols], outs[a].at[f, :, cols], local.at[3 + p]
            )
            keep.start()
            pieces.append((keep, outs[a].at[pl.ds(0, NF - 1), :, cols], 26 + p))
    for keep, others, n in pieces:
        keep.wait()
        await_bytes(others, recv.at[n])
        await_bytes(others, send.at[n])
    for a in range(2):
        for copy in early[a] + onward[a] + late[a][0] + late[a][1]:
            copy.wait_send()
    for copy in begin[0] + begin[1] + relay + dy_relay:
        copy.wait_send()
    for c in range(2):
        await_bytes(others_x[c], send.at[c])
    for store in stores:
        store.wait()


def run_experts(x, dy, near_a, near_b, full, w_in, w_out, collective_id):
    rows = (NF, ROWS, D)
    return pl.pallas_call(
        expert_kernel,
        out_shape=(
            jax.ShapeDtypeStruct(rows, BF16),
            jax.ShapeDtypeStruct(rows, BF16),
            jax.ShapeDtypeStruct((2, D, D), F32),
            jax.ShapeDtypeStruct((2, D, D), F32),
            jax.ShapeDtypeStruct((NF, ROWS, MSG), BF16),
        ),
        in_specs=[any_spec()] * 7,
        out_specs=(any_spec(),) * 5,
        scratch_shapes=[
            pltpu.VMEM((D, 128), BF16),
            pltpu.VMEM((2, D, D), BF16),
            pltpu.VMEM((2, D, D), BF16),
            pltpu.VMEM((2, D, D), F32),
            pltpu.VMEM((2, D, D), F32),
            pltpu.VMEM((NS,) + rows, BF16),
            pltpu.VMEM((NF, ROWS, MSG), BF16),
            pltpu.VMEM((2, NS) + rows, BF16),
            pltpu.VMEM((2, 2) + rows, BF16),
            pltpu.VMEM((2, 2, NF // 2, ROWS, D), BF16),
            pltpu.VMEM((NS - 1, 4, 2, NF * CAP, D), BF16),
            pltpu.SemaphoreType.DMA((30,)),
            pltpu.SemaphoreType.DMA((30,)),
            pltpu.SemaphoreType.DMA((12,)),
        ],
        compiler_params=params(collective_id),
        name="run_experts",
    )(x, dy, near_a, near_b, full, w_in, w_out)


def token_kernel(
    y_in, dx_in, hot_in, x1_in, xn2_in, dy_in, picks_ref, gain_in, full_in, mixed_in,
    out_ref, dx1_ref, do_ref, pack_ref,
    xn2_ref, x1_ref, full_ref, dy_ref, hot_ref, y_ref, dx_ref, gain_ref, mixed_ref, stage,
):
    loads = [
        pltpu.make_async_copy(source, target, stage.at[n])
        for n, (source, target) in enumerate(
            (
                (xn2_in, xn2_ref),
                (x1_in, x1_ref),
                (full_in, full_ref),
                (dy_in, dy_ref),
                (hot_in, hot_ref),
                (y_in, y_ref),
                (dx_in, dx_ref),
                (gain_in, gain_ref),
                (mixed_in, mixed_ref),
            )
        )
    ]
    for load in loads:
        load.start()
    for load in loads[:6]:
        load.wait()
    xn2, x1, router = xn2_ref[...], x1_ref[...], full_ref[:, MISC:]
    dy = dy_ref[...].astype(F32)
    logits = dot(xn2, router)
    lane = lax.broadcasted_iota(jnp.int32, logits.shape, 1)
    named = [lane == picks_ref[:, c : c + 1] for c in range(2)]
    chosen = [jnp.sum(jnp.where(n, logits, 0.0), axis=1, keepdims=True) for n in named]
    top = jnp.maximum(chosen[0], chosen[1])
    chosen = [jnp.exp(value - top) for value in chosen]
    both = chosen[0] + chosen[1]
    gates = [value / both for value in chosen]
    ys = [dot(hot_ref[c], y_ref[...]) for c in range(2)]
    out_ref[...] = (x1 + (gates[0] * ys[0] + gates[1] * ys[1])).astype(BF16)
    dgates = [jnp.sum(dy * y, axis=1, keepdims=True) for y in ys]
    mean = gates[0] * dgates[0] + gates[1] * dgates[1]
    dpicks = [gates[c] * (dgates[c] - mean) for c in range(2)]
    dlogits = sum(jnp.where(named[c], dpicks[c], 0.0) for c in range(2)).astype(BF16)
    for load in loads[6:]:
        load.wait()
    dxn2 = dot(hot_ref[0] + hot_ref[1], dx_ref[...])
    dxn2 = dxn2 + dot(dlogits, router, ((1,), (1,)))
    r2 = row_factor(x1)
    terms = (dxn2 * x1 * r2).astype(BF16)
    grad_gain = dot(terms, jnp.ones((LB, 128), BF16), ((0,), (0,)))
    grad_router = dot(xn2, dlogits, ((0,), (0,)))
    lane = lax.broadcasted_iota(jnp.int32, grad_gain.shape, 1)
    pack_ref[:, D:] = jnp.where(lane == E, grad_gain, grad_router).astype(BF16)
    scaled = dxn2 * gain_ref[1:2]
    mean = jnp.mean(scaled * x1, axis=1, keepdims=True)
    dx1 = dy + r2 * scaled - x1 * (r2 * r2 * r2) * mean
    dx1_ref[...] = dx1
    dat = dx1.astype(BF16)
    for i in range(NS):
        rows = slice(i * HW, (i + 1) * HW)
        do_ref[i] = dot(dat, full_ref[rows, :D], ((1,), (1,))).astype(BF16)
        pack_ref[rows, :D] = dot(mixed_ref[i], dat, ((0,), (0,))).astype(BF16)


def token_side(y, dx, hot, x1, xn2, dy, picks, gains, full, mixed):
    staged = (xn2, x1, full, dy, hot, y, dx, gains, mixed)
    return pl.pallas_call(
        token_kernel,
        out_shape=(
            jax.ShapeDtypeStruct((LB, D), BF16),
            jax.ShapeDtypeStruct((LB, D), F32),
            jax.ShapeDtypeStruct((NS, LB, HW), BF16),
            jax.ShapeDtypeStruct((D, D + 128), BF16),
        ),
        in_specs=[hbm_spec()] * 6 + [vmem_spec()] + [hbm_spec()] * 3,
        out_specs=(vmem_spec(),) * 4,
        scratch_shapes=[pltpu.VMEM(i.shape, i.dtype) for i in staged]
        + [pltpu.SemaphoreType.DMA((9,))],
        compiler_params=params(),
        name="token_side",
    )(y, dx, hot, x1, xn2, dy, picks, gains, full, mixed)


def project_kernel(
    g_ref, x_ref, gain_ref, full_ref, slots_ref, diag_ref, gi_ref, go_ref,
    part_ref, pack_ref, gi_out, go_out, weight, held, local,
):
    loads = [
        pltpu.make_async_copy(gi_ref, held.at[0], local.at[0]),
        pltpu.make_async_copy(go_ref, held.at[1], local.at[1]),
    ]
    stores = [
        pltpu.make_async_copy(held.at[0], gi_out, local.at[2]),
        pltpu.make_async_copy(held.at[1], go_out, local.at[3]),
    ]
    for copy in loads:
        copy.start()
    weight[...] = jnp.zeros_like(weight)
    misc = jnp.zeros((D, 64), F32)
    for block in range(NS):
        rows = slice(block * LB, (block + 1) * LB)
        x = x_ref[block].astype(F32)
        r1 = row_factor(x)
        xn1 = (x * r1 * gain_ref[0:1]).astype(BF16)
        g = g_ref[rows, :]
        weight[...] += dot(xn1, g, ((0,), (0,)))
        part = dot(g, full_ref[:, D : D + 3 * HW], ((1,), (1,)))
        part_ref[block] = part.astype(BF16)
        terms = (part * x * r1).astype(BF16)
        misc = misc + dot(terms, jnp.ones((LB, 64), BF16), ((0,), (0,)))
        if block < 2:
            loads[block].wait()
            stores[block].start()
    lane = lax.broadcasted_iota(jnp.int32, misc.shape, 1)
    row = lax.broadcasted_iota(jnp.int32, (NB, NS * SPAN), 0)
    hot = (slots_ref[...] == row).astype(BF16)
    diag = jnp.concatenate(
        [jnp.zeros((8, NS * SPAN), F32), diag_ref[...], jnp.zeros((56 - HL, NS * SPAN), F32)],
        axis=0,
    )
    high = diag.astype(BF16)
    low = (diag - high.astype(F32)).astype(BF16)
    table = dot(hot, high, ((1,), (1,))) + dot(hot, low, ((1,), (1,)))
    table = jnp.broadcast_to(table[:, None, :], (NB, D // NF, 64)).reshape(D, 64)
    misc = jnp.where(lane == 0, misc, table)
    pack_ref[:, : 3 * HW] = weight[...].astype(BF16)
    pack_ref[:, 3 * HW :] = misc.astype(BF16)
    for copy in stores:
        copy.wait()


def project_back(g, x, gains, full, slots, diag, gi, go):
    return pl.pallas_call(
        project_kernel,
        out_shape=(
            jax.ShapeDtypeStruct((NS, LB, D), BF16),
            jax.ShapeDtypeStruct((D, 3 * HW + 64), BF16),
            jax.ShapeDtypeStruct(gi.shape, F32),
            jax.ShapeDtypeStruct(go.shape, F32),
        ),
        in_specs=[vmem_spec()] * 6 + [any_spec()] * 2,
        out_specs=(vmem_spec(), vmem_spec(), any_spec(), any_spec()),
        scratch_shapes=[
            pltpu.VMEM((D, 3 * HW), F32),
            pltpu.VMEM((2,) + gi.shape, F32),
            pltpu.SemaphoreType.DMA((4,)),
        ],
        compiler_params=params(),
        name="project_back",
    )(g, x, gains, full, slots, diag, gi, go)


def finish_kernel(
    a_ref, b_ref, part_ref, x_ref, dx1_ref, gain_ref,
    gx_ref, g1_ref, g2_ref, wq_ref, wk_ref, wv_ref, wo_ref, router_ref, table_ref,
):
    total = a_ref[0] + a_ref[1] + a_ref[2] + a_ref[3]
    wo_ref[...] = total[:, :D]
    router_ref[...] = total[:, D : D + E]
    g2_ref[...] = jnp.transpose(total[:, D:])[E : E + 1]
    misc = [b_ref[n, :, 3 * HW :] for n in range(NS)]
    gain = misc[0] + misc[1] + misc[2] + misc[3]
    g1_ref[...] = jnp.transpose(jnp.concatenate([gain, gain], axis=1))[0:1]
    table_ref[...] = jnp.concatenate([m[0:1, 8 : 8 + HL] for m in misc], axis=1)
    for i, out in enumerate((wq_ref, wk_ref, wv_ref)):
        out[...] = jnp.concatenate(
            [b_ref[n, :, i * HW : (i + 1) * HW] for n in range(NS)], axis=1
        )
    x = x_ref[...].astype(F32)
    r1 = row_factor(x)
    dxn1 = part_ref[0].astype(F32) + part_ref[1].astype(F32) + part_ref[2].astype(F32)
    scaled = dxn1 * gain_ref[0:1]
    mean = jnp.mean(scaled * x, axis=1, keepdims=True)
    gx_ref[...] = dx1_ref[...] + r1 * scaled - x * (r1 * r1 * r1) * mean


def finish(a, b, part, x, dx1, gain):
    share = D // NF
    return pl.pallas_call(
        finish_kernel,
        out_shape=(
            jax.ShapeDtypeStruct((LB, D), F32),
            jax.ShapeDtypeStruct((1, share), F32),
            jax.ShapeDtypeStruct((1, share), F32),
            jax.ShapeDtypeStruct((share, D), F32),
            jax.ShapeDtypeStruct((share, D), F32),
            jax.ShapeDtypeStruct((share, D), F32),
            jax.ShapeDtypeStruct((share, D), F32),
            jax.ShapeDtypeStruct((share, E), F32),
            jax.ShapeDtypeStruct((1, H), F32),
        ),
        in_specs=[vmem_spec()] * 6,
        out_specs=(vmem_spec(),) * 9,
        compiler_params=params(),
        name="finish",
    )(a, b, part, x, dx1, gain)


def distance_base(values, near, far):
    long = jnp.concatenate(
        [jnp.full((LB,), near, values.dtype), values, jnp.full((1,), far, values.dtype)]
    )
    rows = []
    for d in range(NS):
        rows.append(long[d * LB + 1 : d * LB + LB + 1][::-1])
        rows.append(long[LB + d * LB + 1 : LB + d * LB + LB + 1][::-1])
    return jnp.concatenate(rows)


def shards(
    tokens,
    gain_attn,
    gain_ffn,
    w_query,
    w_key,
    w_value,
    w_out,
    router,
    bias_table,
    expert_in,
    expert_out,
    choices,
    buckets,
    cotangent,
):
    s = lax.axis_index("seq")
    share = D // NF
    own_tokens = tokens.reshape(LB, D)

    misc = jnp.concatenate(
        [
            gain_attn[:, None],
            gain_ffn[:, None],
            jnp.pad(
                lax.dynamic_slice_in_dim(bias_table, s * HL, HL, 1), ((0, share - 1), (0, 0))
            ),
            jnp.zeros((share, 64 - 2 - HL), BF16),
        ],
        axis=1,
    )
    picks = choices.reshape(LB, 2)
    dy_bf = cotangent.reshape(LB, D)
    gathered, all_tokens, dy_own, near_a, hots = start_exchange(
        w_out, w_query, w_key, w_value, router, misc, own_tokens, picks, dy_bf
    )
    full = gathered.reshape(D, PACK)
    slots = distance_base(buckets, -1, -1).reshape(1, NS * SPAN)
    qkv, base, lse, mixed, x1, xn2, x_rows, gains, near_b = front(
        full, all_tokens, own_tokens, slots, hots, dy_own, 1
    )
    y_back, dx_back, grad_in, grad_out, _ = run_experts(
        x_rows, dy_own, near_a, near_b, full, expert_in, expert_out, 2
    )
    layer_out, dx1, do, pack_a = token_side(
        y_back.reshape(NF * ROWS, D),
        dx_back.reshape(NF * ROWS, D),
        hots,
        x1,
        xn2,
        dy_bf,
        picks,
        gains,
        full,
        mixed,
    )
    dqkv, diag, shares_a = attend_backward(
        qkv, do, lse, base, pack_a.reshape(NF // 2, 2, share, D + 128), 3
    )
    part, pack_b, grad_in, grad_out = project_back(
        dqkv, all_tokens, gains, full, slots, diag.reshape(HL, NS * SPAN), grad_in, grad_out
    )
    all_a, all_b, part_back = last_exchange(
        pack_b.reshape(NF // 2, 2, share, 3 * HW + 64), part, shares_a, 4
    )
    grad_x, grad_one, grad_two, grad_q, grad_k, grad_v, grad_o, grad_router, grad_table = finish(
        all_a, all_b, part_back, own_tokens, dx1, gains
    )
    return (
        layer_out.reshape(1, LB, D),
        grad_x.reshape(1, LB, D),
        grad_one.reshape(share),
        grad_two.reshape(share),
        grad_q,
        grad_k,
        grad_v,
        grad_o,
        grad_router,
        grad_table,
        grad_in,
        grad_out,
    )


def solution(mesh):
    placed = (
        P("fsdp", "seq", None),
        P("fsdp"),
        P("fsdp"),
        P("fsdp", None),
        P("fsdp", None),
        P("fsdp", None),
        P("fsdp", None),
        P("fsdp", None),
        P("fsdp", None),
        P("fsdp", None, "seq"),
        P("fsdp", "seq", None),
        P("fsdp", "seq", None),
        P(),
        P("fsdp", "seq", None),
    )
    return jax.shard_map(
        shards,
        mesh=mesh,
        in_specs=placed,
        out_specs=(
            P("fsdp", "seq", None),
            P("fsdp", "seq", None),
            P("fsdp"),
            P("fsdp"),
            P("fsdp", None),
            P("fsdp", None),
            P("fsdp", None),
            P("fsdp", None),
            P("fsdp", None),
            P("fsdp", None),
            P("fsdp", None, "seq"),
            P("fsdp", "seq", None),
        ),
        check_vma=False,
    )
```

```python
from functools import partial

import jax
import jax.numpy as jnp
from jax import lax
from jax.experimental import pallas as pl
from jax.experimental.pallas import tpu as pltpu
from jax.sharding import PartitionSpec as P

D = 768
H = 12
HD = 64
NS = 4
NF = 32
HL = H // NS
HW = HL * HD
LB = 256
LEN = 1024
E = 64
CAP = 12
ROWS = 2 * CAP
MSG = D + 128
PACK = 1536
NB = 32
MISC = PACK - 128
SPAN = 2 * LB

epsilon = 1e-06
MESH = pl.DeviceIdType.MESH
F32 = jnp.float32
BF16 = jnp.bfloat16
MIB = 1024 * 1024


def any_spec():
    return pl.BlockSpec(memory_space=pl.ANY)


def hbm_spec():
    return pl.BlockSpec(memory_space=pltpu.HBM)


def vmem_spec():
    return pl.BlockSpec(memory_space=pltpu.VMEM)


def dot(a, b, dims=((1,), (0,))):
    return lax.dot_general(a, b, (dims, ((), ())), preferred_element_type=F32)


def row_factor(values):
    return lax.rsqrt(jnp.mean(values * values, axis=1, keepdims=True) + epsilon)


def params(collective_id=None, vmem=63):
    if collective_id is None:
        return pltpu.CompilerParams(vmem_limit_bytes=vmem * MIB)
    return pltpu.CompilerParams(
        collective_id=collective_id, has_side_effects=True, vmem_limit_bytes=vmem * MIB
    )


def place_of():
    return lax.axis_index("seq"), lax.axis_index("fsdp")


def greet_seq(s):
    barrier = pltpu.get_barrier_semaphore()
    for k in range(1, NS):
        pl.semaphore_signal(
            barrier, inc=1, device_id={"seq": lax.rem(s + k, NS)}, device_id_type=MESH
        )
    return NS - 1


def greet_fsdp(f):
    barrier = pltpu.get_barrier_semaphore()

    def one(k, carried):
        pl.semaphore_signal(
            barrier, inc=1, device_id={"fsdp": lax.rem(f + k, NF)}, device_id_type=MESH
        )
        return carried

    lax.fori_loop(1, NF, one, 0)
    return NF - 1


def arrive(count):
    pl.semaphore_wait(pltpu.get_barrier_semaphore(), count)


def send_seq(s, source, target, send, recv):
    for k in range(1, NS):
        peer = lax.rem(s + k, NS)
        pltpu.make_async_remote_copy(
            src_ref=source(peer),
            dst_ref=target,
            send_sem=send,
            recv_sem=recv,
            device_id={"seq": peer},
            device_id_type=MESH,
        ).start()


def send_fsdp(f, source, target, send, recv):
    def one(k, carried):
        peer = lax.rem(f + k, NF)
        pltpu.make_async_remote_copy(
            src_ref=source(peer),
            dst_ref=target,
            send_sem=send,
            recv_sem=recv,
            device_id={"fsdp": peer},
            device_id_type=MESH,
        ).start()
        return carried

    lax.fori_loop(1, NF, one, 0)


def await_bytes(ref, sem):
    pltpu.make_async_copy(ref, ref, sem).wait()


def hop(source, target, to, send, recv, n):
    return pltpu.make_async_remote_copy(
        src_ref=source,
        dst_ref=target,
        send_sem=send.at[n],
        recv_sem=recv.at[n],
        device_id={"seq": to},
        device_id_type=MESH,
    )


def around(s):
    return lax.rem(s + 1, NS), lax.rem(s + NS - 1, NS), lax.rem(s + 2, NS)


def slot_hots(picks):
    lane = lax.broadcasted_iota(jnp.int32, (LB, E), 1)
    named = [picks[:, c : c + 1] == lane for c in range(2)]
    down = lax.broadcasted_iota(jnp.int32, (LB, LB), 0)
    across = lax.broadcasted_iota(jnp.int32, (LB, LB), 1)
    counts = dot((across < down).astype(BF16), (named[0] | named[1]).astype(BF16))
    slots = lax.broadcasted_iota(jnp.int32, (LB, NF * ROWS), 1)
    hots = []
    for c in range(2):
        rank = jnp.sum(jnp.where(named[c], counts, 0.0), axis=1, keepdims=True).astype(jnp.int32)
        pick = picks[:, c : c + 1]
        odd = pick & 1
        row = jnp.where(rank < 8, 8 * odd + rank, 8 + 4 * odd + rank)
        hots.append((slots == (pick >> 1) * ROWS + row).astype(BF16))
    return hots


def start_kernel(
    wo_ref, wq_ref, wk_ref, wv_ref, router_ref, one_ref, two_ref, table_ref, x_ref, picks_ref, dy_in,
    wg_out, xg, dy_own, dy_near, hots_out, packed, wg, dy_rows, hots, send, recv, local,
):
    s, f = place_of()
    right, left, far = around(s)
    pair, core = f // 2, lax.rem(f, 2)
    packed[:, :D] = wo_ref[...]
    for i in range(NS):

        @pl.when(s == i)
        def _():
            for n, w in enumerate((wq_ref, wk_ref, wv_ref)):
                at = D + n * HW
                packed[:, at : at + HW] = w[:, i * HW : (i + 1) * HW]

    packed[:, D + 3 * HW : MISC] = jnp.zeros((D // NF, MISC - D - 3 * HW), BF16)
    packed[:, MISC : MISC + E] = router_ref[...]
    share = D // NF
    square = (share, share)
    across = lax.broadcasted_iota(jnp.int32, square, 1)
    along = lax.broadcasted_iota(jnp.int32, square, 0) == across
    columns = [
        jnp.sum(jnp.where(along, gain[...].astype(F32), 0.0), axis=1, keepdims=True)
        for gain in (one_ref, two_ref)
    ]
    lane = lax.broadcasted_iota(jnp.int32, (H, 64), 1)
    head = lax.broadcasted_iota(jnp.int32, (H, 64), 0)
    taken = (head == HL * s + lane - 2) & (lane >= 2) & (lane < 2 + HL)
    line = dot(jnp.broadcast_to(table_ref[...], (8, H)), taken.astype(BF16))
    lane = lax.broadcasted_iota(jnp.int32, (share, 64), 1)
    row = lax.broadcasted_iota(jnp.int32, (share, 64), 0)
    misc = jnp.where(row == 0, jnp.broadcast_to(line[0:1], (share, 64)), 0.0)
    misc = jnp.where(lane == 0, columns[0], jnp.where(lane == 1, columns[1], misc))
    packed[:, MISC + E :] = misc.astype(BF16)
    count = greet_fsdp(f) + greet_seq(s)
    picks = picks_ref[...]
    one_hot, two_hot = slot_hots(picks)
    hots[0] = one_hot
    hots[1] = two_hot
    dy = dot(one_hot + two_hot, dy_in[...], ((0,), (0,)))
    dy_rows[:, :, :D] = dy.reshape(NF, ROWS, D).astype(BF16)
    named = [jnp.broadcast_to(picks[:, c : c + 1].astype(F32), (LB, 128)) for c in range(2)]
    others = dot(one_hot, named[1].astype(BF16), ((0,), (0,)))
    others = others + dot(two_hot, named[0].astype(BF16), ((0,), (0,)))
    dy_rows[:, :, D:] = others.reshape(NF, ROWS, 128).astype(BF16)
    arrive(count)
    first, second = pl.ds(0, LB // 2), pl.ds(LB // 2, LB // 2)
    x_begin = [hop(x_ref, xg.at[s], to, send, recv, n) for n, to in enumerate((right, left))]
    x_relay = [
        hop(xg.at[left, first], xg.at[left, first], right, send, recv, 2),
        hop(xg.at[right, second], xg.at[right, second], left, send, recv, 3),
    ]
    half = dy_own.at[pl.ds(0, NF // 2)]
    y_begin = [
        hop(half, dy_near.at[n], to, send, recv, 4 + n) for n, to in enumerate((right, left))
    ]
    for copy in x_begin:
        copy.start()
    send_fsdp(f, lambda peer: dy_rows.at[peer], dy_own.at[f], send.at[7], recv.at[7])

    def one(k, carried):
        peer = lax.rem(pair + k, NF // 2)
        pltpu.make_async_remote_copy(
            src_ref=packed,
            dst_ref=wg.at[pair, core],
            send_sem=send.at[6],
            recv_sem=recv.at[6],
            device_id={"fsdp": 2 * peer + core},
            device_id_type=MESH,
        ).start()
        return carried

    lax.fori_loop(1, NF // 2, one, 0)
    own_x = pltpu.make_async_copy(x_ref, xg.at[s], local.at[0])
    own_w = pltpu.make_async_copy(packed, wg.at[pair, core], local.at[1])
    own_x.start()
    own_w.start()
    own_dy = pltpu.make_async_copy(dy_rows.at[f], dy_own.at[f], local.at[2])
    own_dy.start()
    keep = pltpu.make_async_copy(hots, hots_out, local.at[3])
    keep.start()
    for n in range(2):
        x_begin[n].wait_recv()
        x_relay[n].start()
    own_w.wait()
    others_w = wg.at[pl.ds(0, NF // 2 - 1), core]
    swap = pltpu.make_async_remote_copy(
        src_ref=wg.at[:, core],
        dst_ref=wg.at[:, core],
        send_sem=send.at[8],
        recv_sem=recv.at[8],
        device_id={"fsdp": 2 * pair + 1 - core},
        device_id_type=MESH,
    )
    own_dy.wait()
    others_dy = dy_own.at[pl.ds(0, NF - 1)]
    await_bytes(others_dy, recv.at[7])
    for copy in y_begin:
        copy.start()
    await_bytes(others_w, recv.at[6])
    swap.start()
    swap.wait_recv()
    store = pltpu.make_async_copy(wg, wg_out, local.at[4])
    store.start()
    own_x.wait()
    keep.wait()
    store.wait()
    for copy in x_relay + y_begin:
        copy.wait_recv()
    for copy in x_begin + x_relay + y_begin + [swap]:
        copy.wait_send()
    await_bytes(others_w, send.at[6])
    await_bytes(others_dy, send.at[7])


def start_exchange(w_out, w_query, w_key, w_value, router, one, two, table, tokens, picks, dy):
    share = D // NF
    rows = (NF, ROWS, MSG)
    return pl.pallas_call(
        start_kernel,
        out_shape=(
            jax.ShapeDtypeStruct((NF // 2, 2, share, PACK), BF16),
            jax.ShapeDtypeStruct((NS, LB, D), BF16),
            jax.ShapeDtypeStruct(rows, BF16),
            jax.ShapeDtypeStruct((2, NF // 2, ROWS, MSG), BF16),
            jax.ShapeDtypeStruct((2, LB, NF * ROWS), BF16),
        ),
        in_specs=[vmem_spec()] * 11,
        out_specs=(hbm_spec(),) * 5,
        scratch_shapes=[
            pltpu.VMEM((share, PACK), BF16),
            pltpu.VMEM((NF // 2, 2, share, PACK), BF16),
            pltpu.VMEM(rows, BF16),
            pltpu.VMEM((2, LB, NF * ROWS), BF16),
            pltpu.SemaphoreType.DMA((9,)),
            pltpu.SemaphoreType.DMA((9,)),
            pltpu.SemaphoreType.DMA((5,)),
        ],
        compiler_params=params(0),
        name="start_exchange",
    )(w_out, w_query, w_key, w_value, router, one, two, table, tokens, picks, dy)


def sum_pairs(f, w_ref, wg, mine, theirs, send, recv, local, first):
    pair, core = f // 2, lax.rem(f, 2)
    swap = pltpu.make_async_remote_copy(
        src_ref=w_ref.at[:, 1 - core],
        dst_ref=theirs,
        send_sem=send.at[first],
        recv_sem=recv.at[first],
        device_id={"fsdp": 2 * pair + 1 - core},
        device_id_type=MESH,
    )
    own = pltpu.make_async_copy(w_ref.at[:, core], mine, local.at[first])
    keep = pltpu.make_async_copy(mine.at[pair], wg.at[pair], local.at[first + 1])
    others = wg.at[pl.ds(0, NF // 2 - 1)]

    def begin():
        swap.start()
        own.start()

    def middle():
        own.wait()
        swap.wait_recv()

        def add(i, carried):
            mine[i] = (mine[i].astype(F32) + theirs[i].astype(F32)).astype(BF16)
            return carried

        lax.fori_loop(0, NF // 2, add, 0)

        def one(k, carried):
            peer = lax.rem(pair + k, NF // 2)
            pltpu.make_async_remote_copy(
                src_ref=mine.at[peer],
                dst_ref=wg.at[pair],
                send_sem=send.at[first + 1],
                recv_sem=recv.at[first + 1],
                device_id={"fsdp": 2 * peer + core},
                device_id_type=MESH,
            ).start()
            return carried

        lax.fori_loop(1, NF // 2, one, 0)
        keep.start()

    def finish():
        keep.wait()
        await_bytes(others, recv.at[first + 1])

    def end():
        swap.wait_send()
        await_bytes(others, send.at[first + 1])

    return begin, middle, finish, end


def last_kernel(
    b_ref, x_ref, a_ref, all_a, all_b, xg, mine, theirs, got, sum_a, sum_b, summed, work,
    send, recv, local,
):
    s, f = place_of()
    right, left, far = around(s)
    half = LB // 2
    first, second = pl.ds(0, half), pl.ds(half, half)
    arrive(greet_fsdp(f) + greet_seq(s))
    begin, middle, finish, end = sum_pairs(f, b_ref, got, mine, theirs, send, recv, local, 0)
    onward = [
        hop(x_ref.at[far, first], summed.at[0], right, send, recv, 2),
        hop(x_ref.at[far, second], summed.at[1], left, send, recv, 3),
    ]
    early = [
        hop(x_ref.at[right, second], xg.at[0, second], right, send, recv, 4),
        hop(x_ref.at[left, first], xg.at[1, first], left, send, recv, 5),
    ]
    late = [
        hop(work.at[0], xg.at[0, first], right, send, recv, 6),
        hop(work.at[1], xg.at[1, second], left, send, recv, 7),
    ]
    for copy in onward:
        copy.start()
    begin()
    for copy in early:
        copy.start()
    own_x = pltpu.make_async_copy(x_ref.at[s], xg.at[2], local.at[2])
    own_x.start()
    middle()
    for n, block, rows in ((0, right, first), (1, left, second)):
        onward[n].wait_recv()
        work[n] = (x_ref[block, rows].astype(F32) + summed[n].astype(F32)).astype(BF16)
        late[n].start()

    def total(blocks):
        value = blocks[0].astype(F32)
        for i in range(1, NF // 2):
            value = value + blocks[i].astype(F32)
        return value

    sum_a[...] = total(a_ref)
    send_seq(s, lambda peer: sum_a, all_a.at[s], send.at[8], recv.at[8])
    own_a = pltpu.make_async_copy(sum_a, all_a.at[s], local.at[3])
    own_a.start()
    finish()
    sum_b[...] = total(got)
    send_seq(s, lambda peer: sum_b, all_b.at[s], send.at[9], recv.at[9])
    own_b = pltpu.make_async_copy(sum_b, all_b.at[s], local.at[4])
    own_b.start()
    own_x.wait()
    own_a.wait()
    own_b.wait()
    for n, out in ((8, all_a), (9, all_b)):
        others = out.at[pl.ds(0, NS - 1)]
        await_bytes(others, recv.at[n])
        await_bytes(others, send.at[n])
    for copy in early + late:
        copy.wait_recv()
    for copy in onward + early + late:
        copy.wait_send()
    end()


def last_exchange(b, x, a, collective_id):
    half = (b.shape[0],) + b.shape[2:]
    return pl.pallas_call(
        last_kernel,
        out_shape=(
            jax.ShapeDtypeStruct((NS,) + a.shape[1:], F32),
            jax.ShapeDtypeStruct((NS,) + b.shape[2:], F32),
            jax.ShapeDtypeStruct((3,) + x.shape[1:], x.dtype),
        ),
        in_specs=[vmem_spec()] * 3,
        out_specs=(any_spec(), any_spec(), any_spec()),
        scratch_shapes=[
            pltpu.VMEM(half, BF16),
            pltpu.VMEM(half, BF16),
            pltpu.VMEM(half, BF16),
            pltpu.VMEM(a.shape[1:], F32),
            pltpu.VMEM(b.shape[2:], F32),
            pltpu.VMEM((2, LB // 2, D), BF16),
            pltpu.VMEM((2, LB // 2, D), BF16),
            pltpu.SemaphoreType.DMA((10,)),
            pltpu.SemaphoreType.DMA((10,)),
            pltpu.SemaphoreType.DMA((5,)),
        ],
        compiler_params=params(collective_id),
        name="last_exchange",
    )(b, x, a)


def bias_tiles(base_ref, tiles, head):
    for d in range(NS):
        wide = jnp.broadcast_to(base_ref[head, d : d + 1, :], (LB, SPAN))
        tiles[d] = pltpu.roll(wide, 0, 1, stride=1, stride_axis=0)[:, :LB]


def score_tiles(qkv_ref, tiles, head, block):
    rows, cols = slice(block * LB, (block + 1) * LB), head * HD
    query = qkv_ref[rows, cols : cols + HD]
    parts = []
    for kb in range(block + 1):
        keys = qkv_ref[kb * LB : (kb + 1) * LB, HW + cols : HW + cols + HD]
        parts.append(dot(query, keys, ((1,), (1,))) * (HD**-0.5) + tiles[block - kb])
    return parts


def front_kernel(
    full_in, all_in, x_in, slots_in, hots_in, dy_ref,
    qkv_out, base_out, lse_out, mixed_out, x1_out, xn2_out, rows_out, gains_out, dy_near,
    full_ref, all_ref, x_ref, slots_ref, hots_ref,
    qkv_ref, base_ref, lse_ref, mixed, x1_ref, xn2_ref, rows_ref, gains_ref,
    o, tiles, send, recv, local, stage,
):
    s, f = place_of()
    right, left, _ = around(s)
    loads = [
        pltpu.make_async_copy(source, target, stage.at[n])
        for n, (source, target) in enumerate(
            (
                (full_in, full_ref),
                (slots_in, slots_ref),
                (all_in, all_ref),
                (x_in, x_ref),
                (hots_in, hots_ref),
            )
        )
    ]
    stores = [
        pltpu.make_async_copy(source, target, stage.at[5 + n])
        for n, (source, target) in enumerate(
            (
                (gains_ref, gains_out),
                (base_ref, base_out),
                (qkv_ref, qkv_out),
                (lse_ref, lse_out),
                (mixed, mixed_out),
                (x1_ref, x1_out),
                (xn2_ref, xn2_out),
                (rows_ref, rows_out),
            )
        )
    ]
    for load in loads:
        load.start()
    arrive(greet_seq(s))
    half = dy_ref.at[pl.ds(NF // 2, NF // 2)]
    beside = [hop(half, dy_near.at[n], to, send, recv, n) for n, to in enumerate((right, left))]
    for copy in beside:
        copy.start()
    for load in loads[:2]:
        load.wait()
    misc = full_ref[:, MISC:].astype(F32)
    turned = jnp.transpose(misc)
    gains_ref[...] = turned[E : E + 8]
    stores[0].start()
    gain_one, gain_two = turned[E : E + 1], turned[E + 1 : E + 2]
    table = misc.reshape(NB, D // NF, 128)[:, 0, :].astype(BF16)
    slots = slots_ref[...]
    hot = (slots == lax.broadcasted_iota(jnp.int32, (NB, NS * SPAN), 0)).astype(BF16)
    base = dot(table, hot, ((0,), (0,)))[E : E + 8]
    base = jnp.where(slots < 0, -1e30, base)
    for head in range(HL):
        for d in range(NS):
            line = base[2 + head : 3 + head, d * SPAN : (d + 1) * SPAN]
            base_ref[head, d : d + 1, :] = line
        bias_tiles(base_ref, tiles.at[head], head)
    stores[1].start()
    loads[2].wait()
    for block in range(NS):
        x = all_ref[block].astype(F32)
        xn1 = (x * row_factor(x) * gain_one).astype(BF16)
        rows = slice(block * LB, (block + 1) * LB)
        qkv_ref[rows, :] = dot(xn1, full_ref[:, D : D + 3 * HW]).astype(BF16)
    stores[2].start()
    for block in range(NS):
        rows = slice(block * LB, (block + 1) * LB)
        for head in range(HL):
            cols = slice(head * HD, (head + 1) * HD)
            parts = score_tiles(qkv_ref, tiles.at[head], head, block)
            top = parts[0].max(axis=1, keepdims=True)
            for part in parts[1:]:
                top = jnp.maximum(top, part.max(axis=1, keepdims=True))
            parts = [jnp.exp(part - top) for part in parts]
            total = parts[0].sum(axis=1, keepdims=True)
            for part in parts[1:]:
                total = total + part.sum(axis=1, keepdims=True)
            inverse = 1.0 / total
            value = None
            for kb, part in enumerate(parts):
                keys = slice(kb * LB, (kb + 1) * LB)
                values = qkv_ref[keys, 2 * HW + head * HD : 2 * HW + (head + 1) * HD]
                term = dot((part * inverse).astype(BF16), values)
                value = term if value is None else value + term
            o[block, :, cols] = value.astype(BF16)
            lse_ref[rows, head : head + 1] = top + jnp.log(total)

        @pl.when(s != block)
        def _():
            pltpu.make_async_remote_copy(
                src_ref=o.at[block],
                dst_ref=mixed.at[s],
                send_sem=send.at[2],
                recv_sem=recv.at[2],
                device_id={"seq": block},
                device_id_type=MESH,
            ).start()

    own = pltpu.make_async_copy(o.at[s], mixed.at[s], local)
    own.start()
    stores[3].start()
    for load in loads[3:]:
        load.wait()
    own.wait()
    others = mixed.at[pl.ds(0, NS - 1)]
    await_bytes(others, recv.at[2])
    stores[4].start()
    x1 = x_ref[...].astype(F32)
    for i in range(NS):
        x1 = x1 + dot(mixed[i], full_ref[i * HW : (i + 1) * HW, :D])
    x1_ref[...] = x1
    stores[5].start()
    xn2 = (x1 * row_factor(x1) * gain_two).astype(BF16)
    xn2_ref[...] = xn2
    stores[6].start()
    rows = dot(hots_ref[0] + hots_ref[1], xn2, ((0,), (0,)))
    rows_ref[...] = rows.reshape(NF, ROWS, D).astype(BF16)
    stores[7].start()
    await_bytes(others, send.at[2])
    for copy in beside:
        copy.wait_recv()
        copy.wait_send()
    for store in stores:
        store.wait()


def front(full, all_tokens, tokens, slots, hots, dy_own, collective_id):
    inputs = (full, all_tokens, tokens, slots, hots)
    made = [
        ((LEN, 3 * HW), BF16),
        ((HL, NS, SPAN), F32),
        ((LEN, 128), F32),
        ((NS, LB, HW), BF16),
        ((LB, D), F32),
        ((LB, D), BF16),
        ((NF, ROWS, D), BF16),
        ((8, D), F32),
    ]
    return pl.pallas_call(
        front_kernel,
        out_shape=tuple(jax.ShapeDtypeStruct(*m) for m in made)
        + (jax.ShapeDtypeStruct((2, NF // 2) + dy_own.shape[1:], BF16),),
        in_specs=[hbm_spec()] * 6,
        out_specs=(hbm_spec(),) * 9,
        scratch_shapes=[pltpu.VMEM(i.shape, i.dtype) for i in inputs]
        + [pltpu.VMEM(*m) for m in made]
        + [
            pltpu.VMEM((NS, LB, HW), BF16),
            pltpu.VMEM((HL, NS, LB, LB), F32),
            pltpu.SemaphoreType.DMA((3,)),
            pltpu.SemaphoreType.DMA((3,)),
            pltpu.SemaphoreType.DMA,
            pltpu.SemaphoreType.DMA((13,)),
        ],
        compiler_params=params(collective_id),
        name="front",
    )(full, all_tokens, tokens, slots, hots, dy_own)


def flip_rows(values):
    down = lax.broadcasted_iota(jnp.int32, (LB, LB), 0)
    across = lax.broadcasted_iota(jnp.int32, (LB, LB), 1)
    swap = (down + across == LB - 1).astype(BF16)
    high = values.astype(BF16)
    low = (values - high.astype(F32)).astype(BF16)
    return dot(swap, high) + dot(swap, low)


def backward_kernel(
    qkv_ref, do_ref, lse_ref, base_ref, pack_ref, g_ref, diag_ref, sums,
    do, tiles, folds, dk, dv, mine, theirs, send, recv, local,
):
    s, f = place_of()
    arrive(greet_fsdp(f) + greet_seq(s))
    begin, middle, finish, end = sum_pairs(
        f, pack_ref, sums, mine, theirs, send, recv, local, 0
    )
    send_seq(s, lambda peer: do_ref.at[peer], do.at[s], send.at[2], recv.at[2])
    own = pltpu.make_async_copy(do_ref.at[s], do.at[s], local.at[2])
    own.start()
    begin()
    for head in range(HL):
        bias_tiles(base_ref, tiles.at[head], head)
    middle()
    own.wait()
    others = do.at[pl.ds(0, NS - 1)]
    await_bytes(others, recv.at[2])
    scale = HD**-0.5
    for head in range(HL):
        cols = slice(head * HD, (head + 1) * HD)
        values = slice(2 * HW + head * HD, 2 * HW + (head + 1) * HD)
        for block in range(NS):
            rows = slice(block * LB, (block + 1) * LB)
            query, grad = qkv_ref[rows, cols], do[block, :, cols]
            lse = lse_ref[rows, head : head + 1]
            parts = score_tiles(qkv_ref, tiles.at[head], head, block)
            probs = [jnp.exp(part - lse) for part in parts]
            grads = [
                dot(grad, qkv_ref[kb * LB : (kb + 1) * LB, values], ((1,), (1,)))
                for kb in range(block + 1)
            ]
            delta = None
            for prob, part in zip(probs, grads):
                term = (prob * part).sum(axis=1, keepdims=True)
                delta = term if delta is None else delta + term
            grad_query = None
            for kb in range(block + 1):
                keys = slice(kb * LB, (kb + 1) * LB)
                d = block - kb
                ds = probs[kb] * (grads[kb] - delta)
                if kb == 0:
                    folds[d] = ds
                else:
                    folds[d] += ds
                raw = (ds * scale).astype(BF16)
                term = dot(raw, qkv_ref[keys, HW + head * HD : HW + (head + 1) * HD])
                grad_query = term if grad_query is None else grad_query + term
                to_key = dot(raw, query, ((0,), (0,)))
                to_value = dot(probs[kb].astype(BF16), grad, ((0,), (0,)))
                if d == 0:
                    dk[keys, :] = to_key
                    dv[keys, :] = to_value
                else:
                    dk[keys, :] += to_key
                    dv[keys, :] += to_value
            g_ref[rows, cols] = grad_query.astype(BF16)
        g_ref[:, HW + head * HD : HW + (head + 1) * HD] = dk[...].astype(BF16)
        g_ref[:, 2 * HW + head * HD : 2 * HW + (head + 1) * HD] = dv[...].astype(BF16)
        for d in range(NS):
            wide = jnp.concatenate(
                [flip_rows(folds[d]), jnp.zeros((LB, SPAN - LB), F32)], axis=1
            )
            turned = pltpu.roll(wide, LB + 1, 1, stride=1, stride_axis=0)
            at = slice(d * SPAN, (d + 1) * SPAN)
            diag_ref[head : head + 1, at] = turned.sum(axis=0, keepdims=True)
    await_bytes(others, send.at[2])
    finish()
    end()


def attend_backward(qkv, do, lse, base, pack, collective_id):
    half = (pack.shape[0],) + pack.shape[2:]
    return pl.pallas_call(
        backward_kernel,
        out_shape=(
            jax.ShapeDtypeStruct((LEN, 3 * HW), BF16),
            jax.ShapeDtypeStruct((HL, NS * SPAN), F32),
            jax.ShapeDtypeStruct(half, BF16),
        ),
        in_specs=[vmem_spec()] * 5,
        out_specs=(vmem_spec(), vmem_spec(), any_spec()),
        scratch_shapes=[
            pltpu.VMEM((NS, LB, HW), BF16),
            pltpu.VMEM((HL, NS, LB, LB), F32),
            pltpu.VMEM((NS, LB, LB), F32),
            pltpu.VMEM((LEN, HD), F32),
            pltpu.VMEM((LEN, HD), F32),
            pltpu.VMEM(half, BF16),
            pltpu.VMEM(half, BF16),
            pltpu.SemaphoreType.DMA((3,)),
            pltpu.SemaphoreType.DMA((3,)),
            pltpu.SemaphoreType.DMA((3,)),
        ],
        compiler_params=params(collective_id),
        name="attend_backward",
    )(qkv, do, lse, base, pack)


def split_rows(rows):
    width = rows.shape[-1]
    half = NF // 2
    mixed = rows[:, 16:24]
    left, right = mixed[:half], mixed[half:]
    low = lax.broadcasted_iota(jnp.int32, left.shape, 1) < 4
    one = jnp.where(low, left, pltpu.roll(right, 4, 1)).reshape(half * 8, width)
    two = jnp.where(low, pltpu.roll(left, 4, 1), right).reshape(half * 8, width)
    return (
        jnp.concatenate([rows[:, 0:8].reshape(NF * 8, width), one], axis=0),
        jnp.concatenate([rows[:, 8:16].reshape(NF * 8, width), two], axis=0),
    )


def join_rows(first, second):
    width = first.shape[-1]
    half = NF // 2
    one = first[NF * 8 :].reshape(half, 8, width)
    two = second[NF * 8 :].reshape(half, 8, width)
    low = lax.broadcasted_iota(jnp.int32, one.shape, 1) < 4
    left = jnp.where(low, one, pltpu.roll(two, 4, 1))
    right = jnp.where(low, pltpu.roll(one, 4, 1), two)
    return jnp.concatenate(
        [
            first[: NF * 8].reshape(NF, 8, width),
            second[: NF * 8].reshape(NF, 8, width),
            jnp.concatenate([left, right], axis=0),
        ],
        axis=1,
    )


def expert_rows(x, dy, ids, own, router, w_in, w_out):
    logits = dot(x, router)
    lane = lax.broadcasted_iota(jnp.int32, logits.shape, 1)
    one = jnp.sum(jnp.where(lane == own, logits, 0.0), axis=1, keepdims=True)
    two = jnp.sum(jnp.where(lane == ids, logits, 0.0), axis=1, keepdims=True)
    top = jnp.maximum(one, two)
    one, two = jnp.exp(one - top), jnp.exp(two - top)
    gate = one / (one + two)
    grad = (dy * gate).astype(BF16)
    u = dot(x, w_in)
    square = u * u
    tanh = jnp.tanh(u * (0.7978845608028654 + (0.7978845608028654 * 0.044715) * square))
    half = 0.5 * (1.0 + tanh)
    hid = (u * half).astype(BF16)
    slope = half + (0.5 * u) * (1.0 - tanh * tanh) * (
        0.7978845608028654 + (3.0 * 0.7978845608028654 * 0.044715) * square
    )
    y = dot(hid, w_out)
    du = (dot(grad, w_out, ((1,), (1,))) * slope).astype(BF16)
    dx = dot(du, w_in, ((1,), (1,)))
    return y, dx, hid, grad, du


def expert_kernel(
    x_ref, dy_own, near_a, near_b, full_ref, wi_in, wo_in,
    y_out, dx_out, gi_out, go_out, dy_far,
    router_ref, wi_ref, wo_ref, gi_ref, go_ref,
    x, dy, part, near, summed, kept, send, recv, local,
):
    s, f = place_of()
    right, left, far = around(s)
    half = NF // 2
    first, second = pl.ds(0, half), pl.ds(half, half)
    columns = [pl.ds(0, D // 2), pl.ds(D // 2, D // 2)]
    loads = [
        pltpu.make_async_copy(source, target, local.at[7 + n])
        for n, (source, target) in enumerate(
            ((wi_in, wi_ref), (wo_in, wo_ref), (full_ref.at[:, pl.ds(MISC, 128)], router_ref))
        )
    ]
    stores = [
        pltpu.make_async_copy(gi_ref, gi_out, local.at[10]),
        pltpu.make_async_copy(go_ref, go_out, local.at[11]),
    ]
    for load in loads:
        load.start()
    arrive(greet_fsdp(f) + greet_seq(s))

    def step_to(source, target, to, n):
        return hop(source, target, to, send, recv, n)

    for c in range(2):
        send_fsdp(
            f,
            lambda peer: x_ref.at[peer, :, columns[c]],
            x.at[s, f, :, columns[c]],
            send.at[c],
            recv.at[c],
        )
    dy_relay = [
        step_to(near_a.at[0], dy_far.at[first], right, 2),
        step_to(near_b.at[1], dy_far.at[second], left, 3),
    ]
    for copy in dy_relay:
        copy.start()
    own_x = pltpu.make_async_copy(x_ref.at[f], x.at[s, f], local.at[0])
    own_x.start()
    gi_ref[...] = jnp.zeros_like(gi_ref)
    go_ref[...] = jnp.zeros_like(go_ref)
    begin, early, onward, late = [], [], [], []
    for c in range(2):
        block = x.at[s, :, :, columns[c]]
        begin.append([step_to(block, block, to, 4 + 2 * c + n) for n, to in enumerate((right, left))])
    relay = [
        step_to(x.at[left, first], x.at[left, first], right, 8),
        step_to(x.at[right, second], x.at[right, second], left, 9),
    ]
    for a in range(2):
        early.append(
            [
                step_to(part.at[a, right, second], near.at[a, 0, second], right, 10 + 2 * a),
                step_to(part.at[a, left, first], near.at[a, 1, first], left, 11 + 2 * a),
            ]
        )
        onward.append(
            [
                step_to(part.at[a, far, first], summed.at[a, 0], right, 14 + 2 * a),
                step_to(part.at[a, far, second], summed.at[a, 1], left, 15 + 2 * a),
            ]
        )
        late.append(
            [
                [
                    step_to(
                        part.at[a, right, first, :, columns[c]],
                        near.at[a, 0, first, :, columns[c]],
                        right,
                        18 + 4 * a + 2 * c,
                    ),
                    step_to(
                        part.at[a, left, second, :, columns[c]],
                        near.at[a, 1, second, :, columns[c]],
                        left,
                        19 + 4 * a + 2 * c,
                    ),
                ]
                for c in range(2)
            ]
        )
    for load in loads:
        load.wait()
    own_x.wait()
    others_x = [x.at[s, pl.ds(0, NF - 1), :, columns[c]] for c in range(2)]
    for c in range(2):
        await_bytes(others_x[c], recv.at[c])
        for copy in begin[c]:
            copy.start()

    def step(k, carried):
        chunk = lax.rem(s + jnp.where(k == 1, 3, jnp.where(k == 0, 0, k - 1)), NS)

        @pl.when(k == 3)
        def _():
            for copy in dy_relay + relay:
                copy.wait_recv()

        for n, (low, high) in enumerate(
            (
                (dy_own.at[first], dy_own.at[second]),
                (near_a.at[0], near_b.at[0]),
                (near_a.at[1], near_b.at[1]),
                (dy_far.at[first], dy_far.at[second]),
            )
        ):

            @pl.when(k == n)
            def _():
                loads = [
                    pltpu.make_async_copy(low, dy.at[first], local.at[1]),
                    pltpu.make_async_copy(high, dy.at[second], local.at[2]),
                ]
                for load in loads:
                    load.start()
                for load in loads:
                    load.wait()

        @pl.when(k == 1)
        def _():
            for n in range(2):
                for c in range(2):
                    begin[c][n].wait_recv()
                relay[n].start()

        xs = split_rows(x[chunk].astype(F32))
        dys = split_rows(dy[...].astype(F32))
        ys, dxs = [], []
        for j in range(2):
            rows = xs[j].astype(BF16)
            ids = dys[j][:, D:].astype(jnp.int32)
            y, dx, hid, grad, du = expert_rows(
                rows, dys[j][:, :D], ids, 2 * f + j, router_ref[...], wi_ref[j], wo_ref[j]
            )
            ys.append(y)
            dxs.append(dx)
            slot = jnp.where(k == 0, 0, k - 1)
            for n, value in enumerate((rows, hid, grad, du)):
                kept[slot, n, j] = value
        part[0, chunk] = join_rows(*ys).astype(BF16)
        part[1, chunk] = join_rows(*dxs).astype(BF16)

        @pl.when(k == 1)
        def _():
            for a in range(2):
                early[a][1].start()

        @pl.when(k == 2)
        def _():
            early[0][0].start()

        @pl.when(k == 3)
        def _():
            for a in range(2):
                for n in range(2):
                    onward[a][n].start()

        @pl.when(k == 0)
        def _():
            weights(0, 0)

        return carried

    def weights(slot, carried):
        for j in range(2):
            go_ref[j] += dot(kept[slot, 1, j], kept[slot, 2, j], ((0,), (0,)))
            gi_ref[j] += dot(kept[slot, 0, j], kept[slot, 3, j], ((0,), (0,)))
        return carried

    lax.fori_loop(0, NS, step, 0)
    lax.fori_loop(0, NS - 1, weights, 0)
    for store in stores:
        store.start()

    def add(a, block, offset, cols, other):
        def one(i, carried):
            rows = pl.ds(offset + 8 * i, 8)
            total = part[a, block, rows, :, cols].astype(F32) + other(pl.ds(8 * i, 8))
            part[a, block, rows, :, cols] = total.astype(BF16)
            return carried

        return one

    for a in range(2):
        for n in range(2):
            onward[a][n].wait_recv()
        for c in range(2):
            for n, block, offset in ((0, right, 0), (1, left, half)):
                lax.fori_loop(
                    0,
                    half // 8,
                    add(
                        a,
                        block,
                        offset,
                        columns[c],
                        lambda i: summed[a, n, i, :, columns[c]].astype(F32),
                    ),
                    0,
                )
                late[a][c][n].start()
        if a == 0:
            early[1][0].start()
    outs = (y_out, dx_out)
    pieces = []
    for a in range(2):
        for n in range(2):
            early[a][n].wait_recv()
        for c in range(2):
            cols = columns[c]
            for n in range(2):
                late[a][c][n].wait_recv()
            lax.fori_loop(
                0,
                NF // 8,
                add(
                    a,
                    s,
                    0,
                    cols,
                    lambda i: near[a, 0, i, :, cols].astype(F32)
                    + near[a, 1, i, :, cols].astype(F32),
                ),
                0,
            )
            p = 2 * a + c
            send_fsdp(
                f,
                lambda peer: part.at[a, s, peer, :, cols],
                outs[a].at[f, :, cols],
                send.at[26 + p],
                recv.at[26 + p],
            )
            keep = pltpu.make_async_copy(
                part.at[a, s, f, :, cols], outs[a].at[f, :, cols], local.at[3 + p]
            )
            keep.start()
            pieces.append((keep, outs[a].at[pl.ds(0, NF - 1), :, cols], 26 + p))
    for keep, others, n in pieces:
        keep.wait()
        await_bytes(others, recv.at[n])
        await_bytes(others, send.at[n])
    for a in range(2):
        for copy in early[a] + onward[a] + late[a][0] + late[a][1]:
            copy.wait_send()
    for copy in begin[0] + begin[1] + relay + dy_relay:
        copy.wait_send()
    for c in range(2):
        await_bytes(others_x[c], send.at[c])
    for store in stores:
        store.wait()


def run_experts(x, dy, near_a, near_b, full, w_in, w_out, collective_id):
    rows = (NF, ROWS, D)
    return pl.pallas_call(
        expert_kernel,
        out_shape=(
            jax.ShapeDtypeStruct(rows, BF16),
            jax.ShapeDtypeStruct(rows, BF16),
            jax.ShapeDtypeStruct((2, D, D), F32),
            jax.ShapeDtypeStruct((2, D, D), F32),
            jax.ShapeDtypeStruct((NF, ROWS, MSG), BF16),
        ),
        in_specs=[any_spec()] * 7,
        out_specs=(any_spec(),) * 5,
        scratch_shapes=[
            pltpu.VMEM((D, 128), BF16),
            pltpu.VMEM((2, D, D), BF16),
            pltpu.VMEM((2, D, D), BF16),
            pltpu.VMEM((2, D, D), F32),
            pltpu.VMEM((2, D, D), F32),
            pltpu.VMEM((NS,) + rows, BF16),
            pltpu.VMEM((NF, ROWS, MSG), BF16),
            pltpu.VMEM((2, NS) + rows, BF16),
            pltpu.VMEM((2, 2) + rows, BF16),
            pltpu.VMEM((2, 2, NF // 2, ROWS, D), BF16),
            pltpu.VMEM((NS - 1, 4, 2, NF * CAP, D), BF16),
            pltpu.SemaphoreType.DMA((30,)),
            pltpu.SemaphoreType.DMA((30,)),
            pltpu.SemaphoreType.DMA((12,)),
        ],
        compiler_params=params(collective_id),
        name="run_experts",
    )(x, dy, near_a, near_b, full, w_in, w_out)


def token_kernel(
    y_in, dx_in, hot_in, x1_in, xn2_in, dy_in, picks_ref, gain_in, full_in, mixed_in,
    out_ref, dx1_ref, do_ref, pack_ref,
    xn2_ref, x1_ref, full_ref, dy_ref, hot_ref, y_ref, dx_ref, gain_ref, mixed_ref, stage,
):
    loads = [
        pltpu.make_async_copy(source, target, stage.at[n])
        for n, (source, target) in enumerate(
            (
                (xn2_in, xn2_ref),
                (x1_in, x1_ref),
                (full_in, full_ref),
                (dy_in, dy_ref),
                (hot_in, hot_ref),
                (y_in, y_ref),
                (dx_in, dx_ref),
                (gain_in, gain_ref),
                (mixed_in, mixed_ref),
            )
        )
    ]
    for load in loads:
        load.start()
    for load in loads[:6]:
        load.wait()
    xn2, x1, router = xn2_ref[...], x1_ref[...], full_ref[:, MISC:]
    dy = dy_ref[...].astype(F32)
    logits = dot(xn2, router)
    lane = lax.broadcasted_iota(jnp.int32, logits.shape, 1)
    named = [lane == picks_ref[:, c : c + 1] for c in range(2)]
    chosen = [jnp.sum(jnp.where(n, logits, 0.0), axis=1, keepdims=True) for n in named]
    top = jnp.maximum(chosen[0], chosen[1])
    chosen = [jnp.exp(value - top) for value in chosen]
    both = chosen[0] + chosen[1]
    gates = [value / both for value in chosen]
    ys = [dot(hot_ref[c], y_ref[...]) for c in range(2)]
    out_ref[...] = (x1 + (gates[0] * ys[0] + gates[1] * ys[1])).astype(BF16)
    dgates = [jnp.sum(dy * y, axis=1, keepdims=True) for y in ys]
    mean = gates[0] * dgates[0] + gates[1] * dgates[1]
    dpicks = [gates[c] * (dgates[c] - mean) for c in range(2)]
    dlogits = sum(jnp.where(named[c], dpicks[c], 0.0) for c in range(2)).astype(BF16)
    for load in loads[6:]:
        load.wait()
    dxn2 = dot(hot_ref[0] + hot_ref[1], dx_ref[...])
    dxn2 = dxn2 + dot(dlogits, router, ((1,), (1,)))
    r2 = row_factor(x1)
    terms = (dxn2 * x1 * r2).astype(BF16)
    grad_gain = dot(terms, jnp.ones((LB, 128), BF16), ((0,), (0,)))
    grad_router = dot(xn2, dlogits, ((0,), (0,)))
    lane = lax.broadcasted_iota(jnp.int32, grad_gain.shape, 1)
    pack_ref[:, D:] = jnp.where(lane == E, grad_gain, grad_router).astype(BF16)
    scaled = dxn2 * gain_ref[1:2]
    mean = jnp.mean(scaled * x1, axis=1, keepdims=True)
    dx1 = dy + r2 * scaled - x1 * (r2 * r2 * r2) * mean
    dx1_ref[...] = dx1
    dat = dx1.astype(BF16)
    for i in range(NS):
        rows = slice(i * HW, (i + 1) * HW)
        do_ref[i] = dot(dat, full_ref[rows, :D], ((1,), (1,))).astype(BF16)
        pack_ref[rows, :D] = dot(mixed_ref[i], dat, ((0,), (0,))).astype(BF16)


def token_side(y, dx, hot, x1, xn2, dy, picks, gains, full, mixed):
    staged = (xn2, x1, full, dy, hot, y, dx, gains, mixed)
    return pl.pallas_call(
        token_kernel,
        out_shape=(
            jax.ShapeDtypeStruct((LB, D), BF16),
            jax.ShapeDtypeStruct((LB, D), F32),
            jax.ShapeDtypeStruct((NS, LB, HW), BF16),
            jax.ShapeDtypeStruct((D, D + 128), BF16),
        ),
        in_specs=[hbm_spec()] * 6 + [vmem_spec()] + [hbm_spec()] * 3,
        out_specs=(vmem_spec(),) * 4,
        scratch_shapes=[pltpu.VMEM(i.shape, i.dtype) for i in staged]
        + [pltpu.SemaphoreType.DMA((9,))],
        compiler_params=params(),
        name="token_side",
    )(y, dx, hot, x1, xn2, dy, picks, gains, full, mixed)


def project_kernel(
    g_ref, x_ref, gain_ref, full_ref, slots_ref, diag_ref, gi_ref, go_ref,
    part_ref, pack_ref, gi_out, go_out, weight, held, local,
):
    loads = [
        pltpu.make_async_copy(gi_ref, held.at[0], local.at[0]),
        pltpu.make_async_copy(go_ref, held.at[1], local.at[1]),
    ]
    stores = [
        pltpu.make_async_copy(held.at[0], gi_out, local.at[2]),
        pltpu.make_async_copy(held.at[1], go_out, local.at[3]),
    ]
    for copy in loads:
        copy.start()
    weight[...] = jnp.zeros_like(weight)
    misc = jnp.zeros((D, 64), F32)
    for block in range(NS):
        rows = slice(block * LB, (block + 1) * LB)
        x = x_ref[block].astype(F32)
        r1 = row_factor(x)
        xn1 = (x * r1 * gain_ref[0:1]).astype(BF16)
        g = g_ref[rows, :]
        weight[...] += dot(xn1, g, ((0,), (0,)))
        part = dot(g, full_ref[:, D : D + 3 * HW], ((1,), (1,)))
        part_ref[block] = part.astype(BF16)
        terms = (part * x * r1).astype(BF16)
        misc = misc + dot(terms, jnp.ones((LB, 64), BF16), ((0,), (0,)))
        if block < 2:
            loads[block].wait()
            stores[block].start()
    lane = lax.broadcasted_iota(jnp.int32, misc.shape, 1)
    row = lax.broadcasted_iota(jnp.int32, (NB, NS * SPAN), 0)
    hot = (slots_ref[...] == row).astype(BF16)
    diag = jnp.concatenate(
        [jnp.zeros((8, NS * SPAN), F32), diag_ref[...], jnp.zeros((56 - HL, NS * SPAN), F32)],
        axis=0,
    )
    high = diag.astype(BF16)
    low = (diag - high.astype(F32)).astype(BF16)
    table = dot(hot, high, ((1,), (1,))) + dot(hot, low, ((1,), (1,)))
    table = jnp.broadcast_to(table[:, None, :], (NB, D // NF, 64)).reshape(D, 64)
    misc = jnp.where(lane == 0, misc, table)
    pack_ref[:, : 3 * HW] = weight[...].astype(BF16)
    pack_ref[:, 3 * HW :] = misc.astype(BF16)
    for copy in stores:
        copy.wait()


def project_back(g, x, gains, full, slots, diag, gi, go):
    return pl.pallas_call(
        project_kernel,
        out_shape=(
            jax.ShapeDtypeStruct((NS, LB, D), BF16),
            jax.ShapeDtypeStruct((D, 3 * HW + 64), BF16),
            jax.ShapeDtypeStruct(gi.shape, F32),
            jax.ShapeDtypeStruct(go.shape, F32),
        ),
        in_specs=[vmem_spec()] * 6 + [any_spec()] * 2,
        out_specs=(vmem_spec(), vmem_spec(), any_spec(), any_spec()),
        scratch_shapes=[
            pltpu.VMEM((D, 3 * HW), F32),
            pltpu.VMEM((2,) + gi.shape, F32),
            pltpu.SemaphoreType.DMA((4,)),
        ],
        compiler_params=params(),
        name="project_back",
    )(g, x, gains, full, slots, diag, gi, go)


def finish_kernel(
    a_ref, b_ref, part_ref, x_ref, dx1_ref, gain_ref,
    gx_ref, g1_ref, g2_ref, wq_ref, wk_ref, wv_ref, wo_ref, router_ref, table_ref,
):
    total = a_ref[0] + a_ref[1] + a_ref[2] + a_ref[3]
    wo_ref[...] = total[:, :D]
    router_ref[...] = total[:, D : D + E]
    g2_ref[...] = jnp.transpose(total[:, D:])[E : E + 1]
    misc = [b_ref[n, :, 3 * HW :] for n in range(NS)]
    gain = misc[0] + misc[1] + misc[2] + misc[3]
    g1_ref[...] = jnp.transpose(jnp.concatenate([gain, gain], axis=1))[0:1]
    table_ref[...] = jnp.concatenate([m[0:1, 8 : 8 + HL] for m in misc], axis=1)
    for i, out in enumerate((wq_ref, wk_ref, wv_ref)):
        out[...] = jnp.concatenate(
            [b_ref[n, :, i * HW : (i + 1) * HW] for n in range(NS)], axis=1
        )
    x = x_ref[...].astype(F32)
    r1 = row_factor(x)
    dxn1 = part_ref[0].astype(F32) + part_ref[1].astype(F32) + part_ref[2].astype(F32)
    scaled = dxn1 * gain_ref[0:1]
    mean = jnp.mean(scaled * x, axis=1, keepdims=True)
    gx_ref[...] = dx1_ref[...] + r1 * scaled - x * (r1 * r1 * r1) * mean


def finish(a, b, part, x, dx1, gain):
    share = D // NF
    return pl.pallas_call(
        finish_kernel,
        out_shape=(
            jax.ShapeDtypeStruct((LB, D), F32),
            jax.ShapeDtypeStruct((1, share), F32),
            jax.ShapeDtypeStruct((1, share), F32),
            jax.ShapeDtypeStruct((share, D), F32),
            jax.ShapeDtypeStruct((share, D), F32),
            jax.ShapeDtypeStruct((share, D), F32),
            jax.ShapeDtypeStruct((share, D), F32),
            jax.ShapeDtypeStruct((share, E), F32),
            jax.ShapeDtypeStruct((1, H), F32),
        ),
        in_specs=[vmem_spec()] * 6,
        out_specs=(vmem_spec(),) * 9,
        compiler_params=params(),
        name="finish",
    )(a, b, part, x, dx1, gain)


def distance_base(values, near, far):
    long = jnp.concatenate(
        [jnp.full((LB,), near, values.dtype), values, jnp.full((1,), far, values.dtype)]
    )
    rows = []
    for d in range(NS):
        rows.append(long[d * LB + 1 : d * LB + LB + 1][::-1])
        rows.append(long[LB + d * LB + 1 : LB + d * LB + LB + 1][::-1])
    return jnp.concatenate(rows)


def shards(
    tokens,
    gain_attn,
    gain_ffn,
    w_query,
    w_key,
    w_value,
    w_out,
    router,
    bias_table,
    expert_in,
    expert_out,
    choices,
    buckets,
    cotangent,
):
    s = lax.axis_index("seq")
    share = D // NF
    own_tokens = tokens.reshape(LB, D)

    picks = choices.reshape(LB, 2)
    dy_bf = cotangent.reshape(LB, D)
    gathered, all_tokens, dy_own, near_a, hots = start_exchange(
        w_out,
        w_query,
        w_key,
        w_value,
        router,
        gain_attn.reshape(1, share),
        gain_ffn.reshape(1, share),
        bias_table,
        own_tokens,
        picks,
        dy_bf,
    )
    full = gathered.reshape(D, PACK)
    slots = distance_base(buckets, -1, -1).reshape(1, NS * SPAN)
    qkv, base, lse, mixed, x1, xn2, x_rows, gains, near_b = front(
        full, all_tokens, own_tokens, slots, hots, dy_own, 1
    )
    y_back, dx_back, grad_in, grad_out, _ = run_experts(
        x_rows, dy_own, near_a, near_b, full, expert_in, expert_out, 2
    )
    layer_out, dx1, do, pack_a = token_side(
        y_back.reshape(NF * ROWS, D),
        dx_back.reshape(NF * ROWS, D),
        hots,
        x1,
        xn2,
        dy_bf,
        picks,
        gains,
        full,
        mixed,
    )
    dqkv, diag, shares_a = attend_backward(
        qkv, do, lse, base, pack_a.reshape(NF // 2, 2, share, D + 128), 3
    )
    part, pack_b, grad_in, grad_out = project_back(
        dqkv, all_tokens, gains, full, slots, diag, grad_in, grad_out
    )
    all_a, all_b, part_back = last_exchange(
        pack_b.reshape(NF // 2, 2, share, 3 * HW + 64), part, shares_a, 4
    )
    grad_x, grad_one, grad_two, grad_q, grad_k, grad_v, grad_o, grad_router, grad_table = finish(
        all_a, all_b, part_back, own_tokens, dx1, gains
    )
    return (
        layer_out.reshape(1, LB, D),
        grad_x.reshape(1, LB, D),
        grad_one.reshape(share),
        grad_two.reshape(share),
        grad_q,
        grad_k,
        grad_v,
        grad_o,
        grad_router,
        grad_table,
        grad_in,
        grad_out,
    )


def solution(mesh):
    placed = (
        P("fsdp", "seq", None),
        P("fsdp"),
        P("fsdp"),
        P("fsdp", None),
        P("fsdp", None),
        P("fsdp", None),
        P("fsdp", None),
        P("fsdp", None),
        P("fsdp", None),
        P("fsdp", None, "seq"),
        P("fsdp", "seq", None),
        P("fsdp", "seq", None),
        P(),
        P("fsdp", "seq", None),
    )
    return jax.shard_map(
        shards,
        mesh=mesh,
        in_specs=placed,
        out_specs=(
            P("fsdp", "seq", None),
            P("fsdp", "seq", None),
            P("fsdp"),
            P("fsdp"),
            P("fsdp", None),
            P("fsdp", None),
            P("fsdp", None),
            P("fsdp", None),
            P("fsdp", None),
            P("fsdp", None),
            P("fsdp", None, "seq"),
            P("fsdp", "seq", None),
        ),
        check_vma=False,
    )
```

```python
from functools import partial

import jax
import jax.numpy as jnp
from jax import lax
from jax.experimental import pallas as pl
from jax.experimental.pallas import tpu as pltpu
from jax.sharding import PartitionSpec as P

D = 768
H = 12
HD = 64
NS = 4
NF = 32
HL = H // NS
HW = HL * HD
LB = 256
LEN = 1024
E = 64
CAP = 12
ROWS = 2 * CAP
MSG = D + 128
PACK = 1536
NB = 32
MISC = PACK - 128
SPAN = 2 * LB

epsilon = 1e-06
MESH = pl.DeviceIdType.MESH
F32 = jnp.float32
BF16 = jnp.bfloat16
MIB = 1024 * 1024


def any_spec():
    return pl.BlockSpec(memory_space=pl.ANY)


def hbm_spec():
    return pl.BlockSpec(memory_space=pltpu.HBM)


def vmem_spec():
    return pl.BlockSpec(memory_space=pltpu.VMEM)


def dot(a, b, dims=((1,), (0,))):
    return lax.dot_general(a, b, (dims, ((), ())), preferred_element_type=F32)


def row_factor(values):
    return lax.rsqrt(jnp.mean(values * values, axis=1, keepdims=True) + epsilon)


def params(collective_id=None, vmem=63):
    if collective_id is None:
        return pltpu.CompilerParams(vmem_limit_bytes=vmem * MIB)
    return pltpu.CompilerParams(
        collective_id=collective_id, has_side_effects=True, vmem_limit_bytes=vmem * MIB
    )


def place_of():
    return lax.axis_index("seq"), lax.axis_index("fsdp")


def greet_seq(s):
    barrier = pltpu.get_barrier_semaphore()
    for k in range(1, NS):
        pl.semaphore_signal(
            barrier, inc=1, device_id={"seq": lax.rem(s + k, NS)}, device_id_type=MESH
        )
    return NS - 1


def greet_fsdp(f):
    barrier = pltpu.get_barrier_semaphore()

    def one(k, carried):
        pl.semaphore_signal(
            barrier, inc=1, device_id={"fsdp": lax.rem(f + k, NF)}, device_id_type=MESH
        )
        return carried

    lax.fori_loop(1, NF, one, 0)
    return NF - 1


def arrive(count):
    pl.semaphore_wait(pltpu.get_barrier_semaphore(), count)


def send_seq(s, source, target, send, recv):
    for k in range(1, NS):
        peer = lax.rem(s + k, NS)
        pltpu.make_async_remote_copy(
            src_ref=source(peer),
            dst_ref=target,
            send_sem=send,
            recv_sem=recv,
            device_id={"seq": peer},
            device_id_type=MESH,
        ).start()


def send_fsdp(f, source, target, send, recv):
    def one(k, carried):
        peer = lax.rem(f + k, NF)
        pltpu.make_async_remote_copy(
            src_ref=source(peer),
            dst_ref=target,
            send_sem=send,
            recv_sem=recv,
            device_id={"fsdp": peer},
            device_id_type=MESH,
        ).start()
        return carried

    lax.fori_loop(1, NF, one, 0)


def await_bytes(ref, sem):
    pltpu.make_async_copy(ref, ref, sem).wait()


def hop(source, target, to, send, recv, n):
    return pltpu.make_async_remote_copy(
        src_ref=source,
        dst_ref=target,
        send_sem=send.at[n],
        recv_sem=recv.at[n],
        device_id={"seq": to},
        device_id_type=MESH,
    )


def around(s):
    return lax.rem(s + 1, NS), lax.rem(s + NS - 1, NS), lax.rem(s + 2, NS)


def slot_hots(picks):
    lane = lax.broadcasted_iota(jnp.int32, (LB, E), 1)
    named = [picks[:, c : c + 1] == lane for c in range(2)]
    down = lax.broadcasted_iota(jnp.int32, (LB, LB), 0)
    across = lax.broadcasted_iota(jnp.int32, (LB, LB), 1)
    counts = dot((across < down).astype(BF16), (named[0] | named[1]).astype(BF16))
    slots = lax.broadcasted_iota(jnp.int32, (LB, NF * ROWS), 1)
    hots = []
    for c in range(2):
        rank = jnp.sum(jnp.where(named[c], counts, 0.0), axis=1, keepdims=True).astype(jnp.int32)
        pick = picks[:, c : c + 1]
        odd = pick & 1
        row = jnp.where(rank < 8, 8 * odd + rank, 8 + 4 * odd + rank)
        hots.append((slots == (pick >> 1) * ROWS + row).astype(BF16))
    return hots


def start_kernel(
    wo_ref, wq_ref, wk_ref, wv_ref, router_ref, one_ref, two_ref, table_ref, x_ref, picks_ref, dy_in,
    wg_out, xg, dy_own, dy_near, hots_out, packed, wg, dy_rows, hots, send, recv, local,
):
    s, f = place_of()
    right, left, far = around(s)
    pair, core = f // 2, lax.rem(f, 2)
    packed[:, :D] = wo_ref[...]
    for i in range(NS):

        @pl.when(s == i)
        def _():
            for n, w in enumerate((wq_ref, wk_ref, wv_ref)):
                at = D + n * HW
                packed[:, at : at + HW] = w[:, i * HW : (i + 1) * HW]

    packed[:, D + 3 * HW : MISC] = jnp.zeros((D // NF, MISC - D - 3 * HW), BF16)
    packed[:, MISC : MISC + E] = router_ref[...]
    share = D // NF
    square = (share, share)
    across = lax.broadcasted_iota(jnp.int32, square, 1)
    along = lax.broadcasted_iota(jnp.int32, square, 0) == across
    columns = [
        jnp.sum(jnp.where(along, gain[...].astype(F32), 0.0), axis=1, keepdims=True)
        for gain in (one_ref, two_ref)
    ]
    lane = lax.broadcasted_iota(jnp.int32, (H, 64), 1)
    head = lax.broadcasted_iota(jnp.int32, (H, 64), 0)
    taken = (head == HL * s + lane - 2) & (lane >= 2) & (lane < 2 + HL)
    line = dot(jnp.broadcast_to(table_ref[...], (8, H)), taken.astype(BF16))
    lane = lax.broadcasted_iota(jnp.int32, (share, 64), 1)
    row = lax.broadcasted_iota(jnp.int32, (share, 64), 0)
    misc = jnp.where(row == 0, jnp.broadcast_to(line[0:1], (share, 64)), 0.0)
    misc = jnp.where(lane == 0, columns[0], jnp.where(lane == 1, columns[1], misc))
    packed[:, MISC + E :] = misc.astype(BF16)
    count = greet_fsdp(f) + greet_seq(s)
    picks = picks_ref[...]
    one_hot, two_hot = slot_hots(picks)
    hots[0] = one_hot
    hots[1] = two_hot
    dy = dot(one_hot + two_hot, dy_in[...], ((0,), (0,)))
    dy_rows[:, :, :D] = dy.reshape(NF, ROWS, D).astype(BF16)
    named = [jnp.broadcast_to(picks[:, c : c + 1].astype(F32), (LB, 128)) for c in range(2)]
    others = dot(one_hot, named[1].astype(BF16), ((0,), (0,)))
    others = others + dot(two_hot, named[0].astype(BF16), ((0,), (0,)))
    dy_rows[:, :, D:] = others.reshape(NF, ROWS, 128).astype(BF16)
    arrive(count)
    first, second = pl.ds(0, LB // 2), pl.ds(LB // 2, LB // 2)
    x_begin = [hop(x_ref, xg.at[s], to, send, recv, n) for n, to in enumerate((right, left))]
    x_relay = [
        hop(xg.at[left, first], xg.at[left, first], right, send, recv, 2),
        hop(xg.at[right, second], xg.at[right, second], left, send, recv, 3),
    ]
    half = dy_own.at[pl.ds(0, NF // 2)]
    y_begin = [
        hop(half, dy_near.at[n], to, send, recv, 4 + n) for n, to in enumerate((right, left))
    ]
    for copy in x_begin:
        copy.start()
    send_fsdp(f, lambda peer: dy_rows.at[peer], dy_own.at[f], send.at[7], recv.at[7])

    def one(k, carried):
        peer = lax.rem(pair + k, NF // 2)
        pltpu.make_async_remote_copy(
            src_ref=packed,
            dst_ref=wg.at[pair, core],
            send_sem=send.at[6],
            recv_sem=recv.at[6],
            device_id={"fsdp": 2 * peer + core},
            device_id_type=MESH,
        ).start()
        return carried

    lax.fori_loop(1, NF // 2, one, 0)
    own_x = pltpu.make_async_copy(x_ref, xg.at[s], local.at[0])
    own_w = pltpu.make_async_copy(packed, wg.at[pair, core], local.at[1])
    own_x.start()
    own_w.start()
    own_dy = pltpu.make_async_copy(dy_rows.at[f], dy_own.at[f], local.at[2])
    own_dy.start()
    keep = pltpu.make_async_copy(hots, hots_out, local.at[3])
    keep.start()
    for n in range(2):
        x_begin[n].wait_recv()
        x_relay[n].start()
    own_w.wait()
    others_w = wg.at[pl.ds(0, NF // 2 - 1), core]
    swap = pltpu.make_async_remote_copy(
        src_ref=wg.at[:, core],
        dst_ref=wg.at[:, core],
        send_sem=send.at[8],
        recv_sem=recv.at[8],
        device_id={"fsdp": 2 * pair + 1 - core},
        device_id_type=MESH,
    )
    own_dy.wait()
    others_dy = dy_own.at[pl.ds(0, NF - 1)]
    await_bytes(others_dy, recv.at[7])
    for copy in y_begin:
        copy.start()
    await_bytes(others_w, recv.at[6])
    swap.start()
    swap.wait_recv()
    store = pltpu.make_async_copy(wg, wg_out, local.at[4])
    store.start()
    own_x.wait()
    keep.wait()
    store.wait()
    for copy in x_relay + y_begin:
        copy.wait_recv()
    for copy in x_begin + x_relay + y_begin + [swap]:
        copy.wait_send()
    await_bytes(others_w, send.at[6])
    await_bytes(others_dy, send.at[7])


def start_exchange(w_out, w_query, w_key, w_value, router, one, two, table, tokens, picks, dy):
    share = D // NF
    rows = (NF, ROWS, MSG)
    return pl.pallas_call(
        start_kernel,
        out_shape=(
            jax.ShapeDtypeStruct((NF // 2, 2, share, PACK), BF16),
            jax.ShapeDtypeStruct((NS, LB, D), BF16),
            jax.ShapeDtypeStruct(rows, BF16),
            jax.ShapeDtypeStruct((2, NF // 2, ROWS, MSG), BF16),
            jax.ShapeDtypeStruct((2, LB, NF * ROWS), BF16),
        ),
        in_specs=[vmem_spec()] * 11,
        out_specs=(hbm_spec(),) * 5,
        scratch_shapes=[
            pltpu.VMEM((share, PACK), BF16),
            pltpu.VMEM((NF // 2, 2, share, PACK), BF16),
            pltpu.VMEM(rows, BF16),
            pltpu.VMEM((2, LB, NF * ROWS), BF16),
            pltpu.SemaphoreType.DMA((9,)),
            pltpu.SemaphoreType.DMA((9,)),
            pltpu.SemaphoreType.DMA((5,)),
        ],
        compiler_params=params(0),
        name="start_exchange",
    )(w_out, w_query, w_key, w_value, router, one, two, table, tokens, picks, dy)


def sum_pairs(f, w_ref, wg, mine, theirs, send, recv, local, first):
    pair, core = f // 2, lax.rem(f, 2)
    swap = pltpu.make_async_remote_copy(
        src_ref=w_ref.at[:, 1 - core],
        dst_ref=theirs,
        send_sem=send.at[first],
        recv_sem=recv.at[first],
        device_id={"fsdp": 2 * pair + 1 - core},
        device_id_type=MESH,
    )
    own = pltpu.make_async_copy(w_ref.at[:, core], mine, local.at[first])
    keep = pltpu.make_async_copy(mine.at[pair], wg.at[pair], local.at[first + 1])
    others = wg.at[pl.ds(0, NF // 2 - 1)]

    def begin():
        swap.start()
        own.start()

    def middle():
        own.wait()
        swap.wait_recv()

        def add(i, carried):
            mine[i] = (mine[i].astype(F32) + theirs[i].astype(F32)).astype(BF16)
            return carried

        lax.fori_loop(0, NF // 2, add, 0)

        def one(k, carried):
            peer = lax.rem(pair + k, NF // 2)
            pltpu.make_async_remote_copy(
                src_ref=mine.at[peer],
                dst_ref=wg.at[pair],
                send_sem=send.at[first + 1],
                recv_sem=recv.at[first + 1],
                device_id={"fsdp": 2 * peer + core},
                device_id_type=MESH,
            ).start()
            return carried

        lax.fori_loop(1, NF // 2, one, 0)
        keep.start()

    def finish():
        keep.wait()
        await_bytes(others, recv.at[first + 1])

    def end():
        swap.wait_send()
        await_bytes(others, send.at[first + 1])

    return begin, middle, finish, end


def last_kernel(
    b_ref, x_ref, a_ref, all_a, all_b, xg, mine, theirs, got, sum_a, sum_b, summed, work,
    send, recv, local,
):
    s, f = place_of()
    right, left, far = around(s)
    half = LB // 2
    first, second = pl.ds(0, half), pl.ds(half, half)
    arrive(greet_fsdp(f) + greet_seq(s))
    begin, middle, finish, end = sum_pairs(f, b_ref, got, mine, theirs, send, recv, local, 0)
    onward = [
        hop(x_ref.at[far, first], summed.at[0], right, send, recv, 2),
        hop(x_ref.at[far, second], summed.at[1], left, send, recv, 3),
    ]
    early = [
        hop(x_ref.at[right, second], xg.at[0, second], right, send, recv, 4),
        hop(x_ref.at[left, first], xg.at[1, first], left, send, recv, 5),
    ]
    late = [
        hop(work.at[0], xg.at[0, first], right, send, recv, 6),
        hop(work.at[1], xg.at[1, second], left, send, recv, 7),
    ]
    for copy in onward:
        copy.start()
    begin()
    for copy in early:
        copy.start()
    own_x = pltpu.make_async_copy(x_ref.at[s], xg.at[2], local.at[2])
    own_x.start()
    middle()
    for n, block, rows in ((0, right, first), (1, left, second)):
        onward[n].wait_recv()
        work[n] = (x_ref[block, rows].astype(F32) + summed[n].astype(F32)).astype(BF16)
        late[n].start()

    def total(blocks):
        value = blocks[0].astype(F32)
        for i in range(1, NF // 2):
            value = value + blocks[i].astype(F32)
        return value

    sum_a[...] = total(a_ref)
    send_seq(s, lambda peer: sum_a, all_a.at[s], send.at[8], recv.at[8])
    own_a = pltpu.make_async_copy(sum_a, all_a.at[s], local.at[3])
    own_a.start()
    finish()
    sum_b[...] = total(got)
    send_seq(s, lambda peer: sum_b, all_b.at[s], send.at[9], recv.at[9])
    own_b = pltpu.make_async_copy(sum_b, all_b.at[s], local.at[4])
    own_b.start()
    own_x.wait()
    own_a.wait()
    own_b.wait()
    for n, out in ((8, all_a), (9, all_b)):
        others = out.at[pl.ds(0, NS - 1)]
        await_bytes(others, recv.at[n])
        await_bytes(others, send.at[n])
    for copy in early + late:
        copy.wait_recv()
    for copy in onward + early + late:
        copy.wait_send()
    end()


def last_exchange(b, x, a, collective_id):
    half = (b.shape[0],) + b.shape[2:]
    return pl.pallas_call(
        last_kernel,
        out_shape=(
            jax.ShapeDtypeStruct((NS,) + a.shape[1:], F32),
            jax.ShapeDtypeStruct((NS,) + b.shape[2:], F32),
            jax.ShapeDtypeStruct((3,) + x.shape[1:], x.dtype),
        ),
        in_specs=[vmem_spec()] * 3,
        out_specs=(any_spec(), any_spec(), any_spec()),
        scratch_shapes=[
            pltpu.VMEM(half, BF16),
            pltpu.VMEM(half, BF16),
            pltpu.VMEM(half, BF16),
            pltpu.VMEM(a.shape[1:], F32),
            pltpu.VMEM(b.shape[2:], F32),
            pltpu.VMEM((2, LB // 2, D), BF16),
            pltpu.VMEM((2, LB // 2, D), BF16),
            pltpu.SemaphoreType.DMA((10,)),
            pltpu.SemaphoreType.DMA((10,)),
            pltpu.SemaphoreType.DMA((5,)),
        ],
        compiler_params=params(collective_id),
        name="last_exchange",
    )(b, x, a)


def bias_tiles(base_ref, tiles, head):
    for d in range(NS):
        wide = jnp.broadcast_to(base_ref[head, d : d + 1, :], (LB, SPAN))
        tiles[d] = pltpu.roll(wide, 0, 1, stride=1, stride_axis=0)[:, :LB]


def score_tiles(qkv_ref, tiles, head, block):
    rows, cols = slice(block * LB, (block + 1) * LB), head * HD
    query = qkv_ref[rows, cols : cols + HD]
    parts = []
    for kb in range(block + 1):
        keys = qkv_ref[kb * LB : (kb + 1) * LB, HW + cols : HW + cols + HD]
        parts.append(dot(query, keys, ((1,), (1,))) * (HD**-0.5) + tiles[block - kb])
    return parts


def front_kernel(
    full_in, all_in, x_in, slots_in, hots_in, dy_ref,
    qkv_out, base_out, lse_out, mixed_out, x1_out, xn2_out, rows_out, gains_out, dy_near,
    full_ref, all_ref, x_ref, slots_ref, hots_ref,
    qkv_ref, base_ref, lse_ref, mixed, x1_ref, xn2_ref, rows_ref, gains_ref,
    o, tiles, send, recv, local, stage,
):
    s, f = place_of()
    right, left, _ = around(s)
    loads = [
        pltpu.make_async_copy(source, target, stage.at[n])
        for n, (source, target) in enumerate(
            (
                (full_in, full_ref),
                (slots_in, slots_ref),
                (all_in, all_ref),
                (x_in, x_ref),
                (hots_in, hots_ref),
            )
        )
    ]
    stores = [
        pltpu.make_async_copy(source, target, stage.at[5 + n])
        for n, (source, target) in enumerate(
            (
                (gains_ref, gains_out),
                (base_ref, base_out),
                (qkv_ref, qkv_out),
                (lse_ref, lse_out),
                (mixed, mixed_out),
                (x1_ref, x1_out),
                (xn2_ref, xn2_out),
                (rows_ref, rows_out),
            )
        )
    ]
    for load in loads:
        load.start()
    arrive(greet_seq(s))
    half = dy_ref.at[pl.ds(NF // 2, NF // 2)]
    beside = [hop(half, dy_near.at[n], to, send, recv, n) for n, to in enumerate((right, left))]
    for copy in beside:
        copy.start()
    for load in loads[:2]:
        load.wait()
    misc = full_ref[:, MISC:].astype(F32)
    turned = jnp.transpose(misc)
    gains_ref[...] = turned[E : E + 8]
    stores[0].start()
    gain_one, gain_two = turned[E : E + 1], turned[E + 1 : E + 2]
    table = misc.reshape(NB, D // NF, 128)[:, 0, :].astype(BF16)
    slots = slots_ref[...]
    hot = (slots == lax.broadcasted_iota(jnp.int32, (NB, NS * SPAN), 0)).astype(BF16)
    base = dot(table, hot, ((0,), (0,)))[E : E + 8]
    base = jnp.where(slots < 0, -1e30, base)
    for head in range(HL):
        for d in range(NS):
            line = base[2 + head : 3 + head, d * SPAN : (d + 1) * SPAN]
            base_ref[head, d : d + 1, :] = line
        bias_tiles(base_ref, tiles.at[head], head)
    stores[1].start()
    loads[2].wait()
    for block in range(NS):
        x = all_ref[block].astype(F32)
        xn1 = (x * row_factor(x) * gain_one).astype(BF16)
        rows = slice(block * LB, (block + 1) * LB)
        qkv_ref[rows, :] = dot(xn1, full_ref[:, D : D + 3 * HW]).astype(BF16)
    stores[2].start()
    for block in range(NS):
        rows = slice(block * LB, (block + 1) * LB)
        for head in range(HL):
            cols = slice(head * HD, (head + 1) * HD)
            parts = score_tiles(qkv_ref, tiles.at[head], head, block)
            top = parts[0].max(axis=1, keepdims=True)
            for part in parts[1:]:
                top = jnp.maximum(top, part.max(axis=1, keepdims=True))
            parts = [jnp.exp(part - top) for part in parts]
            total = parts[0].sum(axis=1, keepdims=True)
            for part in parts[1:]:
                total = total + part.sum(axis=1, keepdims=True)
            inverse = 1.0 / total
            value = None
            for kb, part in enumerate(parts):
                keys = slice(kb * LB, (kb + 1) * LB)
                values = qkv_ref[keys, 2 * HW + head * HD : 2 * HW + (head + 1) * HD]
                term = dot((part * inverse).astype(BF16), values)
                value = term if value is None else value + term
            o[block, :, cols] = value.astype(BF16)
            lse_ref[rows, head : head + 1] = top + jnp.log(total)

        @pl.when(s != block)
        def _():
            pltpu.make_async_remote_copy(
                src_ref=o.at[block],
                dst_ref=mixed.at[s],
                send_sem=send.at[2],
                recv_sem=recv.at[2],
                device_id={"seq": block},
                device_id_type=MESH,
            ).start()

    own = pltpu.make_async_copy(o.at[s], mixed.at[s], local)
    own.start()
    stores[3].start()
    for load in loads[3:]:
        load.wait()
    own.wait()
    others = mixed.at[pl.ds(0, NS - 1)]
    await_bytes(others, recv.at[2])
    stores[4].start()
    x1 = x_ref[...].astype(F32)
    for i in range(NS):
        x1 = x1 + dot(mixed[i], full_ref[i * HW : (i + 1) * HW, :D])
    x1_ref[...] = x1
    stores[5].start()
    xn2 = (x1 * row_factor(x1) * gain_two).astype(BF16)
    xn2_ref[...] = xn2
    stores[6].start()
    rows = dot(hots_ref[0] + hots_ref[1], xn2, ((0,), (0,)))
    rows_ref[...] = rows.reshape(NF, ROWS, D).astype(BF16)
    stores[7].start()
    await_bytes(others, send.at[2])
    for copy in beside:
        copy.wait_recv()
        copy.wait_send()
    for store in stores:
        store.wait()


def front(full, all_tokens, tokens, slots, hots, dy_own, collective_id):
    inputs = (full, all_tokens, tokens, slots, hots)
    made = [
        ((LEN, 3 * HW), BF16),
        ((HL, NS, SPAN), F32),
        ((LEN, 128), F32),
        ((NS, LB, HW), BF16),
        ((LB, D), F32),
        ((LB, D), BF16),
        ((NF, ROWS, D), BF16),
        ((8, D), F32),
    ]
    return pl.pallas_call(
        front_kernel,
        out_shape=tuple(jax.ShapeDtypeStruct(*m) for m in made)
        + (jax.ShapeDtypeStruct((2, NF // 2) + dy_own.shape[1:], BF16),),
        in_specs=[hbm_spec()] * 6,
        out_specs=(hbm_spec(),) * 9,
        scratch_shapes=[pltpu.VMEM(i.shape, i.dtype) for i in inputs]
        + [pltpu.VMEM(*m) for m in made]
        + [
            pltpu.VMEM((NS, LB, HW), BF16),
            pltpu.VMEM((HL, NS, LB, LB), F32),
            pltpu.SemaphoreType.DMA((3,)),
            pltpu.SemaphoreType.DMA((3,)),
            pltpu.SemaphoreType.DMA,
            pltpu.SemaphoreType.DMA((13,)),
        ],
        compiler_params=params(collective_id),
        name="front",
    )(full, all_tokens, tokens, slots, hots, dy_own)


def flip_rows(values):
    down = lax.broadcasted_iota(jnp.int32, (LB, LB), 0)
    across = lax.broadcasted_iota(jnp.int32, (LB, LB), 1)
    swap = (down + across == LB - 1).astype(BF16)
    high = values.astype(BF16)
    low = (values - high.astype(F32)).astype(BF16)
    return dot(swap, high) + dot(swap, low)


def backward_kernel(
    qkv_ref, do_ref, lse_ref, base_ref, pack_ref, g_ref, diag_ref, sums,
    do, tiles, folds, dk, dv, mine, theirs, send, recv, local,
):
    s, f = place_of()
    arrive(greet_fsdp(f) + greet_seq(s))
    begin, middle, finish, end = sum_pairs(
        f, pack_ref, sums, mine, theirs, send, recv, local, 0
    )
    send_seq(s, lambda peer: do_ref.at[peer], do.at[s], send.at[2], recv.at[2])
    own = pltpu.make_async_copy(do_ref.at[s], do.at[s], local.at[2])
    own.start()
    begin()
    for head in range(HL):
        bias_tiles(base_ref, tiles.at[head], head)
    middle()
    own.wait()
    others = do.at[pl.ds(0, NS - 1)]
    await_bytes(others, recv.at[2])
    scale = HD**-0.5
    for head in range(HL):
        cols = slice(head * HD, (head + 1) * HD)
        values = slice(2 * HW + head * HD, 2 * HW + (head + 1) * HD)
        for block in range(NS):
            rows = slice(block * LB, (block + 1) * LB)
            query, grad = qkv_ref[rows, cols], do[block, :, cols]
            lse = lse_ref[rows, head : head + 1]
            parts = score_tiles(qkv_ref, tiles.at[head], head, block)
            probs = [jnp.exp(part - lse) for part in parts]
            grads = [
                dot(grad, qkv_ref[kb * LB : (kb + 1) * LB, values], ((1,), (1,)))
                for kb in range(block + 1)
            ]
            delta = None
            for prob, part in zip(probs, grads):
                term = (prob * part).sum(axis=1, keepdims=True)
                delta = term if delta is None else delta + term
            grad_query = None
            for kb in range(block + 1):
                keys = slice(kb * LB, (kb + 1) * LB)
                d = block - kb
                ds = probs[kb] * (grads[kb] - delta)
                if kb == 0:
                    folds[d] = ds
                else:
                    folds[d] += ds
                raw = (ds * scale).astype(BF16)
                term = dot(raw, qkv_ref[keys, HW + head * HD : HW + (head + 1) * HD])
                grad_query = term if grad_query is None else grad_query + term
                to_key = dot(raw, query, ((0,), (0,)))
                to_value = dot(probs[kb].astype(BF16), grad, ((0,), (0,)))
                if d == 0:
                    dk[keys, :] = to_key
                    dv[keys, :] = to_value
                else:
                    dk[keys, :] += to_key
                    dv[keys, :] += to_value
            g_ref[rows, cols] = grad_query.astype(BF16)
        g_ref[:, HW + head * HD : HW + (head + 1) * HD] = dk[...].astype(BF16)
        g_ref[:, 2 * HW + head * HD : 2 * HW + (head + 1) * HD] = dv[...].astype(BF16)
        for d in range(NS):
            wide = jnp.concatenate(
                [flip_rows(folds[d]), jnp.zeros((LB, SPAN - LB), F32)], axis=1
            )
            turned = pltpu.roll(wide, LB + 1, 1, stride=1, stride_axis=0)
            at = slice(d * SPAN, (d + 1) * SPAN)
            diag_ref[head : head + 1, at] = turned.sum(axis=0, keepdims=True)
    await_bytes(others, send.at[2])
    finish()
    end()


def attend_backward(qkv, do, lse, base, pack, collective_id):
    half = (pack.shape[0],) + pack.shape[2:]
    return pl.pallas_call(
        backward_kernel,
        out_shape=(
            jax.ShapeDtypeStruct((LEN, 3 * HW), BF16),
            jax.ShapeDtypeStruct((HL, NS * SPAN), F32),
            jax.ShapeDtypeStruct(half, BF16),
        ),
        in_specs=[vmem_spec()] * 5,
        out_specs=(vmem_spec(), vmem_spec(), any_spec()),
        scratch_shapes=[
            pltpu.VMEM((NS, LB, HW), BF16),
            pltpu.VMEM((HL, NS, LB, LB), F32),
            pltpu.VMEM((NS, LB, LB), F32),
            pltpu.VMEM((LEN, HD), F32),
            pltpu.VMEM((LEN, HD), F32),
            pltpu.VMEM(half, BF16),
            pltpu.VMEM(half, BF16),
            pltpu.SemaphoreType.DMA((3,)),
            pltpu.SemaphoreType.DMA((3,)),
            pltpu.SemaphoreType.DMA((3,)),
        ],
        compiler_params=params(collective_id),
        name="attend_backward",
    )(qkv, do, lse, base, pack)


def split_rows(rows):
    width = rows.shape[-1]
    half = NF // 2
    mixed = rows[:, 16:24]
    left, right = mixed[:half], mixed[half:]
    low = lax.broadcasted_iota(jnp.int32, left.shape, 1) < 4
    one = jnp.where(low, left, pltpu.roll(right, 4, 1)).reshape(half * 8, width)
    two = jnp.where(low, pltpu.roll(left, 4, 1), right).reshape(half * 8, width)
    return (
        jnp.concatenate([rows[:, 0:8].reshape(NF * 8, width), one], axis=0),
        jnp.concatenate([rows[:, 8:16].reshape(NF * 8, width), two], axis=0),
    )


def join_rows(first, second):
    width = first.shape[-1]
    half = NF // 2
    one = first[NF * 8 :].reshape(half, 8, width)
    two = second[NF * 8 :].reshape(half, 8, width)
    low = lax.broadcasted_iota(jnp.int32, one.shape, 1) < 4
    left = jnp.where(low, one, pltpu.roll(two, 4, 1))
    right = jnp.where(low, pltpu.roll(one, 4, 1), two)
    return jnp.concatenate(
        [
            first[: NF * 8].reshape(NF, 8, width),
            second[: NF * 8].reshape(NF, 8, width),
            jnp.concatenate([left, right], axis=0),
        ],
        axis=1,
    )


def expert_rows(x, dy, ids, own, router, w_in, w_out):
    logits = dot(x, router)
    lane = lax.broadcasted_iota(jnp.int32, logits.shape, 1)
    one = jnp.sum(jnp.where(lane == own, logits, 0.0), axis=1, keepdims=True)
    two = jnp.sum(jnp.where(lane == ids, logits, 0.0), axis=1, keepdims=True)
    top = jnp.maximum(one, two)
    one, two = jnp.exp(one - top), jnp.exp(two - top)
    gate = one / (one + two)
    grad = (dy * gate).astype(BF16)
    u = dot(x, w_in)
    square = u * u
    tanh = jnp.tanh(u * (0.7978845608028654 + (0.7978845608028654 * 0.044715) * square))
    half = 0.5 * (1.0 + tanh)
    hid = (u * half).astype(BF16)
    slope = half + (0.5 * u) * (1.0 - tanh * tanh) * (
        0.7978845608028654 + (3.0 * 0.7978845608028654 * 0.044715) * square
    )
    y = dot(hid, w_out)
    du = (dot(grad, w_out, ((1,), (1,))) * slope).astype(BF16)
    dx = dot(du, w_in, ((1,), (1,)))
    return y, dx, hid, grad, du


def expert_kernel(
    x_ref, dy_own, near_a, near_b, full_ref, wi_in, wo_in,
    y_out, dx_out, gi_out, go_out, dy_far,
    router_ref, wi_ref, wo_ref, gi_ref, go_ref,
    x, dy, part, near, summed, kept, send, recv, local,
):
    s, f = place_of()
    right, left, far = around(s)
    half = NF // 2
    first, second = pl.ds(0, half), pl.ds(half, half)
    columns = [pl.ds(0, D // 2), pl.ds(D // 2, D // 2)]
    loads = [
        pltpu.make_async_copy(source, target, local.at[7 + n])
        for n, (source, target) in enumerate(
            ((wi_in, wi_ref), (wo_in, wo_ref), (full_ref.at[:, pl.ds(MISC, 128)], router_ref))
        )
    ]
    stores = [
        pltpu.make_async_copy(gi_ref, gi_out, local.at[10]),
        pltpu.make_async_copy(go_ref, go_out, local.at[11]),
    ]
    for load in loads:
        load.start()
    arrive(greet_fsdp(f) + greet_seq(s))

    def step_to(source, target, to, n):
        return hop(source, target, to, send, recv, n)

    for c in range(2):
        send_fsdp(
            f,
            lambda peer: x_ref.at[peer, :, columns[c]],
            x.at[s, f, :, columns[c]],
            send.at[c],
            recv.at[c],
        )
    dy_relay = [
        step_to(near_a.at[0], dy_far.at[first], right, 2),
        step_to(near_b.at[1], dy_far.at[second], left, 3),
    ]
    for copy in dy_relay:
        copy.start()
    own_x = pltpu.make_async_copy(x_ref.at[f], x.at[s, f], local.at[0])
    own_x.start()
    gi_ref[...] = jnp.zeros_like(gi_ref)
    go_ref[...] = jnp.zeros_like(go_ref)
    begin, early, onward, late = [], [], [], []
    for c in range(2):
        block = x.at[s, :, :, columns[c]]
        begin.append([step_to(block, block, to, 4 + 2 * c + n) for n, to in enumerate((right, left))])
    relay = [
        step_to(x.at[left, first], x.at[left, first], right, 8),
        step_to(x.at[right, second], x.at[right, second], left, 9),
    ]
    for a in range(2):
        early.append(
            [
                step_to(part.at[a, right, second], near.at[a, 0, second], right, 10 + 2 * a),
                step_to(part.at[a, left, first], near.at[a, 1, first], left, 11 + 2 * a),
            ]
        )
        onward.append(
            [
                step_to(part.at[a, far, first], summed.at[a, 0], right, 14 + 2 * a),
                step_to(part.at[a, far, second], summed.at[a, 1], left, 15 + 2 * a),
            ]
        )
        late.append(
            [
                [
                    step_to(
                        part.at[a, right, first, :, columns[c]],
                        near.at[a, 0, first, :, columns[c]],
                        right,
                        18 + 4 * a + 2 * c,
                    ),
                    step_to(
                        part.at[a, left, second, :, columns[c]],
                        near.at[a, 1, second, :, columns[c]],
                        left,
                        19 + 4 * a + 2 * c,
                    ),
                ]
                for c in range(2)
            ]
        )
    for load in loads:
        load.wait()
    own_x.wait()
    others_x = [x.at[s, pl.ds(0, NF - 1), :, columns[c]] for c in range(2)]
    for c in range(2):
        await_bytes(others_x[c], recv.at[c])
        for copy in begin[c]:
            copy.start()

    def step(k, carried):
        chunk = lax.rem(s + jnp.where(k == 1, 3, jnp.where(k == 0, 0, k - 1)), NS)

        @pl.when(k == 3)
        def _():
            for copy in dy_relay + relay:
                copy.wait_recv()

        for n, (low, high) in enumerate(
            (
                (dy_own.at[first], dy_own.at[second]),
                (near_a.at[0], near_b.at[0]),
                (near_a.at[1], near_b.at[1]),
                (dy_far.at[first], dy_far.at[second]),
            )
        ):

            @pl.when(k == n)
            def _():
                loads = [
                    pltpu.make_async_copy(low, dy.at[first], local.at[1]),
                    pltpu.make_async_copy(high, dy.at[second], local.at[2]),
                ]
                for load in loads:
                    load.start()
                for load in loads:
                    load.wait()

        @pl.when(k == 1)
        def _():
            for n in range(2):
                for c in range(2):
                    begin[c][n].wait_recv()
                relay[n].start()

        xs = split_rows(x[chunk].astype(F32))
        dys = split_rows(dy[...].astype(F32))
        ys, dxs = [], []
        for j in range(2):
            rows = xs[j].astype(BF16)
            ids = dys[j][:, D:].astype(jnp.int32)
            y, dx, hid, grad, du = expert_rows(
                rows, dys[j][:, :D], ids, 2 * f + j, router_ref[...], wi_ref[j], wo_ref[j]
            )
            ys.append(y)
            dxs.append(dx)
            slot = jnp.where(k == 0, 0, k - 1)
            for n, value in enumerate((rows, hid, grad, du)):
                kept[slot, n, j] = value
        part[0, chunk] = join_rows(*ys).astype(BF16)
        part[1, chunk] = join_rows(*dxs).astype(BF16)

        @pl.when(k == 1)
        def _():
            for a in range(2):
                early[a][1].start()

        @pl.when(k == 2)
        def _():
            early[0][0].start()

        @pl.when(k == 3)
        def _():
            for a in range(2):
                for n in range(2):
                    onward[a][n].start()

        @pl.when(k == 0)
        def _():
            weights(0, 0)

        return carried

    def weights(slot, carried):
        for j in range(2):
            go_ref[j] += dot(kept[slot, 1, j], kept[slot, 2, j], ((0,), (0,)))
            gi_ref[j] += dot(kept[slot, 0, j], kept[slot, 3, j], ((0,), (0,)))
        return carried

    lax.fori_loop(0, NS, step, 0)
    lax.fori_loop(0, NS - 1, weights, 0)
    for store in stores:
        store.start()

    def add(a, block, offset, cols, other):
        def one(i, carried):
            rows = pl.ds(offset + 8 * i, 8)
            total = part[a, block, rows, :, cols].astype(F32) + other(pl.ds(8 * i, 8))
            part[a, block, rows, :, cols] = total.astype(BF16)
            return carried

        return one

    for a in range(2):
        for n in range(2):
            onward[a][n].wait_recv()
        for c in range(2):
            for n, block, offset in ((0, right, 0), (1, left, half)):
                lax.fori_loop(
                    0,
                    half // 8,
                    add(
                        a,
                        block,
                        offset,
                        columns[c],
                        lambda i: summed[a, n, i, :, columns[c]].astype(F32),
                    ),
                    0,
                )
                late[a][c][n].start()
        if a == 0:
            early[1][0].start()
    outs = (y_out, dx_out)
    pieces = []
    for a in range(2):
        for n in range(2):
            early[a][n].wait_recv()
        for c in range(2):
            cols = columns[c]
            for n in range(2):
                late[a][c][n].wait_recv()
            lax.fori_loop(
                0,
                NF // 8,
                add(
                    a,
                    s,
                    0,
                    cols,
                    lambda i: near[a, 0, i, :, cols].astype(F32)
                    + near[a, 1, i, :, cols].astype(F32),
                ),
                0,
            )
            p = 2 * a + c
            send_fsdp(
                f,
                lambda peer: part.at[a, s, peer, :, cols],
                outs[a].at[f, :, cols],
                send.at[26 + p],
                recv.at[26 + p],
            )
            keep = pltpu.make_async_copy(
                part.at[a, s, f, :, cols], outs[a].at[f, :, cols], local.at[3 + p]
            )
            keep.start()
            pieces.append((keep, outs[a].at[pl.ds(0, NF - 1), :, cols], 26 + p))
    for keep, others, n in pieces:
        keep.wait()
        await_bytes(others, recv.at[n])
        await_bytes(others, send.at[n])
    for a in range(2):
        for copy in early[a] + onward[a] + late[a][0] + late[a][1]:
            copy.wait_send()
    for copy in begin[0] + begin[1] + relay + dy_relay:
        copy.wait_send()
    for c in range(2):
        await_bytes(others_x[c], send.at[c])
    for store in stores:
        store.wait()


def run_experts(x, dy, near_a, near_b, full, w_in, w_out, collective_id):
    rows = (NF, ROWS, D)
    return pl.pallas_call(
        expert_kernel,
        out_shape=(
            jax.ShapeDtypeStruct(rows, BF16),
            jax.ShapeDtypeStruct(rows, BF16),
            jax.ShapeDtypeStruct((2, D, D), F32),
            jax.ShapeDtypeStruct((2, D, D), F32),
            jax.ShapeDtypeStruct((NF, ROWS, MSG), BF16),
        ),
        in_specs=[any_spec()] * 7,
        out_specs=(any_spec(),) * 5,
        scratch_shapes=[
            pltpu.VMEM((D, 128), BF16),
            pltpu.VMEM((2, D, D), BF16),
            pltpu.VMEM((2, D, D), BF16),
            pltpu.VMEM((2, D, D), F32),
            pltpu.VMEM((2, D, D), F32),
            pltpu.VMEM((NS,) + rows, BF16),
            pltpu.VMEM((NF, ROWS, MSG), BF16),
            pltpu.VMEM((2, NS) + rows, BF16),
            pltpu.VMEM((2, 2) + rows, BF16),
            pltpu.VMEM((2, 2, NF // 2, ROWS, D), BF16),
            pltpu.VMEM((NS - 1, 4, 2, NF * CAP, D), BF16),
            pltpu.SemaphoreType.DMA((30,)),
            pltpu.SemaphoreType.DMA((30,)),
            pltpu.SemaphoreType.DMA((12,)),
        ],
        compiler_params=params(collective_id),
        name="run_experts",
    )(x, dy, near_a, near_b, full, w_in, w_out)


def token_kernel(
    y_in, dx_in, hot_in, x1_in, xn2_in, dy_in, picks_ref, gain_in, full_in, mixed_in, go_in,
    out_ref, dx1_ref, do_ref, pack_ref, go_out,
    xn2_ref, x1_ref, full_ref, dy_ref, hot_ref, y_ref, dx_ref, gain_ref, mixed_ref, held, stage,
):
    loads = [
        pltpu.make_async_copy(source, target, stage.at[n])
        for n, (source, target) in enumerate(
            (
                (xn2_in, xn2_ref),
                (x1_in, x1_ref),
                (full_in, full_ref),
                (dy_in, dy_ref),
                (hot_in, hot_ref),
                (y_in, y_ref),
                (dx_in, dx_ref),
                (gain_in, gain_ref),
                (mixed_in, mixed_ref),
            )
        )
    ]
    for load in loads:
        load.start()
    onward = pltpu.make_async_copy(go_in, held, stage.at[9])
    onward.start()
    for load in loads[:6]:
        load.wait()
    xn2, x1, router = xn2_ref[...], x1_ref[...], full_ref[:, MISC:]
    dy = dy_ref[...].astype(F32)
    logits = dot(xn2, router)
    lane = lax.broadcasted_iota(jnp.int32, logits.shape, 1)
    named = [lane == picks_ref[:, c : c + 1] for c in range(2)]
    chosen = [jnp.sum(jnp.where(n, logits, 0.0), axis=1, keepdims=True) for n in named]
    top = jnp.maximum(chosen[0], chosen[1])
    chosen = [jnp.exp(value - top) for value in chosen]
    both = chosen[0] + chosen[1]
    gates = [value / both for value in chosen]
    ys = [dot(hot_ref[c], y_ref[...]) for c in range(2)]
    out_ref[...] = (x1 + (gates[0] * ys[0] + gates[1] * ys[1])).astype(BF16)
    dgates = [jnp.sum(dy * y, axis=1, keepdims=True) for y in ys]
    mean = gates[0] * dgates[0] + gates[1] * dgates[1]
    dpicks = [gates[c] * (dgates[c] - mean) for c in range(2)]
    dlogits = sum(jnp.where(named[c], dpicks[c], 0.0) for c in range(2)).astype(BF16)
    for load in loads[6:]:
        load.wait()
    onward.wait()
    store = pltpu.make_async_copy(held, go_out, stage.at[10])
    store.start()
    dxn2 = dot(hot_ref[0] + hot_ref[1], dx_ref[...])
    dxn2 = dxn2 + dot(dlogits, router, ((1,), (1,)))
    r2 = row_factor(x1)
    terms = (dxn2 * x1 * r2).astype(BF16)
    grad_gain = dot(terms, jnp.ones((LB, 128), BF16), ((0,), (0,)))
    grad_router = dot(xn2, dlogits, ((0,), (0,)))
    lane = lax.broadcasted_iota(jnp.int32, grad_gain.shape, 1)
    pack_ref[:, D:] = jnp.where(lane == E, grad_gain, grad_router).astype(BF16)
    scaled = dxn2 * gain_ref[1:2]
    mean = jnp.mean(scaled * x1, axis=1, keepdims=True)
    dx1 = dy + r2 * scaled - x1 * (r2 * r2 * r2) * mean
    dx1_ref[...] = dx1
    dat = dx1.astype(BF16)
    for i in range(NS):
        rows = slice(i * HW, (i + 1) * HW)
        do_ref[i] = dot(dat, full_ref[rows, :D], ((1,), (1,))).astype(BF16)
        pack_ref[rows, :D] = dot(mixed_ref[i], dat, ((0,), (0,))).astype(BF16)
    store.wait()


def token_side(y, dx, hot, x1, xn2, dy, picks, gains, full, mixed, go):
    staged = (xn2, x1, full, dy, hot, y, dx, gains, mixed)
    return pl.pallas_call(
        token_kernel,
        out_shape=(
            jax.ShapeDtypeStruct((LB, D), BF16),
            jax.ShapeDtypeStruct((LB, D), F32),
            jax.ShapeDtypeStruct((NS, LB, HW), BF16),
            jax.ShapeDtypeStruct((D, D + 128), BF16),
            jax.ShapeDtypeStruct(go.shape, F32),
        ),
        in_specs=[hbm_spec()] * 6 + [vmem_spec()] + [hbm_spec()] * 4,
        out_specs=(vmem_spec(),) * 4 + (hbm_spec(),),
        scratch_shapes=[pltpu.VMEM(i.shape, i.dtype) for i in staged]
        + [pltpu.VMEM(go.shape, F32), pltpu.SemaphoreType.DMA((11,))],
        compiler_params=params(),
        name="token_side",
    )(y, dx, hot, x1, xn2, dy, picks, gains, full, mixed, go)


def project_kernel(
    g_ref, x_ref, gain_ref, full_ref, slots_ref, diag_ref, gi_ref,
    part_ref, pack_ref, gi_out, weight, held, local,
):
    loads = [
        pltpu.make_async_copy(gi_ref, held.at[0], local.at[0]),
    ]
    stores = [
        pltpu.make_async_copy(held.at[0], gi_out, local.at[2]),
    ]
    for copy in loads:
        copy.start()
    weight[...] = jnp.zeros_like(weight)
    misc = jnp.zeros((D, 64), F32)
    for block in range(NS):
        rows = slice(block * LB, (block + 1) * LB)
        x = x_ref[block].astype(F32)
        r1 = row_factor(x)
        xn1 = (x * r1 * gain_ref[0:1]).astype(BF16)
        g = g_ref[rows, :]
        weight[...] += dot(xn1, g, ((0,), (0,)))
        part = dot(g, full_ref[:, D : D + 3 * HW], ((1,), (1,)))
        part_ref[block] = part.astype(BF16)
        terms = (part * x * r1).astype(BF16)
        misc = misc + dot(terms, jnp.ones((LB, 64), BF16), ((0,), (0,)))
        if block < 1:
            loads[block].wait()
            stores[block].start()
    lane = lax.broadcasted_iota(jnp.int32, misc.shape, 1)
    row = lax.broadcasted_iota(jnp.int32, (NB, NS * SPAN), 0)
    hot = (slots_ref[...] == row).astype(BF16)
    diag = jnp.concatenate(
        [jnp.zeros((8, NS * SPAN), F32), diag_ref[...], jnp.zeros((56 - HL, NS * SPAN), F32)],
        axis=0,
    )
    high = diag.astype(BF16)
    low = (diag - high.astype(F32)).astype(BF16)
    table = dot(hot, high, ((1,), (1,))) + dot(hot, low, ((1,), (1,)))
    table = jnp.broadcast_to(table[:, None, :], (NB, D // NF, 64)).reshape(D, 64)
    misc = jnp.where(lane == 0, misc, table)
    pack_ref[:, : 3 * HW] = weight[...].astype(BF16)
    pack_ref[:, 3 * HW :] = misc.astype(BF16)
    for copy in stores:
        copy.wait()


def project_back(g, x, gains, full, slots, diag, gi):
    return pl.pallas_call(
        project_kernel,
        out_shape=(
            jax.ShapeDtypeStruct((NS, LB, D), BF16),
            jax.ShapeDtypeStruct((D, 3 * HW + 64), BF16),
            jax.ShapeDtypeStruct(gi.shape, F32),
        ),
        in_specs=[vmem_spec()] * 6 + [any_spec()],
        out_specs=(vmem_spec(), vmem_spec(), any_spec()),
        scratch_shapes=[
            pltpu.VMEM((D, 3 * HW), F32),
            pltpu.VMEM((1,) + gi.shape, F32),
            pltpu.SemaphoreType.DMA((4,)),
        ],
        compiler_params=params(),
        name="project_back",
    )(g, x, gains, full, slots, diag, gi)


def finish_kernel(
    a_ref, b_ref, part_ref, x_ref, dx1_ref, gain_ref,
    gx_ref, g1_ref, g2_ref, wq_ref, wk_ref, wv_ref, wo_ref, router_ref, table_ref,
):
    total = a_ref[0] + a_ref[1] + a_ref[2] + a_ref[3]
    wo_ref[...] = total[:, :D]
    router_ref[...] = total[:, D : D + E]
    g2_ref[...] = jnp.transpose(total[:, D:])[E : E + 1]
    misc = [b_ref[n, :, 3 * HW :] for n in range(NS)]
    gain = misc[0] + misc[1] + misc[2] + misc[3]
    g1_ref[...] = jnp.transpose(jnp.concatenate([gain, gain], axis=1))[0:1]
    table_ref[...] = jnp.concatenate([m[0:1, 8 : 8 + HL] for m in misc], axis=1)
    for i, out in enumerate((wq_ref, wk_ref, wv_ref)):
        out[...] = jnp.concatenate(
            [b_ref[n, :, i * HW : (i + 1) * HW] for n in range(NS)], axis=1
        )
    x = x_ref[...].astype(F32)
    r1 = row_factor(x)
    dxn1 = part_ref[0].astype(F32) + part_ref[1].astype(F32) + part_ref[2].astype(F32)
    scaled = dxn1 * gain_ref[0:1]
    mean = jnp.mean(scaled * x, axis=1, keepdims=True)
    gx_ref[...] = dx1_ref[...] + r1 * scaled - x * (r1 * r1 * r1) * mean


def finish(a, b, part, x, dx1, gain):
    share = D // NF
    return pl.pallas_call(
        finish_kernel,
        out_shape=(
            jax.ShapeDtypeStruct((LB, D), F32),
            jax.ShapeDtypeStruct((1, share), F32),
            jax.ShapeDtypeStruct((1, share), F32),
            jax.ShapeDtypeStruct((share, D), F32),
            jax.ShapeDtypeStruct((share, D), F32),
            jax.ShapeDtypeStruct((share, D), F32),
            jax.ShapeDtypeStruct((share, D), F32),
            jax.ShapeDtypeStruct((share, E), F32),
            jax.ShapeDtypeStruct((1, H), F32),
        ),
        in_specs=[vmem_spec()] * 6,
        out_specs=(vmem_spec(),) * 9,
        compiler_params=params(),
        name="finish",
    )(a, b, part, x, dx1, gain)


def distance_base(values, near, far):
    long = jnp.concatenate(
        [jnp.full((LB,), near, values.dtype), values, jnp.full((1,), far, values.dtype)]
    )
    rows = []
    for d in range(NS):
        rows.append(long[d * LB + 1 : d * LB + LB + 1][::-1])
        rows.append(long[LB + d * LB + 1 : LB + d * LB + LB + 1][::-1])
    return jnp.concatenate(rows)


def shards(
    tokens,
    gain_attn,
    gain_ffn,
    w_query,
    w_key,
    w_value,
    w_out,
    router,
    bias_table,
    expert_in,
    expert_out,
    choices,
    buckets,
    cotangent,
):
    s = lax.axis_index("seq")
    share = D // NF
    own_tokens = tokens.reshape(LB, D)

    picks = choices.reshape(LB, 2)
    dy_bf = cotangent.reshape(LB, D)
    gathered, all_tokens, dy_own, near_a, hots = start_exchange(
        w_out,
        w_query,
        w_key,
        w_value,
        router,
        gain_attn.reshape(1, share),
        gain_ffn.reshape(1, share),
        bias_table,
        own_tokens,
        picks,
        dy_bf,
    )
    full = gathered.reshape(D, PACK)
    slots = distance_base(buckets, -1, -1).reshape(1, NS * SPAN)
    qkv, base, lse, mixed, x1, xn2, x_rows, gains, near_b = front(
        full, all_tokens, own_tokens, slots, hots, dy_own, 1
    )
    y_back, dx_back, grad_in, grad_out, _ = run_experts(
        x_rows, dy_own, near_a, near_b, full, expert_in, expert_out, 2
    )
    layer_out, dx1, do, pack_a, grad_out = token_side(
        y_back.reshape(NF * ROWS, D),
        dx_back.reshape(NF * ROWS, D),
        hots,
        x1,
        xn2,
        dy_bf,
        picks,
        gains,
        full,
        mixed,
        grad_out,
    )
    dqkv, diag, shares_a = attend_backward(
        qkv, do, lse, base, pack_a.reshape(NF // 2, 2, share, D + 128), 3
    )
    part, pack_b, grad_in = project_back(
        dqkv, all_tokens, gains, full, slots, diag, grad_in
    )
    all_a, all_b, part_back = last_exchange(
        pack_b.reshape(NF // 2, 2, share, 3 * HW + 64), part, shares_a, 4
    )
    grad_x, grad_one, grad_two, grad_q, grad_k, grad_v, grad_o, grad_router, grad_table = finish(
        all_a, all_b, part_back, own_tokens, dx1, gains
    )
    return (
        layer_out.reshape(1, LB, D),
        grad_x.reshape(1, LB, D),
        grad_one.reshape(share),
        grad_two.reshape(share),
        grad_q,
        grad_k,
        grad_v,
        grad_o,
        grad_router,
        grad_table,
        grad_in,
        grad_out,
    )


def solution(mesh):
    placed = (
        P("fsdp", "seq", None),
        P("fsdp"),
        P("fsdp"),
        P("fsdp", None),
        P("fsdp", None),
        P("fsdp", None),
        P("fsdp", None),
        P("fsdp", None),
        P("fsdp", None),
        P("fsdp", None, "seq"),
        P("fsdp", "seq", None),
        P("fsdp", "seq", None),
        P(),
        P("fsdp", "seq", None),
    )
    return jax.shard_map(
        shards,
        mesh=mesh,
        in_specs=placed,
        out_specs=(
            P("fsdp", "seq", None),
            P("fsdp", "seq", None),
            P("fsdp"),
            P("fsdp"),
            P("fsdp", None),
            P("fsdp", None),
            P("fsdp", None),
            P("fsdp", None),
            P("fsdp", None),
            P("fsdp", None),
            P("fsdp", None, "seq"),
            P("fsdp", "seq", None),
        ),
        check_vma=False,
    )
```
